512 devices in a mesh: freq: 32 (over z, x_hi), sky: 16 (over y, x_lo, core).
Axes of the slice: x: 4 (x_hi: 2, x_lo: 2; x = x_hi * 2 + x_lo), y: 4, z: 16, core: 2. Of those that a mesh axis runs over, the one named last changes fastest.
Arguments:
- sky_cube: bfloat16 [64, 32, 2048], P('freq', 'sky'), may hold values from -24 to 24
- free_mask: int32 [64], P('freq'), may hold values 0 or 1
- conv_first: bfloat16 [32, 1, 3, 3, 3], replicated, may hold values from -1.25 to 1.25
- conv_second: bfloat16 [32, 32, 3, 3, 3], replicated, may hold values from -0.21875 to 0.21875
- proposal_conv: bfloat16 [3, 3, 64, 256], replicated, may hold values from -0.25 to 0.25
- score_head: bfloat16 [9, 256], replicated, may hold values from -0.375 to 0.375
- box_head: bfloat16 [36, 256], replicated, may hold values from -0.375 to 0.375
Outputs:
- objectness: float32 [9, 32, 2048], P(None, 'sky', 'freq')
- proposals: float32 [9, 4, 32, 2048], P(None, None, 'sky', 'freq')
The draws below stay inside these ranges and needn't reach their ends.
All inputs are finite; a program needn't handle non-finite values. No bound on the sum of `free_mask` on one device may be relied on, other than what follows from the above.
Results may differ from the reference program's by a relative error of at most 0.0055.
Values may be sent and summed in bfloat16 or wider, within the bound.
A program may use at most 64 MiB of HBM per device.

```python
import jax
import jax.numpy as jnp
from jax import lax

FEAT = 32
RPN = 256
ANCHORS = 9
ROWS_DEV = 2
COLS = 2048
MOM = 64
CHANS = 64
ROWS = 32
N_SKY = 16


def draw_sky_cube(key, part):
    key = jax.random.fold_in(key, 7)
    key_ripple, key_sky, key_noise = jax.random.split(key, 3)
    channel = jnp.arange(CHANS).astype(jnp.float32)
    spectral_ramp = 1.0 + 2.0 * channel / (CHANS - 1)
    ripple = 1.0 + 0.5 * jax.random.normal(key_ripple, (CHANS,), jnp.float32)
    continuum = jnp.exp(jax.random.uniform(key_sky, (ROWS, COLS), jnp.float32, -0.7, 0.7))
    noise_field = jax.random.normal(key_noise, (CHANS, ROWS, COLS), jnp.float32)
    cube_values = 0.5 * continuum[None] * (spectral_ramp * ripple)[:, None, None] + noise_field
    return jnp.clip(cube_values, -24.0, 24.0).astype(jnp.bfloat16)


def plant(drawn, own_key, smallest, top_value):
    dims = drawn.shape
    index_at = [jax.random.randint(jax.random.fold_in(own_key, axis), (), 0, dims[axis]) for axis in range(len(dims))]
    drawn = drawn.at[tuple(index_at)].set(smallest)
    longest = dims.index(max(dims))
    index_at[longest] = (index_at[longest] + 1) % dims[longest]
    return drawn.at[tuple(index_at)].set(top_value)


def normal_values(rng, extent, spread, bound, held_as=jnp.bfloat16):
    return jnp.clip(spread * jax.random.normal(rng, extent, jnp.float32), -bound, bound).astype(held_as)


def setup_inputs(seed: int = 0) -> dict:
    seeds = jax.random.split(jax.random.key(seed), 8)
    sky_cube = draw_sky_cube(jax.random.fold_in(seeds[7], 71), 0)
    free_mask = plant((jax.random.randint(seeds[1], (CHANS,), 0, 16) < 1).astype(jnp.int32), jax.random.fold_in(seeds[1], 1), 0, 1)
    conv_first = normal_values(seeds[2], (FEAT, 1, 3, 3, 3), 27 ** -0.5, 1.25)
    conv_second = normal_values(seeds[3], (FEAT, FEAT, 3, 3, 3), (27 * FEAT) ** -0.5, 0.21875)
    proposal_conv = normal_values(seeds[4], (3, 3, MOM, RPN), (9 * MOM) ** -0.5, 0.25)
    score_head = normal_values(seeds[5], (ANCHORS, RPN), RPN ** -0.5, 0.375)
    box_head = normal_values(seeds[6], (4 * ANCHORS, RPN), RPN ** -0.5, 0.375)
    return {"sky_cube": sky_cube, "free_mask": free_mask, "conv_first": conv_first, "conv_second": conv_second, "proposal_conv": proposal_conv, "score_head": score_head, "box_head": box_head}


def conv_volume(volume, kernel, paddings):
    return lax.conv_general_dilated(volume, kernel, (1, 1, 1), paddings, dimension_numbers=('NCDHW', 'OIDHW', 'NCDHW'), precision=lax.Precision.HIGHEST, preferred_element_type=jnp.float32)

def project_moments(second_layer, velocity, channel_total):
    zeroth = lax.optimization_barrier(jnp.sum(second_layer, axis=1)) / channel_total
    first_moment = jnp.einsum('cnyx,n->cyx', second_layer, velocity, precision=lax.Precision.HIGHEST) * (12.0 / channel_total)
    return jnp.concatenate([zeroth, first_moment], axis=0)

def decode_boxes(box_delta, row_start, col_start):
    anchor_count = box_delta.shape[0]
    map_height = box_delta.shape[2]
    map_width = box_delta.shape[3]
    anchor_index = jnp.arange(anchor_count, dtype=jnp.int32)
    anchor_scale = 4.0 * 2.0 ** (anchor_index // 3).astype(jnp.float32)
    anchor_ratio = 2.0 ** (anchor_index % 3 - 1).astype(jnp.float32)
    anchor_width = (anchor_scale * jnp.sqrt(anchor_ratio))[:, None, None]
    anchor_height = (anchor_scale / jnp.sqrt(anchor_ratio))[:, None, None]
    centre_rows = (row_start + jnp.arange(map_height, dtype=jnp.int32)).astype(jnp.float32) + 0.5
    centre_cols = (col_start + jnp.arange(map_width, dtype=jnp.int32)).astype(jnp.float32) + 0.5
    centre_x = centre_cols[None, None, :] + box_delta[:, 0] * anchor_width
    centre_y = centre_rows[None, :, None] + box_delta[:, 1] * anchor_height
    box_width = anchor_width * jnp.exp(box_delta[:, 2])
    box_height = anchor_height * jnp.exp(box_delta[:, 3])
    corners = jnp.stack([centre_x - 0.5 * box_width, centre_y - 0.5 * box_height, centre_x + 0.5 * box_width, centre_y + 0.5 * box_height], axis=1)
    return corners / 64.0

def reference(sky_cube, free_mask, conv_first, conv_second, proposal_conv, score_head, box_head):
    weights = free_mask.astype(jnp.float32)
    volume = sky_cube.astype(jnp.float32)
    masked_total = jnp.einsum('c,cyx->yx', weights, volume, precision=lax.Precision.HIGHEST)
    free_count = jnp.sum(weights)
    baseline = masked_total / jnp.maximum(free_count, 1.0)
    flattened = (volume - baseline[None]).astype(jnp.bfloat16)
    padded = jnp.pad(flattened, ((0, 0), (2, 2), (0, 0)))
    kernel_one = conv_first.astype(jnp.float32)
    kernel_two = conv_second.astype(jnp.float32)
    channel_index = jnp.arange(CHANS, dtype=jnp.int32)
    velocity = (channel_index.astype(jnp.float32) + 0.5) / CHANS - 0.5

    def strip(strip_index):
        row_start = strip_index * ROWS_DEV
        strip_block = lax.dynamic_slice_in_dim(padded, row_start, ROWS_DEV + 4, 1).astype(jnp.float32)[None, None]
        first_layer = jax.nn.relu(conv_volume(strip_block, kernel_one, [(1, 1), (0, 0), (1, 1)]))
        row_index = row_start - 1 + jnp.arange(ROWS_DEV + 2, dtype=jnp.int32)
        inside = (row_index >= 0) & (row_index < ROWS)
        first_layer = jnp.where(inside[None, None, None, :, None], first_layer, 0.0)
        first_layer = lax.optimization_barrier(first_layer.astype(jnp.bfloat16)).astype(jnp.float32)
        second_layer = jax.nn.relu(conv_volume(first_layer, kernel_two, [(1, 1), (0, 0), (1, 1)]))[0]
        return project_moments(second_layer, velocity, CHANS)
    strips = lax.map(strip, jnp.arange(N_SKY, dtype=jnp.int32))
    moment_maps = jnp.transpose(strips, (1, 0, 2, 3)).reshape(MOM, ROWS, COLS)
    moment_maps = lax.optimization_barrier(moment_maps.astype(jnp.bfloat16)).astype(jnp.float32)
    hidden = lax.conv_general_dilated(moment_maps[None], proposal_conv.astype(jnp.float32), (1, 1), [(1, 1), (1, 1)], dimension_numbers=('NCHW', 'HWIO', 'NCHW'), precision=lax.Precision.HIGHEST, preferred_element_type=jnp.float32)
    hidden = jax.nn.relu(hidden[0])
    hidden = lax.optimization_barrier(hidden.astype(jnp.bfloat16)).astype(jnp.float32)
    objectness = jnp.einsum('kc,cyx->kyx', score_head.astype(jnp.float32), hidden, precision=lax.Precision.HIGHEST)
    box_delta = jnp.einsum('kc,cyx->kyx', box_head.astype(jnp.float32), hidden, precision=lax.Precision.HIGHEST)
    box_delta = box_delta.reshape(ANCHORS, 4, ROWS, COLS)
    return (objectness, decode_boxes(box_delta, 0, 0))
```

```python
import functools

import jax
import jax.numpy as jnp
from jax import lax
from jax.experimental import pallas as pl
from jax.experimental.pallas import tpu as pltpu
from jax.sharding import PartitionSpec as P

F32 = jnp.float32
BF16 = jnp.bfloat16
MESH = pl.DeviceIdType.MESH
CHANS = 64
FEAT = 32
ANCHORS = 9
WIDTH = 64
LANES = 128
SLAB = 16
STRIDE = 5
ROWS_ONE = (STRIDE + 2) * SLAB
ROWS_TWO = STRIDE * SLAB
PAIRS = CHANS // 2 + 1
STEP = 2 * 6 * FEAT
SPAN = 2 * STEP
WINDOW = 8
WINDOW_LANES = WINDOW * 6 * FEAT
GROUP = 3
NT = (((1,), (1,)), ((), ()))


def iota(shape, dim):
    return lax.broadcasted_iota(jnp.int32, shape, dim)


def dot(a, b):
    return jnp.dot(a, b, preferred_element_type=F32)


def dot_nt(a, b):
    return lax.dot_general(a, b, NT, preferred_element_type=F32)


def fill_tx(cube, free, tx):
    chans, rows, cols = cube.shape
    lines = chans * rows
    values = cube[...].astype(F32).reshape(lines, cols)
    line = iota((lines, LANES), 0)
    lane = iota((lines, LANES), 1)
    marks = jnp.zeros((lines, LANES), F32)
    flags = free[...].astype(F32)
    for c in range(chans):
        marks = jnp.where(line // rows == c, flags[0:1, c : c + 1], marks)
    even = jnp.concatenate([values[:, cols - 3 :], values[:, : cols - 3]], axis=1)
    odd = jnp.concatenate([values[:, WIDTH - 3 :], values[:, : WIDTH - 3]], axis=1)
    for block in range(cols // WIDTH):
        source = odd if block % 2 else even
        start = block // 2 * LANES
        piece = source[:, start : start + LANES]
        tx[block] = jnp.where(lane == LANES - 1, marks, piece).astype(BF16)


def fill_first(taps, sky, height, w_one):
    spread = (iota((FEAT, LANES), 1) % FEAT == iota((FEAT, LANES), 0)).astype(BF16)
    rows = dot(taps, spread)
    r = iota((8, LANES), 0)
    lane = iota((8, LANES), 1)
    zero = jnp.zeros((8, LANES), F32)
    for tile in range(WINDOW_LANES // LANES):
        block = 4 * tile + lane // FEAT
        q = block % 6
        b = block // 6
        y = 2 * sky - 2 + q
        inside = (y >= 0) & (y < height)
        row_masks = [(r - q == dy) & inside for dy in range(3)]
        b_values = sorted({(4 * tile) // 6, (4 * tile + 3) // 6})
        masks = {}
        for bv in b_values:
            for dy in range(3):
                masks[bv, dy] = row_masks[dy] & (b == bv) if len(b_values) > 1 else row_masks[dy]
        for dx in range(3):
            parts = []
            for a in range(10):
                value = zero
                for bv in b_values:
                    dc = a - bv
                    if 0 <= dc <= 2:
                        for dy in range(3):
                            tap = (dc * 3 + dy) * 3 + dx
                            value = jnp.where(masks[bv, dy], rows[tap : tap + 1, :], value)
                parts.append(value)
            for half in range(5):
                both = jnp.concatenate([parts[2 * half], parts[2 * half + 1]], axis=0)
                base = 80 * dx + 16 * half
                w_one[base : base + 16, tile * LANES : (tile + 1) * LANES] = both.astype(BF16)
        w_one[240:256, tile * LANES : (tile + 1) * LANES] = jnp.zeros((16, LANES), BF16)


def fill_second(kernel, spread_taps, w_two):
    eye = (iota((FEAT, FEAT), 0) == iota((FEAT, FEAT), 1)).astype(BF16)
    source = iota((LANES, 4 * LANES), 0)
    target = iota((LANES, 4 * LANES), 1)
    spread = (source == target // LANES * FEAT + target % FEAT).astype(BF16)
    for t in range(7):
        count = min(4, 27 - 4 * t)
        part = kernel[4 * t : 4 * t + count].reshape(count * FEAT, FEAT)
        if count < 4:
            part = jnp.concatenate([part, jnp.zeros(((4 - count) * FEAT, FEAT), BF16)], axis=0)
        turned = dot_nt(eye, part).astype(BF16)
        wide = dot(turned, spread).astype(BF16)
        for g in range(count):
            spread_taps[4 * t + g] = wide[:, g * LANES : (g + 1) * LANES]
    group = iota((FEAT, LANES), 1) // FEAT
    zero = jnp.zeros((FEAT, LANES), BF16)
    for dx in range(3):
        for cin in range(4):
            for yin in range(6):
                base = (cin * 6 + yin) * FEAT
                for cout in range(2):
                    value = zero
                    dc = cin - cout
                    if 0 <= dc <= 2:
                        for yout in range(4):
                            dy = yin - yout
                            if 0 <= dy <= 2:
                                tap = spread_taps[(dc * 3 + dy) * 3 + dx]
                                value = jnp.where(group == yout, tap, value)
                    w_two[dx, base : base + FEAT, cout * LANES : (cout + 1) * LANES] = value


def fill_proposal(kernel, w_prop):
    wide = kernel.shape[3]
    zero = jnp.zeros((FEAT, wide), BF16)
    for dx in range(3):
        for moment in range(2):
            for y in range(4):
                base = ((dx * 2 + moment) * 4 + y) * FEAT
                for yout in range(2):
                    dy = y - yout
                    value = zero
                    if 0 <= dy <= 2:
                        value = kernel[dy, dx, moment * FEAT : (moment + 1) * FEAT, :]
                    w_prop[base : base + FEAT, yout * wide : (yout + 1) * wide] = value


def fill_heads(score, box, heads):
    lines = heads.shape[0]

    def picked(count, wanted):
        row = iota((lines, count), 0)
        return (wanted(row // SLAB, row % SLAB) == iota((lines, count), 1)).astype(BF16)

    from_score = picked(ANCHORS, lambda g, k: jnp.where((g == 0) & (k < ANCHORS), k, -1))
    from_box = picked(4 * ANCHORS, lambda g, k: jnp.where((g > 0) & (k < ANCHORS), 4 * k + g - 1, -1))
    heads[...] = (dot(from_score, score[...]) + dot(from_box, box[...])).astype(BF16)


def flatten(rx, lines, planes, freq, cols):
    blocks, rows, _ = rx.shape
    values = rx[...].astype(F32)
    marks = values[:, :, LANES - 1 :]
    total = jnp.sum(values * marks, axis=0)
    count = jnp.sum(jnp.broadcast_to(marks, values.shape), axis=0)
    total = functools.reduce(jnp.add, [total[2 * c : 2 * c + 2] for c in range(rows // 2)])
    count = functools.reduce(jnp.add, [count[2 * c : 2 * c + 2] for c in range(rows // 2)])
    baseline = total / jnp.maximum(count, 1.0)
    baseline = jnp.concatenate([baseline] * (rows // 2), axis=0)
    col = WIDTH * freq - 3 + iota((rows, LANES), 1)
    inside = (col >= 0) & (col < cols)
    for block in range(blocks):
        lines[block * rows : (block + 1) * rows, :] = jnp.where(inside, values[block] - baseline, 0.0)
    for y in range(2):
        planes[3 + y] = lines[pl.ds(y, CHANS, stride=2), :].astype(BF16)


def fill_shifted(planes, lines, shifted, sky, height):
    for r in range(8):
        y = 2 * sky - 3 + r
        value = planes[r].astype(F32)
        if r not in (3, 4):
            value = jnp.where((y >= 0) & (y < height), value, 0.0)
        lines[CHANS * r : CHANS * (r + 1), :] = value
    zero = jnp.zeros((8, LANES), F32)
    for pair in range(PAIRS):
        both = []
        for c in (2 * pair - 1, 2 * pair):
            both.append(lines[pl.ds(c, 8, stride=CHANS), :] if 0 <= c < CHANS else zero)
        for dx in range(3):
            moved = both if dx == 0 else [pltpu.roll(v, LANES - dx, 1) for v in both]
            shifted[dx, 16 * pair : 16 * pair + 16, :] = jnp.concatenate(moved, axis=0).astype(BF16)


def convolve_first(shifted, w_one, layer, freq, cols):
    j = iota((ROWS_ONE, LANES), 0)
    x = j % SLAB * STRIDE + j // SLAB
    col = WIDTH * freq - 2 + x
    inside = (x < WIDTH + 4) & (col >= 0) & (col < cols)
    turn = ((iota((ROWS_ONE, LANES), 1) == x) & inside).astype(BF16)
    zero = jnp.zeros((16, LANES), BF16)
    edge = jnp.zeros((ROWS_ONE, STEP), BF16)
    layer[:, :STEP] = edge
    layer[:, STEP * PAIRS :] = edge
    for w in range(CHANS // WINDOW):
        parts = [shifted[dx, 64 * w : 64 * w + 80, :] for dx in range(3)]
        lhs = dot_nt(turn, jnp.concatenate(parts + [zero], axis=0)).astype(BF16)
        for n in range(WINDOW_LANES // 256):
            value = dot(lhs, w_one[:, 256 * n : 256 * n + 256])
            base = STEP + w * WINDOW_LANES + 256 * n
            layer[:, base : base + 256] = jnp.maximum(value, 0.0).astype(BF16)


def convolve_second(layer, w_two):
    zeroth = jnp.zeros((ROWS_TWO, LANES), F32)
    first = jnp.zeros((ROWS_TWO, LANES), F32)
    for start in range(0, PAIRS, GROUP):
        pairs = range(start, min(PAIRS, start + GROUP))
        total = None
        for dx in range(3):
            parts = [
                layer[SLAB * dx : SLAB * dx + ROWS_TWO, STEP * p : STEP * p + SPAN] for p in pairs
            ]
            part = dot(jnp.concatenate(parts, axis=0), w_two[dx])
            total = part if total is None else total + part
        total = jnp.maximum(total, 0.0)
        for i, p in enumerate(pairs):
            for half in range(2):
                c = 2 * p - 1 + half
                if 0 <= c < CHANS:
                    value = total[
                        ROWS_TWO * i : ROWS_TWO * (i + 1), LANES * half : LANES * (half + 1)
                    ]
                    zeroth = zeroth + value
                    first = first + ((c + 0.5) / CHANS - 0.5) * value
    return zeroth * (1.0 / CHANS), first * (12.0 / CHANS)


def propose(zeroth, first, w_prop, heads, freq, sky, height, cols, objectness, proposals):
    maps = jnp.concatenate([zeroth, first], axis=1)
    y = 2 * sky - 1 + iota(maps.shape, 1) // FEAT % 4
    maps = jnp.where((y >= 0) & (y < height), maps, 0.0).astype(BF16)
    row = iota((3 * WIDTH, ROWS_TWO), 0)
    x = row % WIDTH + row // WIDTH
    col = WIDTH * freq - 1 + x
    j = iota((3 * WIDTH, ROWS_TWO), 1)
    turn = ((j % SLAB * STRIDE + j // SLAB == x) & (col >= 0) & (col < cols)).astype(BF16)
    framed = dot(turn, maps).astype(BF16)
    framed = jnp.concatenate([framed[WIDTH * dx : WIDTH * (dx + 1)] for dx in range(3)], axis=1)
    hidden = jnp.maximum(dot(framed, w_prop[...]), 0.0).astype(BF16)
    k = iota((SLAB, WIDTH), 0)
    anchor_width = jnp.ones((SLAB, WIDTH), F32)
    anchor_height = anchor_width
    for anchor in range(ANCHORS):
        scale = 4.0 * 2.0 ** (anchor // 3)
        root = (2.0 ** (anchor % 3 - 1)) ** 0.5
        anchor_width = jnp.where(k == anchor, scale * root, anchor_width)
        anchor_height = jnp.where(k == anchor, scale / root, anchor_height)
    centre_col = (WIDTH * freq + iota((SLAB, WIDTH), 1)).astype(F32) + 0.5
    wide = hidden.shape[1] // 2
    for row in range(2):
        out = dot_nt(heads[...], hidden[:, wide * row : wide * (row + 1)])
        score, dx, dy, dw, dh = [out[SLAB * g : SLAB * (g + 1)] for g in range(5)]
        centre_row = (2 * sky + row).astype(F32) + 0.5
        centre_x = centre_col + dx * anchor_width
        centre_y = centre_row + dy * anchor_height
        half_width = 0.5 * (anchor_width * jnp.exp(dw))
        half_height = 0.5 * (anchor_height * jnp.exp(dh))
        objectness[:, row, :] = score[:ANCHORS]
        corners = (
            centre_x - half_width,
            centre_y - half_height,
            centre_x + half_width,
            centre_y + half_height,
        )
        for side, corner in enumerate(corners):
            proposals[:, side, row, :] = (corner * (1.0 / 64.0))[:ANCHORS]


def body(
    shape,
    cube_hbm, free_hbm, taps_hbm, kernel_hbm, proposal_hbm, score_hbm, box_hbm,
    objectness, proposals,
    cube, free, taps, kernel, proposal, score, box,
    tx, rx, planes, lines, lines_all, shifted, w_one, spread_taps, w_two, w_prop, heads, layer,
    load_sem, send_sem, recv_sem, halo_send, halo_recv,
):
    freq_count, sky_count, height, cols = shape
    freq = lax.axis_index("freq")
    sky = lax.axis_index("sky")
    barrier = pltpu.get_barrier_semaphore()

    def freq_peer(i):
        return {"freq": lax.rem(freq + i, freq_count)}

    def sky_peer(i):
        return {"sky": lax.rem(sky + i + sky_count, sky_count)}

    def greet(i, carry):
        pl.semaphore_signal(barrier, inc=1, device_id=freq_peer(i), device_id_type=MESH)
        return carry

    lax.fori_loop(1, freq_count, greet, 0)
    for i in (-2, -1, 1, 2):
        pl.semaphore_signal(barrier, inc=1, device_id=sky_peer(i), device_id_type=MESH)

    moves = (
        (cube_hbm, cube), (free_hbm, free), (taps_hbm, taps), (kernel_hbm, kernel),
        (proposal_hbm, proposal), (score_hbm, score), (box_hbm, box),
    )
    loads = [
        pltpu.make_async_copy(source, target, load_sem.at[i])
        for i, (source, target) in enumerate(moves)
    ]
    for load in loads:
        load.start()
    loads[0].wait()
    loads[1].wait()
    fill_tx(cube, free, tx)

    def exchange(i):
        return pltpu.make_async_remote_copy(
            src_ref=tx.at[lax.rem(freq + i, freq_count)],
            dst_ref=rx.at[freq],
            send_sem=send_sem.at[i],
            recv_sem=recv_sem.at[i],
            device_id=freq_peer(i),
            device_id_type=MESH,
        )

    def send(i, carry):
        exchange(i).start()
        return carry

    def finish(i, carry):
        exchange(i).wait()
        return carry

    pl.semaphore_wait(barrier, freq_count + 3)
    lax.fori_loop(1, freq_count, send, 0)
    rx[freq] = tx[freq]
    for load in loads[2:]:
        load.wait()
    fill_first(taps[...], sky, height, w_one)
    fill_second(kernel, spread_taps, w_two)
    fill_proposal(proposal, w_prop)
    fill_heads(score, box, heads)
    lax.fori_loop(1, freq_count, finish, 0)

    flatten(rx, lines, planes, freq, cols)
    halos = []
    for n, (i, source, target) in enumerate(((1, 3, 1), (-1, 3, 5), (2, 4, 0), (-2, 3, 7))):
        size = 2 if abs(i) == 1 else 1
        halos.append(
            pltpu.make_async_remote_copy(
                src_ref=planes.at[pl.ds(source, size)],
                dst_ref=planes.at[pl.ds(target, size)],
                send_sem=halo_send.at[n],
                recv_sem=halo_recv.at[n],
                device_id=sky_peer(i),
                device_id_type=MESH,
            )
        )
    for halo in halos:
        halo.start()
    for halo in halos:
        halo.wait()
    fill_shifted(planes, lines_all, shifted, sky, height)
    convolve_first(shifted, w_one, layer, freq, cols)
    zeroth, first = convolve_second(layer, w_two)
    propose(zeroth, first, w_prop, heads, freq, sky, height, cols, objectness, proposals)


def on_device(sky_cube, free_mask, conv_first, conv_second, proposal_conv, score_head, box_head):
    freq_count = lax.axis_size("freq")
    sky_count = lax.axis_size("sky")
    chans, rows, cols = sky_cube.shape
    wide = proposal_conv.shape[3]
    taps = conv_first.transpose(1, 2, 3, 4, 0).reshape(27, FEAT)
    kernel = conv_second.transpose(2, 3, 4, 0, 1).reshape(27, FEAT, FEAT)
    free = free_mask.reshape(1, chans)
    operands = (sky_cube, free, taps, kernel, proposal_conv, score_head, box_head)
    scratch = [pltpu.VMEM(operand.shape, operand.dtype) for operand in operands] + [
        pltpu.VMEM((freq_count, chans * rows, LANES), BF16),
        pltpu.VMEM((freq_count, chans * rows, LANES), BF16),
        pltpu.VMEM((8, CHANS, LANES), BF16),
        pltpu.VMEM((2 * CHANS, LANES), F32),
        pltpu.VMEM((8 * CHANS, LANES), F32),
        pltpu.VMEM((3, 16 * PAIRS, LANES), BF16),
        pltpu.VMEM((256, WINDOW_LANES), BF16),
        pltpu.VMEM((27, FEAT, LANES), BF16),
        pltpu.VMEM((3, SPAN, 256), BF16),
        pltpu.VMEM((3 * 256, 2 * wide), BF16),
        pltpu.VMEM((5 * SLAB, wide), BF16),
        pltpu.VMEM((ROWS_ONE, STEP * (PAIRS + 1)), BF16),
        pltpu.SemaphoreType.DMA((len(operands),)),
        pltpu.SemaphoreType.DMA((freq_count,)),
        pltpu.SemaphoreType.DMA((freq_count,)),
        pltpu.SemaphoreType.DMA((4,)),
        pltpu.SemaphoreType.DMA((4,)),
    ]
    shape = (freq_count, sky_count, rows * sky_count, cols)
    return pl.pallas_call(
        functools.partial(body, shape),
        out_shape=(
            jax.ShapeDtypeStruct((ANCHORS, rows, WIDTH), F32),
            jax.ShapeDtypeStruct((ANCHORS, 4, rows, WIDTH), F32),
        ),
        in_specs=[pl.BlockSpec(memory_space=pl.ANY)] * len(operands),
        out_specs=(pl.BlockSpec(memory_space=pltpu.VMEM),) * 2,
        scratch_shapes=scratch,
        compiler_params=pltpu.CompilerParams(
            collective_id=0, has_side_effects=True, vmem_limit_bytes=40 * 1024 * 1024
        ),
    )(*operands)


def solution(mesh):
    in_specs = (P("freq", "sky", None), P("freq"), P(), P(), P(), P(), P())
    out_specs = (P(None, "sky", "freq"), P(None, None, "sky", "freq"))
    return jax.shard_map(
        on_device, mesh=mesh, in_specs=in_specs, out_specs=out_specs, check_vma=False
    )
```

```python
import functools

import jax
import jax.numpy as jnp
from jax import lax
from jax.experimental import pallas as pl
from jax.experimental.pallas import tpu as pltpu
from jax.sharding import PartitionSpec as P

F32 = jnp.float32
BF16 = jnp.bfloat16
MESH = pl.DeviceIdType.MESH
CHANS = 64
FEAT = 32
ANCHORS = 9
WIDTH = 64
LANES = 128
SLAB = 16
HEAD = 16
STRIDE = 9
ROWS_ONE = (STRIDE + 2) * SLAB
ROWS_TWO = STRIDE * SLAB
PAIRS = CHANS // 4
STEP = 2 * 6 * FEAT
SPAN = 2 * STEP
WINDOW = 8
WINDOW_LANES = WINDOW * 6 * FEAT
WINDOWS = CHANS // 2 // WINDOW
GROUP = 4
NT = (((1,), (1,)), ((), ()))


def iota(shape, dim):
    return lax.broadcasted_iota(jnp.int32, shape, dim)


def dot(a, b):
    return jnp.dot(a, b, preferred_element_type=F32)


def dot_nt(a, b):
    return lax.dot_general(a, b, NT, preferred_element_type=F32)


def fill_tx(cube, free, tx):
    chans, rows, cols = cube.shape
    lines = chans * rows
    values = cube[...].astype(F32).reshape(lines, cols)
    line = iota((lines, LANES), 0)
    lane = iota((lines, LANES), 1)
    marks = jnp.zeros((lines, LANES), F32)
    flags = free[...].astype(F32)
    for c in range(chans):
        marks = jnp.where(line // rows == c, flags[0:1, c : c + 1], marks)
    even = jnp.concatenate([values[:, cols - 3 :], values[:, : cols - 3]], axis=1)
    odd = jnp.concatenate([values[:, WIDTH - 3 :], values[:, : WIDTH - 3]], axis=1)
    for block in range(cols // WIDTH):
        source = odd if block % 2 else even
        start = block // 2 * LANES
        piece = source[:, start : start + LANES]
        tx[block] = jnp.where(lane == LANES - 1, marks, piece).astype(BF16)


def fill_first(taps, sky, height, w_one):
    spread = (iota((FEAT, LANES), 1) % FEAT == iota((FEAT, LANES), 0)).astype(BF16)
    rows = [dot(taps[i], spread) for i in range(9)]
    r = iota((8, LANES), 0)
    lane = iota((8, LANES), 1)
    zero = jnp.zeros((8, LANES), F32)
    for tile in range(WINDOW_LANES // LANES):
        block = 4 * tile + lane // FEAT
        q = block % 6
        b = block // 6
        y = 2 * sky - 2 + q
        inside = (y >= 0) & (y < height)
        row_masks = [(r - q == dy) & inside for dy in range(3)]
        b_values = sorted({(4 * tile) // 6, (4 * tile + 3) // 6})
        masks = {}
        for bv in b_values:
            for dy in range(3):
                masks[bv, dy] = row_masks[dy] & (b == bv) if len(b_values) > 1 else row_masks[dy]
        for dx in range(3):
            parts = []
            for a in range(10):
                value = zero
                for bv in b_values:
                    dc = a - bv
                    if 0 <= dc <= 2:
                        for dy in range(3):
                            tap = rows[dc * 3 + dy][dx : dx + 1, :]
                            value = jnp.where(masks[bv, dy], tap, value)
                parts.append(value)
            for half in range(5):
                both = jnp.concatenate([parts[2 * half], parts[2 * half + 1]], axis=0)
                base = 80 * dx + 16 * half
                w_one[base : base + 16, tile * LANES : (tile + 1) * LANES] = both.astype(BF16)
        w_one[240:256, tile * LANES : (tile + 1) * LANES] = jnp.zeros((16, LANES), BF16)


def fill_second(kernel, spread_taps, w_two):
    eye = (iota((FEAT, FEAT), 0) == iota((FEAT, FEAT), 1)).astype(BF16)
    source = iota((LANES, 4 * LANES), 0)
    target = iota((LANES, 4 * LANES), 1)
    spread = (source == target // LANES * FEAT + target % FEAT).astype(BF16)
    for t in range(7):
        count = min(4, 27 - 4 * t)
        part = kernel[4 * t : 4 * t + count].reshape(count * FEAT, FEAT)
        if count < 4:
            part = jnp.concatenate([part, jnp.zeros(((4 - count) * FEAT, FEAT), BF16)], axis=0)
        turned = dot_nt(eye, part).astype(BF16)
        wide = dot(turned, spread).astype(BF16)
        for g in range(count):
            spread_taps[4 * t + g] = wide[:, g * LANES : (g + 1) * LANES]
    group = iota((FEAT, LANES), 1) // FEAT
    zero = jnp.zeros((FEAT, LANES), BF16)
    for dx in range(3):
        for cin in range(4):
            for yin in range(6):
                base = (cin * 6 + yin) * FEAT
                for cout in range(2):
                    value = zero
                    dc = cin - cout
                    if 0 <= dc <= 2:
                        for yout in range(4):
                            dy = yin - yout
                            if 0 <= dy <= 2:
                                tap = spread_taps[(dc * 3 + dy) * 3 + dx]
                                value = jnp.where(group == yout, tap, value)
                    w_two[dx, base : base + FEAT, cout * LANES : (cout + 1) * LANES] = value


def fill_proposal(kernel, w_prop):
    wide = kernel.shape[3]
    zero = jnp.zeros((FEAT, wide), BF16)
    for dx in range(3):
        for moment in range(2):
            for y in range(4):
                base = ((dx * 2 + moment) * 4 + y) * FEAT
                for yout in range(2):
                    dy = y - yout
                    value = zero
                    if 0 <= dy <= 2:
                        value = kernel[dy, dx, moment * FEAT : (moment + 1) * FEAT, :]
                    w_prop[base : base + FEAT, yout * wide : (yout + 1) * wide] = value


def fill_heads(score, box, heads):
    lines = heads.shape[0]

    def picked(count, wanted):
        row = iota((lines, count), 0)
        return (wanted(row // HEAD, row % HEAD) == iota((lines, count), 1)).astype(BF16)

    from_score = picked(ANCHORS, lambda g, k: jnp.where((g == 0) & (k < ANCHORS), k, -1))
    from_box = picked(4 * ANCHORS, lambda g, k: jnp.where((g > 0) & (k < ANCHORS), 4 * k + g - 1, -1))
    heads[...] = (dot(from_score, score[...]) + dot(from_box, box[...])).astype(BF16)


def flatten(rx, lines, planes, freq, cols):
    blocks, rows, _ = rx.shape
    values = rx[...].astype(F32)
    marks = values[:, :, LANES - 1 :]
    total = jnp.sum(values * marks, axis=0)
    count = jnp.sum(jnp.broadcast_to(marks, values.shape), axis=0)
    total = functools.reduce(jnp.add, [total[2 * c : 2 * c + 2] for c in range(rows // 2)])
    count = functools.reduce(jnp.add, [count[2 * c : 2 * c + 2] for c in range(rows // 2)])
    baseline = total / jnp.maximum(count, 1.0)
    baseline = jnp.concatenate([baseline] * (rows // 2), axis=0)
    col = WIDTH * freq - 3 + iota((rows, LANES), 1)
    inside = (col >= 0) & (col < cols)
    for block in range(blocks):
        lines[block * rows : (block + 1) * rows, :] = jnp.where(inside, values[block] - baseline, 0.0)
    for y in range(2):
        planes[3 + y] = lines[pl.ds(y, CHANS, stride=2), :].astype(BF16)


def fill_shifted(planes, lines, shifted, sky, height):
    for r in range(8):
        y = 2 * sky - 3 + r
        value = planes[r].astype(F32)
        if r not in (3, 4):
            value = jnp.where((y >= 0) & (y < height), value, 0.0)
        lines[CHANS * r : CHANS * (r + 1), :] = value
    edge = jnp.zeros((16, LANES), BF16)
    for dx in range(3):
        shifted[dx, :16, :] = edge
        for start in range(8 * (CHANS + 2), shifted.shape[1], 16):
            shifted[dx, start : start + 16, :] = edge
    for c in range(0, CHANS, 2):
        both = [lines[pl.ds(c + i, 8, stride=CHANS), :] for i in range(2)]
        for dx in range(3):
            moved = both if dx == 0 else [pltpu.roll(v, LANES - dx, 1) for v in both]
            shifted[dx, 8 * c + 16 : 8 * c + 32, :] = jnp.concatenate(moved, axis=0).astype(BF16)


def convolve_first(shifted, w_one, layer, freq, cols):
    j = iota((ROWS_ONE, 2 * LANES), 0)
    lane = iota((ROWS_ONE, 2 * LANES), 1)
    x = j % 8 * STRIDE + j // SLAB
    col = WIDTH * freq - 2 + x
    inside = (x < WIDTH + 4) & (col >= 0) & (col < cols)
    turn = ((lane == x + j // 8 % 2 * LANES) & inside).astype(BF16)
    zero = jnp.zeros((16, LANES), BF16)
    blocks = []
    for w in range(WINDOWS + 1):
        halves = []
        for start in (64 * w, 64 * w + 8 * CHANS // 2):
            parts = [shifted[dx, start : start + 80, :] for dx in range(3)]
            halves.append(jnp.concatenate(parts + [zero], axis=0))
        blocks.append(dot_nt(turn, jnp.concatenate(halves, axis=1)).astype(BF16))
    lhs = jnp.concatenate(blocks, axis=0)
    row = iota((ROWS_ONE, 256), 0) // 8 % 2
    lane = iota((ROWS_ONE, 256), 1)
    for n in range(WINDOW_LANES // 256):
        count = WINDOWS + 1 if 256 * n < STEP else WINDOWS
        value = jnp.maximum(dot(lhs[: count * ROWS_ONE], w_one[:, 256 * n : 256 * n + 256]), 0.0)
        for w in range(count):
            part = value[ROWS_ONE * w : ROWS_ONE * (w + 1)]
            base = w * WINDOW_LANES + 256 * n
            if base == 0:
                part = jnp.where((row == 0) & (lane < STEP // 2), 0.0, part)
            if w == WINDOWS:
                part = jnp.where((row == 1) & (lane >= STEP // 2 - 256 * n), 0.0, part)
            part = part.astype(BF16)
            if base + 256 > layer.shape[1]:
                part = part[:, : layer.shape[1] - base]
            layer[:, base : base + part.shape[1]] = part


def convolve_second(layer, w_two):
    zeroth = jnp.zeros((ROWS_TWO, LANES), F32)
    first = jnp.zeros((ROWS_TWO, LANES), F32)
    for start in range(0, PAIRS, GROUP):
        pairs = range(start, start + GROUP)
        total = None
        for dx in range(3):
            parts = [
                layer[SLAB * dx : SLAB * dx + ROWS_TWO, STEP * p : STEP * p + SPAN] for p in pairs
            ]
            part = dot(jnp.concatenate(parts, axis=0), w_two[dx])
            total = part if total is None else total + part
        total = jnp.maximum(total, 0.0)
        for i, p in enumerate(pairs):
            for half in range(2):
                c = 2 * p + half
                value = total[
                    ROWS_TWO * i : ROWS_TWO * (i + 1), LANES * half : LANES * (half + 1)
                ]
                zeroth = zeroth + value
                first = first + ((c + 0.5) / CHANS - 0.5) * value
    low, high = [zeroth.reshape(STRIDE, 2, 8, LANES)[:, h].reshape(-1, LANES) for h in range(2)]
    parts = [first.reshape(STRIDE, 2, 8, LANES)[:, h].reshape(-1, LANES) for h in range(2)]
    first = parts[0] + parts[1] + 0.5 * high
    return (low + high) * (1.0 / CHANS), first * (12.0 / CHANS)


def propose(zeroth, first, w_prop, heads, freq, sky, height, cols, result):
    maps = jnp.concatenate([zeroth, first], axis=1)
    y = 2 * sky - 1 + iota(maps.shape, 1) // FEAT % 4
    maps = jnp.where((y >= 0) & (y < height), maps, 0.0).astype(BF16)
    row = iota((3 * WIDTH, 8 * STRIDE), 0)
    x = row % WIDTH + row // WIDTH
    col = WIDTH * freq - 1 + x
    j = iota((3 * WIDTH, 8 * STRIDE), 1)
    turn = ((j % 8 * STRIDE + j // 8 == x) & (col >= 0) & (col < cols)).astype(BF16)
    framed = dot(turn, maps).astype(BF16)
    framed = jnp.concatenate([framed[WIDTH * dx : WIDTH * (dx + 1)] for dx in range(3)], axis=1)
    hidden = jnp.maximum(dot(framed, w_prop[...]), 0.0).astype(BF16)
    k = iota((HEAD, WIDTH), 0)
    anchor_width = jnp.ones((HEAD, WIDTH), F32)
    anchor_height = anchor_width
    for anchor in range(ANCHORS):
        scale = 4.0 * 2.0 ** (anchor // 3)
        root = (2.0 ** (anchor % 3 - 1)) ** 0.5
        anchor_width = jnp.where(k == anchor, scale * root, anchor_width)
        anchor_height = jnp.where(k == anchor, scale / root, anchor_height)
    centre_col = (WIDTH * freq + iota((HEAD, WIDTH), 1)).astype(F32) + 0.5
    wide = hidden.shape[1] // 2
    for row in range(2):
        out = dot_nt(heads[...], hidden[:, wide * row : wide * (row + 1)])
        score, dx, dy, dw, dh = [out[HEAD * g : HEAD * (g + 1)] for g in range(5)]
        centre_row = (2 * sky + row).astype(F32) + 0.5
        centre_x = centre_col + dx * anchor_width
        centre_y = centre_row + dy * anchor_height
        half_width = 0.5 * (anchor_width * jnp.exp(dw))
        half_height = 0.5 * (anchor_height * jnp.exp(dh))
        result[:, 0, row, :] = score[:ANCHORS]
        corners = (
            centre_x - half_width,
            centre_y - half_height,
            centre_x + half_width,
            centre_y + half_height,
        )
        for side, corner in enumerate(corners):
            result[:, 1 + side, row, :] = (corner * (1.0 / 64.0))[:ANCHORS]


def body(
    shape,
    cube_hbm, free_hbm, taps_hbm, kernel_hbm, proposal_hbm, score_hbm, box_hbm,
    result,
    cube, free, taps, kernel, proposal, score, box,
    tx, rx, planes, lines, lines_all, shifted, w_one, spread_taps, w_two, w_prop, heads, layer,
    load_sem, send_sem, recv_sem, halo_send, halo_recv,
):
    freq_count, sky_count, height, cols = shape
    freq = lax.axis_index("freq")
    sky = lax.axis_index("sky")
    barrier = pltpu.get_barrier_semaphore()

    def freq_peer(i):
        return i + (i >= freq).astype(jnp.int32)

    def in_sky(i):
        return (sky + i >= 0) & (sky + i < sky_count)

    def greet(i, carry):
        peer = lax.rem(freq + freq_count // 2 + (i + 1) // 2 * (1 - 2 * (i % 2)) + freq_count, freq_count)
        pl.semaphore_signal(barrier, inc=1, device_id={"freq": peer}, device_id_type=MESH)
        return carry

    lax.fori_loop(0, freq_count - 1, greet, 0)
    neighbours = 0
    for i in (-2, -1, 1, 2):
        neighbours += in_sky(i).astype(jnp.int32)

        @pl.when(in_sky(i))
        def _():
            pl.semaphore_signal(barrier, inc=1, device_id={"sky": sky + i}, device_id_type=MESH)

    moves = (
        (cube_hbm, cube), (free_hbm, free), (taps_hbm, taps), (kernel_hbm, kernel),
        (proposal_hbm, proposal), (score_hbm, score), (box_hbm, box),
    )
    loads = [
        pltpu.make_async_copy(source, target, load_sem.at[i])
        for i, (source, target) in enumerate(moves)
    ]
    for load in loads:
        load.start()
    loads[0].wait()
    loads[1].wait()
    fill_tx(cube, free, tx)

    def exchange(peer):
        return pltpu.make_async_remote_copy(
            src_ref=tx.at[peer],
            dst_ref=rx.at[freq],
            send_sem=send_sem.at[peer],
            recv_sem=recv_sem.at[freq],
            device_id={"freq": peer},
            device_id_type=MESH,
        )

    def arrival(peer):
        return pltpu.make_async_remote_copy(
            src_ref=tx.at[peer],
            dst_ref=rx.at[peer],
            send_sem=send_sem.at[peer],
            recv_sem=recv_sem.at[peer],
            device_id={"freq": peer},
            device_id_type=MESH,
        )

    def send(i, carry):
        exchange(freq_peer(i)).start()
        return carry

    def finish(i, carry):
        arrival(freq_peer(i)).wait_recv()
        return carry

    def settle(i, carry):
        arrival(freq_peer(i)).wait_send()
        return carry

    pl.semaphore_wait(barrier, freq_count - 1 + neighbours)
    lax.fori_loop(0, freq_count - 1, send, 0)
    rx[freq] = tx[freq]
    for load in loads[2:]:
        load.wait()
    fill_first(taps, sky, height, w_one)
    fill_second(kernel, spread_taps, w_two)
    fill_proposal(proposal, w_prop)
    fill_heads(score, box, heads)
    lax.fori_loop(0, freq_count - 1, finish, 0)

    flatten(rx, lines, planes, freq, cols)
    halos = []
    for n, (i, source, target) in enumerate(((2, 4, 0), (-2, 3, 7), (1, 3, 1), (-1, 3, 5))):
        size = 2 if abs(i) == 1 else 1
        halo = pltpu.make_async_remote_copy(
            src_ref=planes.at[pl.ds(source, size)],
            dst_ref=planes.at[pl.ds(target, size)],
            send_sem=halo_send.at[n],
            recv_sem=halo_recv.at[n],
            device_id={"sky": sky + i},
            device_id_type=MESH,
        )
        halos.append((i, halo))
    for i, halo in halos:
        pl.when(in_sky(i))(halo.start)
    for i, halo in halos:
        pl.when(in_sky(-i))(halo.wait_recv)
    fill_shifted(planes, lines_all, shifted, sky, height)
    convolve_first(shifted, w_one, layer, freq, cols)
    zeroth, first = convolve_second(layer, w_two)
    propose(zeroth, first, w_prop, heads, freq, sky, height, cols, result)
    for i, halo in halos:
        pl.when(in_sky(i))(halo.wait_send)
    lax.fori_loop(0, freq_count - 1, settle, 0)


def on_device(sky_cube, free_mask, conv_first, conv_second, proposal_conv, score_head, box_head):
    freq_count = lax.axis_size("freq")
    sky_count = lax.axis_size("sky")
    chans, rows, cols = sky_cube.shape
    wide = proposal_conv.shape[3]
    taps = conv_first.transpose(1, 2, 3, 4, 0).reshape(9, 3, FEAT)
    kernel = conv_second.transpose(2, 3, 4, 0, 1).reshape(27, FEAT, FEAT)
    free = free_mask.reshape(1, chans)
    operands = (sky_cube, free, taps, kernel, proposal_conv, score_head, box_head)
    scratch = [pltpu.VMEM(operand.shape, operand.dtype) for operand in operands] + [
        pltpu.VMEM((freq_count, chans * rows, LANES), BF16),
        pltpu.VMEM((freq_count, chans * rows, LANES), BF16),
        pltpu.VMEM((8, CHANS, LANES), BF16),
        pltpu.VMEM((2 * CHANS, LANES), F32),
        pltpu.VMEM((8 * CHANS, LANES), F32),
        pltpu.VMEM((3, 8 * CHANS + 80, LANES), BF16),
        pltpu.VMEM((256, WINDOW_LANES), BF16),
        pltpu.VMEM((27, FEAT, LANES), BF16),
        pltpu.VMEM((3, SPAN, 256), BF16),
        pltpu.VMEM((3 * 256, 2 * wide), BF16),
        pltpu.VMEM((5 * HEAD, wide), BF16),
        pltpu.VMEM((ROWS_ONE, STEP * (PAIRS + 1)), BF16),
        pltpu.SemaphoreType.DMA((len(operands),)),
        pltpu.SemaphoreType.DMA((freq_count,)),
        pltpu.SemaphoreType.DMA((freq_count,)),
        pltpu.SemaphoreType.DMA((4,)),
        pltpu.SemaphoreType.DMA((4,)),
    ]
    shape = (freq_count, sky_count, rows * sky_count, cols)
    result = pl.pallas_call(
        functools.partial(body, shape),
        out_shape=pltpu.VMEM((ANCHORS, 5, rows, WIDTH), F32),
        in_specs=[pl.BlockSpec(memory_space=pltpu.HBM)] * len(operands),
        out_specs=pl.BlockSpec(memory_space=pltpu.VMEM),
        scratch_shapes=scratch,
        compiler_params=pltpu.CompilerParams(
            collective_id=0, has_side_effects=True, vmem_limit_bytes=60 * 1024 * 1024
        ),
    )(*operands)
    return result[:, 0], result[:, 1:]


def solution(mesh):
    in_specs = (P("freq", "sky", None), P("freq"), P(), P(), P(), P(), P())
    out_specs = (P(None, "sky", "freq"), P(None, None, "sky", "freq"))
    return jax.shard_map(
        on_device, mesh=mesh, in_specs=in_specs, out_specs=out_specs, check_vma=False
    )
```

```python
import functools

import jax
import jax.numpy as jnp
from jax import lax
from jax.experimental import pallas as pl
from jax.experimental.pallas import tpu as pltpu
from jax.sharding import PartitionSpec as P

F32 = jnp.float32
BF16 = jnp.bfloat16
MESH = pl.DeviceIdType.MESH
CHANS = 64
FEAT = 32
ANCHORS = 9
WIDTH = 64
LANES = 128
SLAB = 16
HEAD = 16
STRIDE = 9
ROWS_ONE = (STRIDE + 2) * SLAB
ROWS_TWO = STRIDE * SLAB
PAIRS = CHANS // 4
STEP = 2 * 6 * FEAT
SPAN = 2 * STEP
WINDOW = 8
WINDOW_LANES = WINDOW * 6 * FEAT
WINDOWS = CHANS // 2 // WINDOW
GROUP = 4
NT = (((1,), (1,)), ((), ()))


def iota(shape, dim):
    return lax.broadcasted_iota(jnp.int32, shape, dim)


def dot(a, b):
    return jnp.dot(a, b, preferred_element_type=F32)


def dot_nt(a, b):
    return lax.dot_general(a, b, NT, preferred_element_type=F32)


def fill_tx(cube, free, tx):
    chans, rows, cols = cube.shape
    lines = chans * rows
    values = cube[...].astype(F32).reshape(lines, cols)
    line = iota((lines, LANES), 0)
    lane = iota((lines, LANES), 1)
    marks = jnp.zeros((lines, LANES), F32)
    flags = free[...].astype(F32)
    for c in range(chans):
        marks = jnp.where(line // rows == c, flags[0:1, c : c + 1], marks)
    even = jnp.concatenate([values[:, cols - 3 :], values[:, : cols - 3]], axis=1)
    odd = jnp.concatenate([values[:, WIDTH - 3 :], values[:, : WIDTH - 3]], axis=1)
    for block in range(cols // WIDTH):
        source = odd if block % 2 else even
        start = block // 2 * LANES
        piece = source[:, start : start + LANES]
        tx[block] = jnp.where(lane == LANES - 1, marks, piece).astype(BF16)


def fill_first(taps, sky, height, w_one):
    spread = (iota((FEAT, LANES), 1) % FEAT == iota((FEAT, LANES), 0)).astype(BF16)
    rows = [dot(taps[i], spread) for i in range(9)]
    r = iota((8, LANES), 0)
    lane = iota((8, LANES), 1)
    zero = jnp.zeros((8, LANES), F32)
    for tile in range(WINDOW_LANES // LANES):
        block = 4 * tile + lane // FEAT
        q = block % 6
        b = block // 6
        y = 2 * sky - 2 + q
        inside = (y >= 0) & (y < height)
        row_masks = [(r - q == dy) & inside for dy in range(3)]
        b_values = sorted({(4 * tile) // 6, (4 * tile + 3) // 6})
        masks = {}
        for bv in b_values:
            for dy in range(3):
                masks[bv, dy] = row_masks[dy] & (b == bv) if len(b_values) > 1 else row_masks[dy]
        for dx in range(3):
            parts = []
            for a in range(10):
                value = zero
                for bv in b_values:
                    dc = a - bv
                    if 0 <= dc <= 2:
                        for dy in range(3):
                            tap = rows[dc * 3 + dy][dx : dx + 1, :]
                            value = jnp.where(masks[bv, dy], tap, value)
                parts.append(value)
            for half in range(5):
                both = jnp.concatenate([parts[2 * half], parts[2 * half + 1]], axis=0)
                base = 80 * dx + 16 * half
                w_one[base : base + 16, tile * LANES : (tile + 1) * LANES] = both.astype(BF16)
        w_one[240:256, tile * LANES : (tile + 1) * LANES] = jnp.zeros((16, LANES), BF16)


def fill_second(kernel, spread_taps, w_two):
    eye = (iota((FEAT, FEAT), 0) == iota((FEAT, FEAT), 1)).astype(BF16)
    source = iota((LANES, 4 * LANES), 0)
    target = iota((LANES, 4 * LANES), 1)
    spread = (source == target // LANES * FEAT + target % FEAT).astype(BF16)
    for t in range(7):
        count = min(4, 27 - 4 * t)
        part = kernel[4 * t : 4 * t + count].reshape(count * FEAT, FEAT)
        if count < 4:
            part = jnp.concatenate([part, jnp.zeros(((4 - count) * FEAT, FEAT), BF16)], axis=0)
        turned = dot_nt(eye, part).astype(BF16)
        wide = dot(turned, spread).astype(BF16)
        for g in range(count):
            spread_taps[4 * t + g] = wide[:, g * LANES : (g + 1) * LANES]
    group = iota((FEAT, LANES), 1) // FEAT
    zero = jnp.zeros((FEAT, LANES), BF16)
    for dx in range(3):
        for cin in range(4):
            for yin in range(6):
                base = (cin * 6 + yin) * FEAT
                for cout in range(2):
                    value = zero
                    dc = cin - cout
                    if 0 <= dc <= 2:
                        for yout in range(4):
                            dy = yin - yout
                            if 0 <= dy <= 2:
                                tap = spread_taps[(dc * 3 + dy) * 3 + dx]
                                value = jnp.where(group == yout, tap, value)
                    w_two[dx, base : base + FEAT, cout * LANES : (cout + 1) * LANES] = value


def fill_proposal(kernel, w_prop):
    wide = kernel.shape[3]
    zero = jnp.zeros((FEAT, wide), BF16)
    for dx in range(3):
        for moment in range(2):
            for y in range(4):
                base = ((dx * 2 + moment) * 4 + y) * FEAT
                for yout in range(2):
                    dy = y - yout
                    value = zero
                    if 0 <= dy <= 2:
                        value = kernel[dy, dx, moment * FEAT : (moment + 1) * FEAT, :]
                    w_prop[base : base + FEAT, yout * wide : (yout + 1) * wide] = value


def fill_heads(score, box, heads):
    lines = heads.shape[0]

    def picked(count, wanted):
        row = iota((lines, count), 0)
        return (wanted(row // HEAD, row % HEAD) == iota((lines, count), 1)).astype(BF16)

    from_score = picked(ANCHORS, lambda g, k: jnp.where((g == 0) & (k < ANCHORS), k, -1))
    from_box = picked(4 * ANCHORS, lambda g, k: jnp.where((g > 0) & (k < ANCHORS), 4 * k + g - 1, -1))
    heads[...] = (dot(from_score, score[...]) + dot(from_box, box[...])).astype(BF16)


def flatten(rx, lines, planes, freq, cols):
    blocks, rows, _ = rx.shape
    values = rx[...].astype(F32)
    marks = values[:, :, LANES - 1 :]
    total = jnp.sum(values * marks, axis=0)
    count = jnp.sum(jnp.broadcast_to(marks, values.shape), axis=0)
    total = functools.reduce(jnp.add, [total[2 * c : 2 * c + 2] for c in range(rows // 2)])
    count = functools.reduce(jnp.add, [count[2 * c : 2 * c + 2] for c in range(rows // 2)])
    baseline = total / jnp.maximum(count, 1.0)
    baseline = jnp.concatenate([baseline] * (rows // 2), axis=0)
    col = WIDTH * freq - 3 + iota((rows, LANES), 1)
    inside = (col >= 0) & (col < cols)
    for block in range(blocks):
        lines[block * rows : (block + 1) * rows, :] = jnp.where(inside, values[block] - baseline, 0.0)
    for y in range(2):
        planes[3 + y] = lines[pl.ds(y, CHANS, stride=2), :].astype(BF16)


def fill_shifted(planes, lines, shifted, sky, height):
    for r in range(8):
        y = 2 * sky - 3 + r
        value = planes[r].astype(F32)
        if r not in (3, 4):
            value = jnp.where((y >= 0) & (y < height), value, 0.0)
        lines[CHANS * r : CHANS * (r + 1), :] = value
    edge = jnp.zeros((16, LANES), BF16)
    for dx in range(3):
        shifted[dx, :16, :] = edge
        for start in range(8 * (CHANS + 2), shifted.shape[1], 16):
            shifted[dx, start : start + 16, :] = edge
    for c in range(0, CHANS, 2):
        both = [lines[pl.ds(c + i, 8, stride=CHANS), :] for i in range(2)]
        for dx in range(3):
            moved = both if dx == 0 else [pltpu.roll(v, LANES - dx, 1) for v in both]
            shifted[dx, 8 * c + 16 : 8 * c + 32, :] = jnp.concatenate(moved, axis=0).astype(BF16)


def convolve_first(shifted, w_one, layer, freq, cols):
    j = iota((ROWS_ONE, 2 * LANES), 0)
    lane = iota((ROWS_ONE, 2 * LANES), 1)
    x = j % 8 * STRIDE + j // SLAB
    col = WIDTH * freq - 2 + x
    inside = (x < WIDTH + 4) & (col >= 0) & (col < cols)
    turn = ((lane == x + j // 8 % 2 * LANES) & inside).astype(BF16)
    zero = jnp.zeros((16, LANES), BF16)
    blocks = []
    for w in range(WINDOWS + 1):
        halves = []
        for start in (64 * w, 64 * w + 8 * CHANS // 2):
            parts = [shifted[dx, start : start + 80, :] for dx in range(3)]
            halves.append(jnp.concatenate(parts + [zero], axis=0))
        blocks.append(dot_nt(turn, jnp.concatenate(halves, axis=1)).astype(BF16))
    lhs = jnp.concatenate(blocks, axis=0)
    row = iota((ROWS_ONE, 256), 0) // 8 % 2
    lane = iota((ROWS_ONE, 256), 1)
    for n in range(WINDOW_LANES // 256):
        count = WINDOWS + 1 if 256 * n < STEP else WINDOWS
        value = jnp.maximum(dot(lhs[: count * ROWS_ONE], w_one[:, 256 * n : 256 * n + 256]), 0.0)
        for w in range(count):
            part = value[ROWS_ONE * w : ROWS_ONE * (w + 1)]
            base = w * WINDOW_LANES + 256 * n
            if base == 0:
                part = jnp.where((row == 0) & (lane < STEP // 2), 0.0, part)
            if w == WINDOWS:
                part = jnp.where((row == 1) & (lane >= STEP // 2 - 256 * n), 0.0, part)
            part = part.astype(BF16)
            if base + 256 > layer.shape[1]:
                part = part[:, : layer.shape[1] - base]
            layer[:, base : base + part.shape[1]] = part


def convolve_second(layer, w_two):
    zeroth = jnp.zeros((ROWS_TWO, LANES), F32)
    first = jnp.zeros((ROWS_TWO, LANES), F32)
    for start in range(0, PAIRS, GROUP):
        pairs = range(start, start + GROUP)
        total = None
        for dx in range(3):
            parts = [
                layer[SLAB * dx : SLAB * dx + ROWS_TWO, STEP * p : STEP * p + SPAN] for p in pairs
            ]
            part = dot(jnp.concatenate(parts, axis=0), w_two[dx])
            total = part if total is None else total + part
        total = jnp.maximum(total, 0.0)
        for i, p in enumerate(pairs):
            for half in range(2):
                c = 2 * p + half
                value = total[
                    ROWS_TWO * i : ROWS_TWO * (i + 1), LANES * half : LANES * (half + 1)
                ]
                zeroth = zeroth + value
                first = first + ((c + 0.5) / CHANS - 0.5) * value
    low, high = [zeroth.reshape(STRIDE, 2, 8, LANES)[:, h].reshape(-1, LANES) for h in range(2)]
    parts = [first.reshape(STRIDE, 2, 8, LANES)[:, h].reshape(-1, LANES) for h in range(2)]
    first = parts[0] + parts[1] + 0.5 * high
    return (low + high) * (1.0 / CHANS), first * (12.0 / CHANS)


def propose(zeroth, first, w_prop, heads, freq, sky, height, cols, result):
    maps = jnp.concatenate([zeroth, first], axis=1)
    y = 2 * sky - 1 + iota(maps.shape, 1) // FEAT % 4
    maps = jnp.where((y >= 0) & (y < height), maps, 0.0).astype(BF16)
    row = iota((3 * WIDTH, 8 * STRIDE), 0)
    x = row % WIDTH + row // WIDTH
    col = WIDTH * freq - 1 + x
    j = iota((3 * WIDTH, 8 * STRIDE), 1)
    turn = ((j % 8 * STRIDE + j // 8 == x) & (col >= 0) & (col < cols)).astype(BF16)
    framed = dot(turn, maps).astype(BF16)
    framed = jnp.concatenate([framed[WIDTH * dx : WIDTH * (dx + 1)] for dx in range(3)], axis=1)
    hidden = jnp.maximum(dot(framed, w_prop[...]), 0.0).astype(BF16)
    k = iota((HEAD, WIDTH), 0)
    anchor_width = jnp.ones((HEAD, WIDTH), F32)
    anchor_height = anchor_width
    for anchor in range(ANCHORS):
        scale = 4.0 * 2.0 ** (anchor // 3)
        root = (2.0 ** (anchor % 3 - 1)) ** 0.5
        anchor_width = jnp.where(k == anchor, scale * root, anchor_width)
        anchor_height = jnp.where(k == anchor, scale / root, anchor_height)
    centre_col = (WIDTH * freq + iota((HEAD, WIDTH), 1)).astype(F32) + 0.5
    wide = hidden.shape[1] // 2
    for row in range(2):
        out = dot_nt(heads[...], hidden[:, wide * row : wide * (row + 1)])
        score, dx, dy, dw, dh = [out[HEAD * g : HEAD * (g + 1)] for g in range(5)]
        centre_row = (2 * sky + row).astype(F32) + 0.5
        centre_x = centre_col + dx * anchor_width
        centre_y = centre_row + dy * anchor_height
        half_width = 0.5 * (anchor_width * jnp.exp(dw))
        half_height = 0.5 * (anchor_height * jnp.exp(dh))
        result[:, 0, row, :] = score[:ANCHORS]
        corners = (
            centre_x - half_width,
            centre_y - half_height,
            centre_x + half_width,
            centre_y + half_height,
        )
        for side, corner in enumerate(corners):
            result[:, 1 + side, row, :] = (corner * (1.0 / 64.0))[:ANCHORS]


def body(
    shape,
    cube_hbm, free_hbm, taps_hbm, kernel_hbm, proposal_hbm, score_hbm, box_hbm,
    result,
    cube, free, taps, kernel, proposal, score, box,
    tx, rx, planes, lines, lines_all, shifted, w_one, spread_taps, w_two, w_prop, heads, layer,
    load_sem, send_sem, recv_sem, halo_send, halo_recv, late, clear,
):
    freq_count, sky_count, height, cols = shape
    freq = lax.axis_index("freq")
    sky = lax.axis_index("sky")
    barrier = pltpu.get_barrier_semaphore()
    cut = freq_count * 6 // 16
    is_first = freq < cut

    def freq_peer(i):
        return i + (i >= freq).astype(jnp.int32)

    def in_sky(i):
        return (sky + i >= 0) & (sky + i < sky_count)

    def greet(i, carry):
        peer = lax.rem(freq + freq_count // 2 + (i + 1) // 2 * (1 - 2 * (i % 2)) + freq_count, freq_count)
        pl.semaphore_signal(barrier, inc=1, device_id={"freq": peer}, device_id_type=MESH)
        return carry

    @pl.when(is_first)
    def _():
        for i in range(freq_count - 1):
            greet(i, 0)

    neighbours = 0
    for i in (-2, -1, 1, 2):
        neighbours += in_sky(i).astype(jnp.int32)

        @pl.when(in_sky(i))
        def _():
            pl.semaphore_signal(barrier, inc=1, device_id={"sky": sky + i}, device_id_type=MESH)

    moves = (
        (cube_hbm, cube), (free_hbm, free), (taps_hbm, taps), (kernel_hbm, kernel),
        (proposal_hbm, proposal), (score_hbm, score), (box_hbm, box),
    )
    loads = [
        pltpu.make_async_copy(source, target, load_sem.at[i])
        for i, (source, target) in enumerate(moves)
    ]
    for load in loads:
        load.start()
    pl.semaphore_wait(barrier, cut - is_first.astype(jnp.int32) + neighbours)

    def announce(i, carry):
        pl.semaphore_signal(late, inc=1, device_id={"freq": i}, device_id_type=MESH)
        return carry

    @pl.when(jnp.logical_not(is_first))
    def _():
        for i in range(cut):
            announce(i, 0)

    loads[0].wait()
    loads[1].wait()
    fill_tx(cube, free, tx)

    def exchange(peer):
        return pltpu.make_async_remote_copy(
            src_ref=tx.at[peer],
            dst_ref=rx.at[freq],
            send_sem=send_sem.at[peer],
            recv_sem=recv_sem.at[freq],
            device_id={"freq": peer},
            device_id_type=MESH,
        )

    def arrival(peer):
        return pltpu.make_async_remote_copy(
            src_ref=tx.at[peer],
            dst_ref=rx.at[peer],
            send_sem=send_sem.at[peer],
            recv_sem=recv_sem.at[peer],
            device_id={"freq": peer},
            device_id_type=MESH,
        )

    def send(peer):
        @pl.when(peer != freq)
        def _():
            exchange(peer).start()

    def release(i, carry):
        peer = cut + 2 * i + freq
        pl.semaphore_signal(clear, inc=1, device_id={"freq": peer}, device_id_type=MESH)
        return carry

    def finish(i):
        @pl.when(i != freq)
        def _():
            arrival(i).wait_recv()

    def settle(i):
        @pl.when(i != freq)
        def _():
            arrival(i).wait_send()

    for i in range(cut):
        send(i)
    rx[freq] = tx[freq]
    for load in loads[2:]:
        load.wait()
    fill_first(taps, sky, height, w_one)
    fill_second(kernel, spread_taps, w_two)
    fill_proposal(proposal, w_prop)
    fill_heads(score, box, heads)

    @pl.when(is_first)
    def _():
        pl.semaphore_wait(late, freq_count - cut)

    @pl.when(freq < 2)
    def _():
        for i in range((freq_count - cut) // 2):
            release(i, 0)

    @pl.when(jnp.logical_not(is_first))
    def _():
        pl.semaphore_wait(clear, 1)

    from_end = (freq >= freq_count * 3 // 16) & (freq < freq_count * 11 // 16)

    @pl.when(from_end)
    def _():
        for i in reversed(range(cut, freq_count)):
            send(i)

    @pl.when(jnp.logical_not(from_end))
    def _():
        for i in range(cut, freq_count):
            send(i)

    for i in range(freq_count):
        finish(i)

    flatten(rx, lines, planes, freq, cols)
    halos = []
    for n, (i, source, target) in enumerate(((2, 4, 0), (-2, 3, 7), (1, 3, 1), (-1, 3, 5))):
        size = 2 if abs(i) == 1 else 1
        halo = pltpu.make_async_remote_copy(
            src_ref=planes.at[pl.ds(source, size)],
            dst_ref=planes.at[pl.ds(target, size)],
            send_sem=halo_send.at[n],
            recv_sem=halo_recv.at[n],
            device_id={"sky": sky + i},
            device_id_type=MESH,
        )
        halos.append((i, halo))
    for i, halo in halos:
        pl.when(in_sky(i))(halo.start)
    for i, halo in halos:
        pl.when(in_sky(-i))(halo.wait_recv)
    fill_shifted(planes, lines_all, shifted, sky, height)
    convolve_first(shifted, w_one, layer, freq, cols)
    zeroth, first = convolve_second(layer, w_two)
    propose(zeroth, first, w_prop, heads, freq, sky, height, cols, result)
    for i, halo in halos:
        pl.when(in_sky(i))(halo.wait_send)
    for i in range(freq_count):
        settle(i)


def on_device(sky_cube, free_mask, conv_first, conv_second, proposal_conv, score_head, box_head):
    freq_count = lax.axis_size("freq")
    sky_count = lax.axis_size("sky")
    chans, rows, cols = sky_cube.shape
    wide = proposal_conv.shape[3]
    taps = conv_first.transpose(1, 2, 3, 4, 0).reshape(9, 3, FEAT)
    kernel = conv_second.transpose(2, 3, 4, 0, 1).reshape(27, FEAT, FEAT)
    free = free_mask.reshape(1, chans)
    operands = (sky_cube, free, taps, kernel, proposal_conv, score_head, box_head)
    scratch = [pltpu.VMEM(operand.shape, operand.dtype) for operand in operands] + [
        pltpu.VMEM((freq_count, chans * rows, LANES), BF16),
        pltpu.VMEM((freq_count, chans * rows, LANES), BF16),
        pltpu.VMEM((8, CHANS, LANES), BF16),
        pltpu.VMEM((2 * CHANS, LANES), F32),
        pltpu.VMEM((8 * CHANS, LANES), F32),
        pltpu.VMEM((3, 8 * CHANS + 80, LANES), BF16),
        pltpu.VMEM((256, WINDOW_LANES), BF16),
        pltpu.VMEM((27, FEAT, LANES), BF16),
        pltpu.VMEM((3, SPAN, 256), BF16),
        pltpu.VMEM((3 * 256, 2 * wide), BF16),
        pltpu.VMEM((5 * HEAD, wide), BF16),
        pltpu.VMEM((ROWS_ONE, STEP * (PAIRS + 1)), BF16),
        pltpu.SemaphoreType.DMA((len(operands),)),
        pltpu.SemaphoreType.DMA((freq_count,)),
        pltpu.SemaphoreType.DMA((freq_count,)),
        pltpu.SemaphoreType.DMA((4,)),
        pltpu.SemaphoreType.DMA((4,)),
        pltpu.SemaphoreType.REGULAR,
        pltpu.SemaphoreType.REGULAR,
    ]
    shape = (freq_count, sky_count, rows * sky_count, cols)
    result = pl.pallas_call(
        functools.partial(body, shape),
        out_shape=pltpu.VMEM((ANCHORS, 5, rows, WIDTH), F32),
        in_specs=[pl.BlockSpec(memory_space=pltpu.HBM)] * len(operands),
        out_specs=pl.BlockSpec(memory_space=pltpu.VMEM),
        scratch_shapes=scratch,
        compiler_params=pltpu.CompilerParams(
            collective_id=0, has_side_effects=True, vmem_limit_bytes=60 * 1024 * 1024
        ),
    )(*operands)
    return result[:, 0], result[:, 1:]


def solution(mesh):
    in_specs = (P("freq", "sky", None), P("freq"), P(), P(), P(), P(), P())
    out_specs = (P(None, "sky", "freq"), P(None, None, "sky", "freq"))
    return jax.shard_map(
        on_device, mesh=mesh, in_specs=in_specs, out_specs=out_specs, check_vma=False
    )
```

```python
import functools

import jax
import jax.numpy as jnp
from jax import lax
from jax.experimental import pallas as pl
from jax.experimental.pallas import tpu as pltpu
from jax.sharding import PartitionSpec as P

F32 = jnp.float32
BF16 = jnp.bfloat16
MESH = pl.DeviceIdType.MESH
CHANS = 64
FEAT = 32
ANCHORS = 9
WIDTH = 64
LANES = 128
SLAB = 16
HEAD = 16
STRIDE = 9
ROWS_ONE = (STRIDE + 2) * SLAB
ROWS_TWO = STRIDE * SLAB
PAIRS = CHANS // 4
EARLY = 2
LATE = 4
WINDOW = 8
WINDOWS = CHANS // 2 // WINDOW
GROUP = 4
NT = (((1,), (1,)), ((), ()))


def iota(shape, dim):
    return lax.broadcasted_iota(jnp.int32, shape, dim)


def dot(a, b):
    return jnp.dot(a, b, preferred_element_type=F32)


def dot_nt(a, b):
    return lax.dot_general(a, b, NT, preferred_element_type=F32)


def fill_tx(cube, free, tx):
    chans, rows, cols = cube.shape
    lines = chans * rows
    values = cube[...].astype(F32).reshape(lines, cols)
    line = iota((lines, LANES), 0)
    lane = iota((lines, LANES), 1)
    marks = jnp.zeros((lines, LANES), F32)
    flags = free[...].astype(F32)
    for c in range(chans):
        marks = jnp.where(line // rows == c, flags[0:1, c : c + 1], marks)
    even = jnp.concatenate([values[:, cols - 3 :], values[:, : cols - 3]], axis=1)
    odd = jnp.concatenate([values[:, WIDTH - 3 :], values[:, : WIDTH - 3]], axis=1)
    for block in range(cols // WIDTH):
        source = odd if block % 2 else even
        start = block // 2 * LANES
        piece = source[:, start : start + LANES]
        tx[block] = jnp.where(lane == LANES - 1, marks, piece).astype(BF16)


def late_row(index, odd):
    return index + 2 * (index >= jnp.where(odd, 1, 3)).astype(jnp.int32)


def fill_first(taps, sky, height, odd, w_early, w_late):
    spread = (iota((FEAT, LANES), 1) % FEAT == iota((FEAT, LANES), 0)).astype(BF16)
    rows = [dot(taps[i], spread) for i in range(9)]
    sub = iota((8, LANES), 0)
    lane = iota((8, LANES), 1)
    zero = jnp.zeros((8, LANES), F32)

    def store(target, base, tile, parts):
        for half in range(len(parts) // 2):
            both = jnp.concatenate([parts[2 * half], parts[2 * half + 1]], axis=0)
            start = base + 16 * half
            target[start : start + 16, tile * LANES : (tile + 1) * LANES] = both.astype(BF16)

    step_rows = [sub % 4 - lane // FEAT % 2 == dy for dy in range(3)]
    apart = sub // 4 - lane // (2 * FEAT)
    masks = {}
    for shift in range(-1, 4):
        for dc in range(3):
            if -1 <= dc - shift <= 1:
                for dy in range(3):
                    masks[shift, dc, dy] = step_rows[dy] & (apart == dc - shift)
    for tile in range(WINDOW * EARLY * FEAT // LANES):
        for dx in range(3):
            parts = []
            for pair in range(6):
                value = zero
                for dc in range(3):
                    for dy in range(3):
                        mask = masks.get((2 * pair - 2 * tile, dc, dy))
                        if mask is not None:
                            value = jnp.where(mask, rows[dc * 3 + dy][dx : dx + 1, :], value)
                parts.append(value)
            store(w_early, 48 * dx, tile, parts)
        w_early[144:256, tile * LANES : (tile + 1) * LANES] = jnp.zeros((112, LANES), BF16)

    q = late_row(lane // FEAT, odd)
    y = 2 * sky - 2 + q
    inside = (y >= 0) & (y < height)
    row_masks = [(sub - q == dy) & inside for dy in range(3)]
    for tile in range(WINDOW):
        for dx in range(3):
            parts = []
            for a in range(10):
                value = zero
                dc = a - tile
                if 0 <= dc <= 2:
                    for dy in range(3):
                        value = jnp.where(row_masks[dy], rows[dc * 3 + dy][dx : dx + 1, :], value)
                parts.append(value)
            store(w_late, 80 * dx, tile, parts)
        w_late[240:256, tile * LANES : (tile + 1) * LANES] = jnp.zeros((16, LANES), BF16)


def fill_second(kernel, odd, spread_taps, w_early, w_late):
    eye = (iota((FEAT, FEAT), 0) == iota((FEAT, FEAT), 1)).astype(BF16)
    source = iota((LANES, 4 * LANES), 0)
    target = iota((LANES, 4 * LANES), 1)
    spread = (source == target // LANES * FEAT + target % FEAT).astype(BF16)
    for t in range(7):
        count = min(4, 27 - 4 * t)
        part = kernel[4 * t : 4 * t + count].reshape(count * FEAT, FEAT)
        if count < 4:
            part = jnp.concatenate([part, jnp.zeros(((4 - count) * FEAT, FEAT), BF16)], axis=0)
        turned = dot_nt(eye, part).astype(BF16)
        wide = dot(turned, spread).astype(BF16)
        for g in range(count):
            spread_taps[4 * t + g] = wide[:, g * LANES : (g + 1) * LANES]
    lane = iota((FEAT, LANES), 1) // FEAT
    zero = jnp.zeros((FEAT, LANES), BF16)

    def block(dx, dc, offset):
        value = zero
        if 0 <= dc <= 2:
            for dy in range(3):
                tap = spread_taps[(dc * 3 + dy) * 3 + dx]
                value = jnp.where(lane == offset - dy, tap, value)
        return value

    for dx in range(3):
        for cin in range(4):
            for cout in range(2):
                lanes = slice(cout * LANES, (cout + 1) * LANES)
                for e in range(EARLY):
                    base = (cin * EARLY + e) * FEAT
                    q = jnp.where(odd, 1, 3) + e
                    w_early[dx, base : base + FEAT, lanes] = block(dx, cin - cout, q)
                for l in range(LATE):
                    base = (cin * LATE + l) * FEAT
                    w_late[dx, base : base + FEAT, lanes] = block(
                        dx, cin - cout, late_row(jnp.int32(l), odd)
                    )


def fill_proposal(kernel, w_prop):
    wide = kernel.shape[3]
    zero = jnp.zeros((FEAT, wide), BF16)
    for dx in range(3):
        for moment in range(2):
            for y in range(4):
                base = ((dx * 2 + moment) * 4 + y) * FEAT
                for yout in range(2):
                    dy = y - yout
                    value = zero
                    if 0 <= dy <= 2:
                        value = kernel[dy, dx, moment * FEAT : (moment + 1) * FEAT, :]
                    w_prop[base : base + FEAT, yout * wide : (yout + 1) * wide] = value


def fill_heads(score, box, heads):
    lines = heads.shape[0]

    def picked(count, wanted):
        row = iota((lines, count), 0)
        return (wanted(row // HEAD, row % HEAD) == iota((lines, count), 1)).astype(BF16)

    from_score = picked(ANCHORS, lambda g, k: jnp.where((g == 0) & (k < ANCHORS), k, -1))
    from_box = picked(4 * ANCHORS, lambda g, k: jnp.where((g > 0) & (k < ANCHORS), 4 * k + g - 1, -1))
    heads[...] = (dot(from_score, score[...]) + dot(from_box, box[...])).astype(BF16)


def flatten(rx, lines, planes, freq, cols):
    blocks, rows, _ = rx.shape
    values = rx[...].astype(F32)
    marks = values[:, :, LANES - 1 :]
    total = jnp.sum(values * marks, axis=0)
    count = jnp.sum(jnp.broadcast_to(marks, values.shape), axis=0)
    total = functools.reduce(jnp.add, [total[2 * c : 2 * c + 2] for c in range(rows // 2)])
    count = functools.reduce(jnp.add, [count[2 * c : 2 * c + 2] for c in range(rows // 2)])
    baseline = total / jnp.maximum(count, 1.0)
    baseline = jnp.concatenate([baseline] * (rows // 2), axis=0)
    col = WIDTH * freq - 3 + iota((rows, LANES), 1)
    inside = (col >= 0) & (col < cols)
    for block in range(blocks):
        lines[block * rows : (block + 1) * rows, :] = jnp.where(inside, values[block] - baseline, 0.0)
    for y in range(2):
        planes[3 + y] = lines[pl.ds(y, CHANS, stride=2), :].astype(BF16)


def shift_columns(lines, shifted):
    for start in range(0, lines.shape[0], 16):
        part = lines[start : start + 16, :]
        for dx in range(3):
            moved = part if dx == 0 else pltpu.roll(part, LANES - dx, 1)
            shifted[dx, start : start + 16, :] = moved.astype(BF16)


def clear_edges(lines, count):
    for start, stop in ((0, 2 * count), ((CHANS + 2) * count, lines.shape[0])):
        lines[start:stop, :] = jnp.zeros((stop - start, LANES), F32)


def columns_to_rows(shifted, count, span, freq, cols):
    j = iota((ROWS_ONE, 2 * LANES), 0)
    lane = iota((ROWS_ONE, 2 * LANES), 1)
    x = j % 8 * STRIDE + j // SLAB
    col = WIDTH * freq - 2 + x
    inside = (x < WIDTH + 4) & (col >= 0) & (col < cols)
    turn = ((lane == x + j // 8 % 2 * LANES) & inside).astype(BF16)
    zero = jnp.zeros((256 - 3 * span, LANES), BF16)
    blocks = []
    for w in range(WINDOWS + 1):
        halves = []
        for start in (WINDOW * count * w, WINDOW * count * w + count * CHANS // 2):
            parts = [shifted[dx, start : start + span, :] for dx in range(3)]
            halves.append(jnp.concatenate(parts + [zero], axis=0))
        blocks.append(dot_nt(turn, jnp.concatenate(halves, axis=1)).astype(BF16))
    return jnp.concatenate(blocks, axis=0)


def convolve_first(lhs, weights, layer):
    lanes = weights.shape[1]
    chan = lanes // WINDOW
    tail = layer.shape[1] - WINDOWS * lanes
    row = iota((ROWS_ONE, 256), 0) // 8 % 2
    lane = iota((ROWS_ONE, 256), 1)
    for n in range(lanes // 256):
        count = WINDOWS + 1 if 256 * n < tail else WINDOWS
        value = jnp.maximum(dot(lhs[: count * ROWS_ONE], weights[:, 256 * n : 256 * n + 256]), 0.0)
        for w in range(count):
            part = value[ROWS_ONE * w : ROWS_ONE * (w + 1)]
            base = w * lanes + 256 * n
            if base == 0:
                part = jnp.where((row == 0) & (lane < chan), 0.0, part)
            if w == WINDOWS:
                part = jnp.where((row == 1) & (lane >= chan - 256 * n), 0.0, part)
            part = part[:, : min(256, layer.shape[1] - base)].astype(BF16)
            layer[:, base : base + part.shape[1]] = part


def convolve_second(layer, weights, pairs):
    span = weights.shape[1]
    step = span // 2
    total = None
    for dx in range(3):
        parts = [layer[SLAB * dx : SLAB * dx + ROWS_TWO, step * p : step * p + span] for p in pairs]
        part = dot(jnp.concatenate(parts, axis=0), weights[dx])
        total = part if total is None else total + part
    return total


def groups():
    return [range(start, start + GROUP) for start in range(0, PAIRS, GROUP)]


def sum_moments(layer, weights, partial):
    zeroth = jnp.zeros((ROWS_TWO, LANES), F32)
    first = jnp.zeros((ROWS_TWO, LANES), F32)
    for pairs in groups():
        rows = pl.ds(pairs[0] * ROWS_TWO, GROUP * ROWS_TWO)
        total = jnp.maximum(convolve_second(layer, weights, pairs) + partial[rows, :], 0.0)
        for i, p in enumerate(pairs):
            for half in range(2):
                c = 2 * p + half
                value = total[
                    ROWS_TWO * i : ROWS_TWO * (i + 1), LANES * half : LANES * (half + 1)
                ]
                zeroth = zeroth + value
                first = first + ((c + 0.5) / CHANS - 0.5) * value
    low, high = [zeroth.reshape(STRIDE, 2, 8, LANES)[:, h].reshape(-1, LANES) for h in range(2)]
    parts = [first.reshape(STRIDE, 2, 8, LANES)[:, h].reshape(-1, LANES) for h in range(2)]
    first = parts[0] + parts[1] + 0.5 * high
    return (low + high) * (1.0 / CHANS), first * (12.0 / CHANS)


def propose(zeroth, first, w_prop, heads, freq, sky, height, cols, result):
    maps = jnp.concatenate([zeroth, first], axis=1)
    y = 2 * sky - 1 + iota(maps.shape, 1) // FEAT % 4
    maps = jnp.where((y >= 0) & (y < height), maps, 0.0).astype(BF16)
    row = iota((3 * WIDTH, 8 * STRIDE), 0)
    x = row % WIDTH + row // WIDTH
    col = WIDTH * freq - 1 + x
    j = iota((3 * WIDTH, 8 * STRIDE), 1)
    turn = ((j % 8 * STRIDE + j // 8 == x) & (col >= 0) & (col < cols)).astype(BF16)
    framed = dot(turn, maps).astype(BF16)
    framed = jnp.concatenate([framed[WIDTH * dx : WIDTH * (dx + 1)] for dx in range(3)], axis=1)
    hidden = jnp.maximum(dot(framed, w_prop[...]), 0.0).astype(BF16)
    k = iota((HEAD, WIDTH), 0)
    anchor_width = jnp.ones((HEAD, WIDTH), F32)
    anchor_height = anchor_width
    for anchor in range(ANCHORS):
        scale = 4.0 * 2.0 ** (anchor // 3)
        root = (2.0 ** (anchor % 3 - 1)) ** 0.5
        anchor_width = jnp.where(k == anchor, scale * root, anchor_width)
        anchor_height = jnp.where(k == anchor, scale / root, anchor_height)
    centre_col = (WIDTH * freq + iota((HEAD, WIDTH), 1)).astype(F32) + 0.5
    wide = hidden.shape[1] // 2
    for row in range(2):
        out = dot_nt(heads[...], hidden[:, wide * row : wide * (row + 1)])
        score, dx, dy, dw, dh = [out[HEAD * g : HEAD * (g + 1)] for g in range(5)]
        centre_row = (2 * sky + row).astype(F32) + 0.5
        centre_x = centre_col + dx * anchor_width
        centre_y = centre_row + dy * anchor_height
        half_width = 0.5 * (anchor_width * jnp.exp(dw))
        half_height = 0.5 * (anchor_height * jnp.exp(dh))
        result[:, 0, row, :] = score[:ANCHORS]
        corners = (
            centre_x - half_width,
            centre_y - half_height,
            centre_x + half_width,
            centre_y + half_height,
        )
        for side, corner in enumerate(corners):
            result[:, 1 + side, row, :] = (corner * (1.0 / 64.0))[:ANCHORS]


def body(
    shape,
    cube_hbm, free_hbm, taps_hbm, kernel_hbm, proposal_hbm, score_hbm, box_hbm,
    result,
    cube, free, taps, kernel, proposal, score, box,
    tx, rx, planes, lines, lines_early, lines_late, shifted_early, shifted_late, w_one_early, w_one_late,
    spread_taps, w_two_early, w_two_late, w_prop, heads, layer_early, layer_late, partial,
    load_sem, send_sem, recv_sem, halo_send, halo_recv, late, clear,
):
    freq_count, sky_count, height, cols = shape
    freq = lax.axis_index("freq")
    sky = lax.axis_index("sky")
    odd = lax.rem(sky, 2) == 1
    barrier = pltpu.get_barrier_semaphore()
    cut = max(2, freq_count * 3 // 8 // 2 * 2)
    is_first = freq < cut

    def freq_peer(i):
        return i + (i >= freq).astype(jnp.int32)

    def in_sky(i):
        return (sky + i >= 0) & (sky + i < sky_count)

    def greet(i, carry):
        peer = lax.rem(freq + freq_count // 2 + (i + 1) // 2 * (1 - 2 * (i % 2)) + freq_count, freq_count)
        pl.semaphore_signal(barrier, inc=1, device_id={"freq": peer}, device_id_type=MESH)
        return carry

    @pl.when(is_first)
    def _():
        for i in range(freq_count - 1):
            greet(i, 0)

    neighbours = 0
    for i in (-2, -1, 1, 2):
        neighbours += in_sky(i).astype(jnp.int32)

        @pl.when(in_sky(i))
        def _():
            pl.semaphore_signal(barrier, inc=1, device_id={"sky": sky + i}, device_id_type=MESH)

    moves = (
        (cube_hbm, cube), (free_hbm, free), (taps_hbm, taps), (kernel_hbm, kernel),
        (proposal_hbm, proposal), (score_hbm, score), (box_hbm, box),
    )
    loads = [
        pltpu.make_async_copy(source, target, load_sem.at[i])
        for i, (source, target) in enumerate(moves)
    ]
    for load in loads:
        load.start()
    pl.semaphore_wait(barrier, cut - is_first.astype(jnp.int32) + neighbours)

    def announce(i, carry):
        pl.semaphore_signal(late, inc=1, device_id={"freq": i}, device_id_type=MESH)
        return carry

    @pl.when(jnp.logical_not(is_first))
    def _():
        for i in range(cut):
            announce(i, 0)

    loads[0].wait()
    loads[1].wait()
    fill_tx(cube, free, tx)

    def exchange(peer):
        return pltpu.make_async_remote_copy(
            src_ref=tx.at[peer],
            dst_ref=rx.at[freq],
            send_sem=send_sem.at[peer],
            recv_sem=recv_sem.at[freq],
            device_id={"freq": peer},
            device_id_type=MESH,
        )

    def arrival(peer):
        return pltpu.make_async_remote_copy(
            src_ref=tx.at[peer],
            dst_ref=rx.at[peer],
            send_sem=send_sem.at[peer],
            recv_sem=recv_sem.at[peer],
            device_id={"freq": peer},
            device_id_type=MESH,
        )

    def send(peer):
        @pl.when(peer != freq)
        def _():
            exchange(peer).start()

    def release(i, carry):
        peer = cut + 2 * i + freq
        pl.semaphore_signal(clear, inc=1, device_id={"freq": peer}, device_id_type=MESH)
        return carry

    def finish(i):
        @pl.when(i != freq)
        def _():
            arrival(i).wait_recv()

    def settle(i):
        @pl.when(i != freq)
        def _():
            arrival(i).wait_send()

    for i in range(cut):
        send(i)
    rx[freq] = tx[freq]
    for load in loads[2:]:
        load.wait()
    fill_first(taps, sky, height, odd, w_one_early, w_one_late)
    fill_second(kernel, odd, spread_taps, w_two_early, w_two_late)
    fill_proposal(proposal, w_prop)
    fill_heads(score, box, heads)
    clear_edges(lines_early, 4)
    clear_edges(lines_late, 8)

    @pl.when(is_first)
    def _():
        pl.semaphore_wait(late, freq_count - cut)

    @pl.when(freq < 2)
    def _():
        for i in range((freq_count - cut) // 2):
            release(i, 0)

    @pl.when(jnp.logical_not(is_first))
    def _():
        pl.semaphore_wait(clear, 1)

    from_end = (freq >= freq_count * 3 // 16) & (freq < freq_count * 11 // 16)

    @pl.when(from_end)
    def _():
        for i in reversed(range(cut, freq_count)):
            send(i)

    @pl.when(jnp.logical_not(from_end))
    def _():
        for i in range(cut, freq_count):
            send(i)

    for i in range(freq_count):
        finish(i)

    flatten(rx, lines, planes, freq, cols)
    halos = []
    for n, (i, source, target) in enumerate(((2, 4, 0), (-2, 3, 7), (1, 3, 1), (-1, 3, 5))):
        size = 2 if abs(i) == 1 else 1
        halo = pltpu.make_async_remote_copy(
            src_ref=planes.at[pl.ds(source, size)],
            dst_ref=planes.at[pl.ds(target, size)],
            send_sem=halo_send.at[n],
            recv_sem=halo_recv.at[n],
            device_id={"sky": sky + i},
            device_id_type=MESH,
        )
        halos.append((i, halo))
    for i, halo in halos:
        pl.when(in_sky(i))(halo.start)
    mate = dict(halos)
    pl.when(odd)(mate[1].wait_recv)
    pl.when(jnp.logical_not(odd))(mate[-1].wait_recv)
    for i in range(4):
        lines_early[pl.ds(8 + i, CHANS, stride=4), :] = planes[jnp.where(odd, 1, 3) + i].astype(F32)
    shift_columns(lines_early, shifted_early)
    convolve_first(
        columns_to_rows(shifted_early, 4, 48, freq, cols), w_one_early, layer_early
    )
    for pairs in groups():
        rows = pl.ds(pairs[0] * ROWS_TWO, GROUP * ROWS_TWO)
        partial[rows, :] = convolve_second(layer_early, w_two_early, pairs)

    for i, halo in halos:
        if abs(i) == 2:
            pl.when(in_sky(-i))(halo.wait_recv)
    pl.when(jnp.logical_not(odd) & in_sky(-1))(mate[1].wait_recv)
    pl.when(odd & in_sky(1))(mate[-1].wait_recv)
    for r in range(8):
        y = 2 * sky - 3 + r
        value = planes[r].astype(F32)
        if r not in (3, 4):
            value = jnp.where((y >= 0) & (y < height), value, 0.0)
        lines_late[pl.ds(16 + r, CHANS, stride=8), :] = value
    shift_columns(lines_late, shifted_late)
    convolve_first(columns_to_rows(shifted_late, 8, 80, freq, cols), w_one_late, layer_late)
    zeroth, first = sum_moments(layer_late, w_two_late, partial)
    propose(zeroth, first, w_prop, heads, freq, sky, height, cols, result)
    for i, halo in halos:
        pl.when(in_sky(i))(halo.wait_send)
    for i in range(freq_count):
        settle(i)


def on_device(sky_cube, free_mask, conv_first, conv_second, proposal_conv, score_head, box_head):
    freq_count = lax.axis_size("freq")
    sky_count = lax.axis_size("sky")
    chans, rows, cols = sky_cube.shape
    wide = proposal_conv.shape[3]
    taps = conv_first.transpose(1, 2, 3, 4, 0).reshape(9, 3, FEAT)
    kernel = conv_second.transpose(2, 3, 4, 0, 1).reshape(27, FEAT, FEAT)
    free = free_mask.reshape(1, chans)
    operands = (sky_cube, free, taps, kernel, proposal_conv, score_head, box_head)
    scratch = [pltpu.VMEM(operand.shape, operand.dtype) for operand in operands] + [
        pltpu.VMEM((freq_count, chans * rows, LANES), BF16),
        pltpu.VMEM((freq_count, chans * rows, LANES), BF16),
        pltpu.VMEM((8, CHANS, LANES), BF16),
        pltpu.VMEM((2 * CHANS, LANES), F32),
        pltpu.VMEM((4 * CHANS + 48, LANES), F32),
        pltpu.VMEM((8 * CHANS + 80, LANES), F32),
        pltpu.VMEM((3, 4 * CHANS + 48, LANES), BF16),
        pltpu.VMEM((3, 8 * CHANS + 80, LANES), BF16),
        pltpu.VMEM((256, WINDOW * EARLY * FEAT), BF16),
        pltpu.VMEM((256, WINDOW * LATE * FEAT), BF16),
        pltpu.VMEM((27, FEAT, LANES), BF16),
        pltpu.VMEM((3, 4 * EARLY * FEAT, 256), BF16),
        pltpu.VMEM((3, 4 * LATE * FEAT, 256), BF16),
        pltpu.VMEM((3 * 256, 2 * wide), BF16),
        pltpu.VMEM((5 * HEAD, wide), BF16),
        pltpu.VMEM((ROWS_ONE, 2 * (PAIRS + 1) * EARLY * FEAT), BF16),
        pltpu.VMEM((ROWS_ONE, 2 * (PAIRS + 1) * LATE * FEAT), BF16),
        pltpu.VMEM((PAIRS * ROWS_TWO, 256), F32),
        pltpu.SemaphoreType.DMA((len(operands),)),
        pltpu.SemaphoreType.DMA((freq_count,)),
        pltpu.SemaphoreType.DMA((freq_count,)),
        pltpu.SemaphoreType.DMA((4,)),
        pltpu.SemaphoreType.DMA((4,)),
        pltpu.SemaphoreType.REGULAR,
        pltpu.SemaphoreType.REGULAR,
    ]
    shape = (freq_count, sky_count, rows * sky_count, cols)
    result = pl.pallas_call(
        functools.partial(body, shape),
        out_shape=pltpu.VMEM((ANCHORS, 5, rows, WIDTH), F32),
        in_specs=[pl.BlockSpec(memory_space=pltpu.HBM)] * len(operands),
        out_specs=pl.BlockSpec(memory_space=pltpu.VMEM),
        scratch_shapes=scratch,
        compiler_params=pltpu.CompilerParams(
            collective_id=0, has_side_effects=True, vmem_limit_bytes=60 * 1024 * 1024
        ),
    )(*operands)
    return result[:, 0], result[:, 1:]


def solution(mesh):
    in_specs = (P("freq", "sky", None), P("freq"), P(), P(), P(), P(), P())
    out_specs = (P(None, "sky", "freq"), P(None, None, "sky", "freq"))
    return jax.shard_map(
        on_device, mesh=mesh, in_specs=in_specs, out_specs=out_specs, check_vma=False
    )
```

```python
import functools

import jax
import jax.numpy as jnp
from jax import lax
from jax.experimental import pallas as pl
from jax.experimental.pallas import tpu as pltpu
from jax.sharding import PartitionSpec as P

F32 = jnp.float32
BF16 = jnp.bfloat16
MESH = pl.DeviceIdType.MESH
CHANS = 64
FEAT = 32
ANCHORS = 9
WIDTH = 64
LANES = 128
SLAB = 16
HEAD = 16
STRIDE = 9
ROWS_ONE = (STRIDE + 2) * SLAB
ROWS_TWO = STRIDE * SLAB
PAIRS = CHANS // 4
EARLY = 2
LATE = 4
WINDOW = 8
WINDOWS = CHANS // 2 // WINDOW
GROUP = 4
NT = (((1,), (1,)), ((), ()))


def iota(shape, dim):
    return lax.broadcasted_iota(jnp.int32, shape, dim)


def dot(a, b):
    return jnp.dot(a, b, preferred_element_type=F32)


def dot_nt(a, b):
    return lax.dot_general(a, b, NT, preferred_element_type=F32)


def fill_tx(cube, free, tx):
    chans, rows, cols = cube.shape
    lines = chans * rows
    values = cube[...].astype(F32).reshape(lines, cols)
    line = iota((lines, LANES), 0)
    lane = iota((lines, LANES), 1)
    marks = jnp.zeros((lines, LANES), F32)
    flags = free[...].astype(F32)
    for c in range(chans):
        marks = jnp.where(line // rows == c, flags[0:1, c : c + 1], marks)
    even = jnp.concatenate([values[:, cols - 3 :], values[:, : cols - 3]], axis=1)
    odd = jnp.concatenate([values[:, WIDTH - 3 :], values[:, : WIDTH - 3]], axis=1)
    for block in range(cols // WIDTH):
        source = odd if block % 2 else even
        start = block // 2 * LANES
        piece = source[:, start : start + LANES]
        tx[block] = jnp.where(lane == LANES - 1, marks, piece).astype(BF16)


def late_row(index, odd):
    return index + 2 * (index >= jnp.where(odd, 1, 3)).astype(jnp.int32)


def fill_first(taps, sky, height, odd, w_early, w_late):
    spread = (iota((FEAT, LANES), 1) % FEAT == iota((FEAT, LANES), 0)).astype(BF16)
    rows = [dot(taps[i], spread) for i in range(9)]
    sub = iota((8, LANES), 0)
    lane = iota((8, LANES), 1)
    zero = jnp.zeros((8, LANES), F32)

    def store(target, base, tile, parts):
        for half in range(len(parts) // 2):
            both = jnp.concatenate([parts[2 * half], parts[2 * half + 1]], axis=0)
            start = base + 16 * half
            target[start : start + 16, tile * LANES : (tile + 1) * LANES] = both.astype(BF16)

    step_rows = [sub % 4 - lane // FEAT % 2 == dy for dy in range(3)]
    apart = sub // 4 - lane // (2 * FEAT)
    masks = {}
    for shift in range(-1, 4):
        for dc in range(3):
            if -1 <= dc - shift <= 1:
                for dy in range(3):
                    masks[shift, dc, dy] = step_rows[dy] & (apart == dc - shift)
    for tile in range(WINDOW * EARLY * FEAT // LANES):
        for dx in range(3):
            parts = []
            for pair in range(6):
                value = zero
                for dc in range(3):
                    for dy in range(3):
                        mask = masks.get((2 * pair - 2 * tile, dc, dy))
                        if mask is not None:
                            value = jnp.where(mask, rows[dc * 3 + dy][dx : dx + 1, :], value)
                parts.append(value)
            store(w_early, 48 * dx, tile, parts)
        w_early[144:256, tile * LANES : (tile + 1) * LANES] = jnp.zeros((112, LANES), BF16)

    q = late_row(lane // FEAT, odd)
    y = 2 * sky - 2 + q
    inside = (y >= 0) & (y < height)
    row_masks = [(sub - q == dy) & inside for dy in range(3)]
    for tile in range(WINDOW):
        for dx in range(3):
            parts = []
            for a in range(10):
                value = zero
                dc = a - tile
                if 0 <= dc <= 2:
                    for dy in range(3):
                        value = jnp.where(row_masks[dy], rows[dc * 3 + dy][dx : dx + 1, :], value)
                parts.append(value)
            store(w_late, 80 * dx, tile, parts)
        w_late[240:256, tile * LANES : (tile + 1) * LANES] = jnp.zeros((16, LANES), BF16)


def fill_second(kernel, odd, spread_taps, w_early, w_late):
    eye = (iota((FEAT, FEAT), 0) == iota((FEAT, FEAT), 1)).astype(BF16)
    source = iota((LANES, 4 * LANES), 0)
    target = iota((LANES, 4 * LANES), 1)
    spread = (source == target // LANES * FEAT + target % FEAT).astype(BF16)
    for t in range(7):
        count = min(4, 27 - 4 * t)
        part = kernel[4 * t : 4 * t + count].reshape(count * FEAT, FEAT)
        if count < 4:
            part = jnp.concatenate([part, jnp.zeros(((4 - count) * FEAT, FEAT), BF16)], axis=0)
        turned = dot_nt(eye, part).astype(BF16)
        wide = dot(turned, spread).astype(BF16)
        for g in range(count):
            spread_taps[4 * t + g] = wide[:, g * LANES : (g + 1) * LANES]
    lane = iota((FEAT, LANES), 1) // FEAT
    zero = jnp.zeros((FEAT, LANES), BF16)

    def block(dx, dc, offset):
        value = zero
        if 0 <= dc <= 2:
            for dy in range(3):
                tap = spread_taps[(dc * 3 + dy) * 3 + dx]
                value = jnp.where(lane == offset - dy, tap, value)
        return value

    for dx in range(3):
        for cin in range(4):
            for cout in range(2):
                lanes = slice(cout * LANES, (cout + 1) * LANES)
                for e in range(EARLY):
                    base = (cin * EARLY + e) * FEAT
                    q = jnp.where(odd, 1, 3) + e
                    w_early[dx, base : base + FEAT, lanes] = block(dx, cin - cout, q)
                for l in range(LATE):
                    base = (cin * LATE + l) * FEAT
                    w_late[dx, base : base + FEAT, lanes] = block(
                        dx, cin - cout, late_row(jnp.int32(l), odd)
                    )


def fill_proposal(kernel, w_prop):
    wide = kernel.shape[3]
    zero = jnp.zeros((FEAT, wide), BF16)
    for dx in range(3):
        for moment in range(2):
            for y in range(4):
                base = ((dx * 2 + moment) * 4 + y) * FEAT
                for yout in range(2):
                    dy = y - yout
                    value = zero
                    if 0 <= dy <= 2:
                        value = kernel[dy, dx, moment * FEAT : (moment + 1) * FEAT, :]
                    w_prop[base : base + FEAT, yout * wide : (yout + 1) * wide] = value


def fill_heads(score, box, heads):
    lines = heads.shape[0]

    def picked(count, wanted):
        row = iota((lines, count), 0)
        return (wanted(row // HEAD, row % HEAD) == iota((lines, count), 1)).astype(BF16)

    from_score = picked(ANCHORS, lambda g, k: jnp.where((g == 0) & (k < ANCHORS), k, -1))
    from_box = picked(4 * ANCHORS, lambda g, k: jnp.where((g > 0) & (k < ANCHORS), 4 * k + g - 1, -1))
    heads[...] = (dot(from_score, score[...]) + dot(from_box, box[...])).astype(BF16)


def flatten(rx, lines, planes, freq, cols):
    blocks, rows, _ = rx.shape
    values = rx[...].astype(F32)
    marks = values[:, :, LANES - 1 :]
    total = jnp.sum(values * marks, axis=0)
    count = jnp.sum(jnp.broadcast_to(marks, values.shape), axis=0)
    total = functools.reduce(jnp.add, [total[2 * c : 2 * c + 2] for c in range(rows // 2)])
    count = functools.reduce(jnp.add, [count[2 * c : 2 * c + 2] for c in range(rows // 2)])
    baseline = total / jnp.maximum(count, 1.0)
    baseline = jnp.concatenate([baseline] * (rows // 2), axis=0)
    col = WIDTH * freq - 3 + iota((rows, LANES), 1)
    inside = (col >= 0) & (col < cols)
    for block in range(blocks):
        lines[block * rows : (block + 1) * rows, :] = jnp.where(inside, values[block] - baseline, 0.0)
    for y in range(2):
        planes[3 + y] = lines[pl.ds(y, CHANS, stride=2), :].astype(BF16)


def shift_columns(lines, shifted):
    for start in range(0, lines.shape[0], 16):
        part = lines[start : start + 16, :]
        for dx in range(3):
            moved = part if dx == 0 else pltpu.roll(part, LANES - dx, 1)
            shifted[dx, start : start + 16, :] = moved.astype(BF16)


def clear_edges(lines, count):
    for start, stop in ((0, 2 * count), ((CHANS + 2) * count, lines.shape[0])):
        lines[start:stop, :] = jnp.zeros((stop - start, LANES), F32)


def columns_to_rows(shifted, count, span, freq, cols):
    j = iota((ROWS_ONE, 2 * LANES), 0)
    lane = iota((ROWS_ONE, 2 * LANES), 1)
    x = j % 8 * STRIDE + j // SLAB
    col = WIDTH * freq - 2 + x
    inside = (x < WIDTH + 4) & (col >= 0) & (col < cols)
    turn = ((lane == x + j // 8 % 2 * LANES) & inside).astype(BF16)
    zero = jnp.zeros((256 - 3 * span, LANES), BF16)
    blocks = []
    for w in range(WINDOWS + 1):
        halves = []
        for start in (WINDOW * count * w, WINDOW * count * w + count * CHANS // 2):
            parts = [shifted[dx, start : start + span, :] for dx in range(3)]
            halves.append(jnp.concatenate(parts + [zero], axis=0))
        blocks.append(dot_nt(turn, jnp.concatenate(halves, axis=1)).astype(BF16))
    return jnp.concatenate(blocks, axis=0)


def convolve_first(lhs, weights, layer):
    lanes = weights.shape[1]
    chan = lanes // WINDOW
    tail = layer.shape[1] - WINDOWS * lanes
    row = iota((ROWS_ONE, 256), 0) // 8 % 2
    lane = iota((ROWS_ONE, 256), 1)
    for n in range(lanes // 256):
        count = WINDOWS + 1 if 256 * n < tail else WINDOWS
        value = jnp.maximum(dot(lhs[: count * ROWS_ONE], weights[:, 256 * n : 256 * n + 256]), 0.0)
        for w in range(count):
            part = value[ROWS_ONE * w : ROWS_ONE * (w + 1)]
            base = w * lanes + 256 * n
            if base == 0:
                part = jnp.where((row == 0) & (lane < chan), 0.0, part)
            if w == WINDOWS:
                part = jnp.where((row == 1) & (lane >= chan - 256 * n), 0.0, part)
            part = part[:, : min(256, layer.shape[1] - base)].astype(BF16)
            layer[:, base : base + part.shape[1]] = part


def convolve_second(layer, weights, pairs):
    span = weights.shape[1]
    step = span // 2
    total = None
    for dx in range(3):
        parts = [layer[SLAB * dx : SLAB * dx + ROWS_TWO, step * p : step * p + span] for p in pairs]
        part = dot(jnp.concatenate(parts, axis=0), weights[dx])
        total = part if total is None else total + part
    return total


def groups():
    return [range(start, start + GROUP) for start in range(0, PAIRS, GROUP)]


def sum_moments(layer, weights, partial):
    zeroth = jnp.zeros((ROWS_TWO, LANES), F32)
    first = jnp.zeros((ROWS_TWO, LANES), F32)
    for pairs in groups():
        rows = pl.ds(pairs[0] * ROWS_TWO, GROUP * ROWS_TWO)
        total = jnp.maximum(convolve_second(layer, weights, pairs) + partial[rows, :], 0.0)
        for i, p in enumerate(pairs):
            for half in range(2):
                c = 2 * p + half
                value = total[
                    ROWS_TWO * i : ROWS_TWO * (i + 1), LANES * half : LANES * (half + 1)
                ]
                zeroth = zeroth + value
                first = first + ((c + 0.5) / CHANS - 0.5) * value
    low, high = [zeroth.reshape(STRIDE, 2, 8, LANES)[:, h].reshape(-1, LANES) for h in range(2)]
    parts = [first.reshape(STRIDE, 2, 8, LANES)[:, h].reshape(-1, LANES) for h in range(2)]
    first = parts[0] + parts[1] + 0.5 * high
    return (low + high) * (1.0 / CHANS), first * (12.0 / CHANS)


def propose(zeroth, first, w_prop, heads, freq, sky, height, cols, result):
    maps = jnp.concatenate([zeroth, first], axis=1)
    y = 2 * sky - 1 + iota(maps.shape, 1) // FEAT % 4
    maps = jnp.where((y >= 0) & (y < height), maps, 0.0).astype(BF16)
    row = iota((3 * WIDTH, 8 * STRIDE), 0)
    x = row % WIDTH + row // WIDTH
    col = WIDTH * freq - 1 + x
    j = iota((3 * WIDTH, 8 * STRIDE), 1)
    turn = ((j % 8 * STRIDE + j // 8 == x) & (col >= 0) & (col < cols)).astype(BF16)
    framed = dot(turn, maps).astype(BF16)
    framed = jnp.concatenate([framed[WIDTH * dx : WIDTH * (dx + 1)] for dx in range(3)], axis=1)
    hidden = jnp.maximum(dot(framed, w_prop[...]), 0.0).astype(BF16)
    k = iota((HEAD, WIDTH), 0)
    anchor_width = jnp.ones((HEAD, WIDTH), F32)
    anchor_height = anchor_width
    for anchor in range(ANCHORS):
        scale = 4.0 * 2.0 ** (anchor // 3)
        root = (2.0 ** (anchor % 3 - 1)) ** 0.5
        anchor_width = jnp.where(k == anchor, scale * root, anchor_width)
        anchor_height = jnp.where(k == anchor, scale / root, anchor_height)
    centre_col = (WIDTH * freq + iota((HEAD, WIDTH), 1)).astype(F32) + 0.5
    wide = hidden.shape[1] // 2
    for row in range(2):
        out = dot_nt(heads[...], hidden[:, wide * row : wide * (row + 1)])
        score, dx, dy, dw, dh = [out[HEAD * g : HEAD * (g + 1)] for g in range(5)]
        centre_row = (2 * sky + row).astype(F32) + 0.5
        centre_x = centre_col + dx * anchor_width
        centre_y = centre_row + dy * anchor_height
        half_width = 0.5 * (anchor_width * jnp.exp(dw))
        half_height = 0.5 * (anchor_height * jnp.exp(dh))
        result[:, 0, row, :] = score[:ANCHORS]
        corners = (
            centre_x - half_width,
            centre_y - half_height,
            centre_x + half_width,
            centre_y + half_height,
        )
        for side, corner in enumerate(corners):
            result[:, 1 + side, row, :] = (corner * (1.0 / 64.0))[:ANCHORS]


def body(
    shape,
    cube_hbm, free_hbm, taps_hbm, kernel_hbm, proposal_hbm, score_hbm, box_hbm,
    result,
    cube, free, taps, kernel, proposal, score, box,
    tx, rx, planes, lines, lines_early, lines_late, shifted_early, shifted_late, w_one_early, w_one_late,
    spread_taps, w_two_early, w_two_late, w_prop, heads, layer_early, layer_late, partial,
    load_sem, send_sem, recv_sem, halo_send, halo_recv, late, clear,
    passing, hub_send, hub_recv,
):
    freq_count, sky_count, height, cols = shape
    freq = lax.axis_index("freq")
    sky = lax.axis_index("sky")
    odd = lax.rem(sky, 2) == 1
    barrier = pltpu.get_barrier_semaphore()
    cut = max(2, freq_count * 7 // 16 // 2 * 2)
    is_first = freq < cut
    middle = freq_count * 11 // 16
    end = freq_count * 3 // 4
    hubs = (freq_count - end) // 2
    is_source = (freq >= cut) & (freq < middle)
    is_hub = (freq >= 2) & (freq < 2 + 2 * hubs)

    def hub_of(target):
        return 2 * (hubs - (target - end) // 2) + target % 2

    def freq_peer(i):
        return i + (i >= freq).astype(jnp.int32)

    def in_sky(i):
        return (sky + i >= 0) & (sky + i < sky_count)

    def greet(i, carry):
        peer = lax.rem(freq + freq_count // 2 + (i + 1) // 2 * (1 - 2 * (i % 2)) + freq_count, freq_count)
        pl.semaphore_signal(barrier, inc=1, device_id={"freq": peer}, device_id_type=MESH)
        return carry

    @pl.when(is_first)
    def _():
        for i in range(freq_count - 1):
            greet(i, 0)

    neighbours = 0
    for i in (-2, -1, 1, 2):
        neighbours += in_sky(i).astype(jnp.int32)

        @pl.when(in_sky(i))
        def _():
            pl.semaphore_signal(barrier, inc=1, device_id={"sky": sky + i}, device_id_type=MESH)

    moves = (
        (cube_hbm, cube), (free_hbm, free), (taps_hbm, taps), (kernel_hbm, kernel),
        (proposal_hbm, proposal), (score_hbm, score), (box_hbm, box),
    )
    loads = [
        pltpu.make_async_copy(source, target, load_sem.at[i])
        for i, (source, target) in enumerate(moves)
    ]
    for load in loads:
        load.start()
    pl.semaphore_wait(barrier, cut - is_first.astype(jnp.int32) + neighbours)

    def announce(i, carry):
        pl.semaphore_signal(late, inc=1, device_id={"freq": i}, device_id_type=MESH)
        return carry

    @pl.when(jnp.logical_not(is_first))
    def _():
        for i in range(cut):
            announce(i, 0)

    loads[0].wait()
    loads[1].wait()
    fill_tx(cube, free, tx)

    def exchange(peer):
        return pltpu.make_async_remote_copy(
            src_ref=tx.at[peer],
            dst_ref=rx.at[freq],
            send_sem=send_sem.at[peer],
            recv_sem=recv_sem.at[freq],
            device_id={"freq": peer},
            device_id_type=MESH,
        )

    def arrival(peer):
        return pltpu.make_async_remote_copy(
            src_ref=tx.at[peer],
            dst_ref=rx.at[peer],
            send_sem=send_sem.at[peer],
            recv_sem=recv_sem.at[peer],
            device_id={"freq": peer},
            device_id_type=MESH,
        )

    def send(peer):
        wanted = peer != freq
        if peer >= end:
            wanted &= jnp.logical_not(is_source)

        @pl.when(wanted)
        def _():
            exchange(peer).start()

    def to_hub(peer):
        return pltpu.make_async_remote_copy(
            src_ref=tx.at[peer],
            dst_ref=passing.at[freq - cut],
            send_sem=send_sem.at[peer],
            recv_sem=hub_recv.at[freq - cut],
            device_id={"freq": hub_of(peer)},
            device_id_type=MESH,
        )

    def from_hub(slot):
        return pltpu.make_async_remote_copy(
            src_ref=passing.at[slot],
            dst_ref=rx.at[cut + slot],
            send_sem=hub_send.at[slot],
            recv_sem=recv_sem.at[cut + slot],
            device_id={"freq": end + 2 * (hubs - freq // 2) + lax.rem(freq, 2)},
            device_id_type=MESH,
        )

    def at_hub(slot):
        return pltpu.make_async_remote_copy(
            src_ref=passing.at[slot],
            dst_ref=passing.at[slot],
            send_sem=hub_send.at[slot],
            recv_sem=hub_recv.at[slot],
            device_id={"freq": cut + slot},
            device_id_type=MESH,
        )

    def release(i, carry):
        peer = cut + 2 * i + freq
        pl.semaphore_signal(clear, inc=1, device_id={"freq": peer}, device_id_type=MESH)
        return carry

    def finish(i):
        @pl.when(i != freq)
        def _():
            arrival(i).wait_recv()

    def settle(i):
        @pl.when(i != freq)
        def _():
            arrival(i).wait_send()

    for i in range(cut):
        send(i)

    @pl.when(is_source)
    def _():
        for peer in reversed(range(end, freq_count)):
            to_hub(peer).start()

    rx[freq] = tx[freq]
    for load in loads[2:]:
        load.wait()
    fill_first(taps, sky, height, odd, w_one_early, w_one_late)
    fill_second(kernel, odd, spread_taps, w_two_early, w_two_late)
    fill_proposal(proposal, w_prop)
    fill_heads(score, box, heads)
    clear_edges(lines_early, 4)
    clear_edges(lines_late, 8)

    @pl.when(is_first)
    def _():
        pl.semaphore_wait(late, freq_count - cut)

    @pl.when(freq < 2)
    def _():
        for i in range((freq_count - cut) // 2):
            release(i, 0)

    @pl.when(jnp.logical_not(is_first))
    def _():
        pl.semaphore_wait(clear, 1)

    from_end = (freq >= freq_count * 3 // 16) & (freq < freq_count * 11 // 16)

    @pl.when(from_end)
    def _():
        for i in reversed(range(cut, freq_count)):
            send(i)

    @pl.when(jnp.logical_not(from_end))
    def _():
        for i in range(cut, freq_count):
            send(i)

    @pl.when(is_hub)
    def _():
        for slot in range(middle - cut):
            at_hub(slot).wait_recv()
            from_hub(slot).start()

    for i in range(freq_count):
        finish(i)

    flatten(rx, lines, planes, freq, cols)
    halos = []
    for n, (i, source, target) in enumerate(((2, 4, 0), (-2, 3, 7), (1, 3, 1), (-1, 3, 5))):
        size = 2 if abs(i) == 1 else 1
        halo = pltpu.make_async_remote_copy(
            src_ref=planes.at[pl.ds(source, size)],
            dst_ref=planes.at[pl.ds(target, size)],
            send_sem=halo_send.at[n],
            recv_sem=halo_recv.at[n],
            device_id={"sky": sky + i},
            device_id_type=MESH,
        )
        halos.append((i, halo))
    for i, halo in halos:
        pl.when(in_sky(i))(halo.start)
    mate = dict(halos)
    pl.when(odd)(mate[1].wait_recv)
    pl.when(jnp.logical_not(odd))(mate[-1].wait_recv)
    for i in range(4):
        lines_early[pl.ds(8 + i, CHANS, stride=4), :] = planes[jnp.where(odd, 1, 3) + i].astype(F32)
    shift_columns(lines_early, shifted_early)
    convolve_first(
        columns_to_rows(shifted_early, 4, 48, freq, cols), w_one_early, layer_early
    )
    for pairs in groups():
        rows = pl.ds(pairs[0] * ROWS_TWO, GROUP * ROWS_TWO)
        partial[rows, :] = convolve_second(layer_early, w_two_early, pairs)

    for i, halo in halos:
        pl.when(in_sky(i))(halo.wait_send)
    for i in range(freq_count):
        settle(i)

    @pl.when(is_hub)
    def _():
        for slot in range(middle - cut):
            from_hub(slot).wait_send()

    for i, halo in halos:
        if abs(i) == 2:
            pl.when(in_sky(-i))(halo.wait_recv)
    pl.when(jnp.logical_not(odd) & in_sky(-1))(mate[1].wait_recv)
    pl.when(odd & in_sky(1))(mate[-1].wait_recv)
    for r in range(8):
        y = 2 * sky - 3 + r
        value = planes[r].astype(F32)
        if r not in (3, 4):
            value = jnp.where((y >= 0) & (y < height), value, 0.0)
        lines_late[pl.ds(16 + r, CHANS, stride=8), :] = value
    shift_columns(lines_late, shifted_late)
    convolve_first(columns_to_rows(shifted_late, 8, 80, freq, cols), w_one_late, layer_late)
    zeroth, first = sum_moments(layer_late, w_two_late, partial)
    propose(zeroth, first, w_prop, heads, freq, sky, height, cols, result)


def on_device(sky_cube, free_mask, conv_first, conv_second, proposal_conv, score_head, box_head):
    freq_count = lax.axis_size("freq")
    sky_count = lax.axis_size("sky")
    chans, rows, cols = sky_cube.shape
    wide = proposal_conv.shape[3]
    taps = conv_first.transpose(1, 2, 3, 4, 0).reshape(9, 3, FEAT)
    kernel = conv_second.transpose(2, 3, 4, 0, 1).reshape(27, FEAT, FEAT)
    free = free_mask.reshape(1, chans)
    operands = (sky_cube, free, taps, kernel, proposal_conv, score_head, box_head)
    scratch = [pltpu.VMEM(operand.shape, operand.dtype) for operand in operands] + [
        pltpu.VMEM((freq_count, chans * rows, LANES), BF16),
        pltpu.VMEM((freq_count, chans * rows, LANES), BF16),
        pltpu.VMEM((8, CHANS, LANES), BF16),
        pltpu.VMEM((2 * CHANS, LANES), F32),
        pltpu.VMEM((4 * CHANS + 48, LANES), F32),
        pltpu.VMEM((8 * CHANS + 80, LANES), F32),
        pltpu.VMEM((3, 4 * CHANS + 48, LANES), BF16),
        pltpu.VMEM((3, 8 * CHANS + 80, LANES), BF16),
        pltpu.VMEM((256, WINDOW * EARLY * FEAT), BF16),
        pltpu.VMEM((256, WINDOW * LATE * FEAT), BF16),
        pltpu.VMEM((27, FEAT, LANES), BF16),
        pltpu.VMEM((3, 4 * EARLY * FEAT, 256), BF16),
        pltpu.VMEM((3, 4 * LATE * FEAT, 256), BF16),
        pltpu.VMEM((3 * 256, 2 * wide), BF16),
        pltpu.VMEM((5 * HEAD, wide), BF16),
        pltpu.VMEM((ROWS_ONE, 2 * (PAIRS + 1) * EARLY * FEAT), BF16),
        pltpu.VMEM((ROWS_ONE, 2 * (PAIRS + 1) * LATE * FEAT), BF16),
        pltpu.VMEM((PAIRS * ROWS_TWO, 256), F32),
        pltpu.SemaphoreType.DMA((len(operands),)),
        pltpu.SemaphoreType.DMA((freq_count,)),
        pltpu.SemaphoreType.DMA((freq_count,)),
        pltpu.SemaphoreType.DMA((4,)),
        pltpu.SemaphoreType.DMA((4,)),
        pltpu.SemaphoreType.REGULAR,
        pltpu.SemaphoreType.REGULAR,
        pltpu.VMEM((freq_count // 4, chans * rows, LANES), BF16),
        pltpu.SemaphoreType.DMA((freq_count // 4,)),
        pltpu.SemaphoreType.DMA((freq_count // 4,)),
    ]
    shape = (freq_count, sky_count, rows * sky_count, cols)
    result = pl.pallas_call(
        functools.partial(body, shape),
        out_shape=pltpu.VMEM((ANCHORS, 5, rows, WIDTH), F32),
        in_specs=[pl.BlockSpec(memory_space=pltpu.HBM)] * len(operands),
        out_specs=pl.BlockSpec(memory_space=pltpu.VMEM),
        scratch_shapes=scratch,
        compiler_params=pltpu.CompilerParams(
            collective_id=0, has_side_effects=True, vmem_limit_bytes=60 * 1024 * 1024
        ),
    )(*operands)
    return result[:, 0], result[:, 1:]


def solution(mesh):
    in_specs = (P("freq", "sky", None), P("freq"), P(), P(), P(), P(), P())
    out_specs = (P(None, "sky", "freq"), P(None, None, "sky", "freq"))
    return jax.shard_map(
        on_device, mesh=mesh, in_specs=in_specs, out_specs=out_specs, check_vma=False
    )
```

```python
import functools

import jax
import jax.numpy as jnp
from jax import lax
from jax.experimental import pallas as pl
from jax.experimental.pallas import tpu as pltpu
from jax.sharding import PartitionSpec as P

F32 = jnp.float32
BF16 = jnp.bfloat16
MESH = pl.DeviceIdType.MESH
CHANS = 64
FEAT = 32
ANCHORS = 9
WIDTH = 64
LANES = 128
SLAB = 16
HEAD = 16
STRIDE = 9
ROWS_ONE = (STRIDE + 2) * SLAB
ROWS_TWO = STRIDE * SLAB
PAIRS = CHANS // 4
EARLY = 2
LATE = 4
WINDOW = 8
WINDOWS = CHANS // 2 // WINDOW
GROUP = 4
NT = (((1,), (1,)), ((), ()))


def iota(shape, dim):
    return lax.broadcasted_iota(jnp.int32, shape, dim)


def dot(a, b):
    return jnp.dot(a, b, preferred_element_type=F32)


def dot_nt(a, b):
    return lax.dot_general(a, b, NT, preferred_element_type=F32)


def fill_tx(cube, free, tx, count, send):
    chans, rows, cols = cube.shape
    lines = chans * rows
    values = cube[...].astype(F32).reshape(lines, cols)
    line = iota((lines, LANES), 0)
    lane = iota((lines, LANES), 1)
    marks = jnp.zeros((lines, LANES), F32)
    flags = free[...].astype(F32)
    for c in range(chans):
        marks = jnp.where(line // rows == c, flags[0:1, c : c + 1], marks)
    even = jnp.concatenate([values[:, cols - 3 :], values[:, : cols - 3]], axis=1)
    odd = jnp.concatenate([values[:, WIDTH - 3 :], values[:, : WIDTH - 3]], axis=1)
    for block in range(cols // WIDTH):
        source = odd if block % 2 else even
        start = block // 2 * LANES
        piece = source[:, start : start + LANES]
        tx[block] = jnp.where(lane == LANES - 1, marks, piece).astype(BF16)
        if block == count - 1:
            for peer in range(count):
                send(peer)


def late_row(index, odd):
    return index + 2 * (index >= jnp.where(odd, 1, 3)).astype(jnp.int32)


def fill_first(taps, sky, height, odd, w_early, w_late):
    spread = (iota((FEAT, LANES), 1) % FEAT == iota((FEAT, LANES), 0)).astype(BF16)
    rows = [dot(taps[i], spread) for i in range(9)]
    sub = iota((8, LANES), 0)
    lane = iota((8, LANES), 1)
    zero = jnp.zeros((8, LANES), F32)

    def store(target, base, tile, parts):
        for half in range(len(parts) // 2):
            both = jnp.concatenate([parts[2 * half], parts[2 * half + 1]], axis=0)
            start = base + 16 * half
            target[start : start + 16, tile * LANES : (tile + 1) * LANES] = both.astype(BF16)

    step_rows = [sub % 4 - lane // FEAT % 2 == dy for dy in range(3)]
    apart = sub // 4 - lane // (2 * FEAT)
    masks = {}
    for shift in range(-1, 4):
        for dc in range(3):
            if -1 <= dc - shift <= 1:
                for dy in range(3):
                    masks[shift, dc, dy] = step_rows[dy] & (apart == dc - shift)
    for tile in range(WINDOW * EARLY * FEAT // LANES):
        for dx in range(3):
            parts = []
            for pair in range(6):
                value = zero
                for dc in range(3):
                    for dy in range(3):
                        mask = masks.get((2 * pair - 2 * tile, dc, dy))
                        if mask is not None:
                            value = jnp.where(mask, rows[dc * 3 + dy][dx : dx + 1, :], value)
                parts.append(value)
            store(w_early, 48 * dx, tile, parts)
        w_early[144:256, tile * LANES : (tile + 1) * LANES] = jnp.zeros((112, LANES), BF16)

    q = late_row(lane // FEAT, odd)
    y = 2 * sky - 2 + q
    inside = (y >= 0) & (y < height)
    row_masks = [(sub - q == dy) & inside for dy in range(3)]
    for tile in range(WINDOW):
        for dx in range(3):
            parts = []
            for a in range(10):
                value = zero
                dc = a - tile
                if 0 <= dc <= 2:
                    for dy in range(3):
                        value = jnp.where(row_masks[dy], rows[dc * 3 + dy][dx : dx + 1, :], value)
                parts.append(value)
            store(w_late, 80 * dx, tile, parts)
        w_late[240:256, tile * LANES : (tile + 1) * LANES] = jnp.zeros((16, LANES), BF16)


def fill_second(kernel, odd, spread_taps, w_early, w_late):
    eye = (iota((FEAT, FEAT), 0) == iota((FEAT, FEAT), 1)).astype(BF16)
    source = iota((LANES, 4 * LANES), 0)
    target = iota((LANES, 4 * LANES), 1)
    spread = (source == target // LANES * FEAT + target % FEAT).astype(BF16)
    for t in range(7):
        count = min(4, 27 - 4 * t)
        part = kernel[4 * t : 4 * t + count].reshape(count * FEAT, FEAT)
        if count < 4:
            part = jnp.concatenate([part, jnp.zeros(((4 - count) * FEAT, FEAT), BF16)], axis=0)
        turned = dot_nt(eye, part).astype(BF16)
        wide = dot(turned, spread).astype(BF16)
        for g in range(count):
            spread_taps[4 * t + g] = wide[:, g * LANES : (g + 1) * LANES]
    lane = iota((FEAT, LANES), 1) // FEAT
    zero = jnp.zeros((FEAT, LANES), BF16)

    def block(dx, dc, offset):
        value = zero
        if 0 <= dc <= 2:
            for dy in range(3):
                tap = spread_taps[(dc * 3 + dy) * 3 + dx]
                value = jnp.where(lane == offset - dy, tap, value)
        return value

    for dx in range(3):
        for cin in range(4):
            for cout in range(2):
                lanes = slice(cout * LANES, (cout + 1) * LANES)
                for e in range(EARLY):
                    base = (cin * EARLY + e) * FEAT
                    q = jnp.where(odd, 1, 3) + e
                    w_early[dx, base : base + FEAT, lanes] = block(dx, cin - cout, q)
                for l in range(LATE):
                    base = (cin * LATE + l) * FEAT
                    w_late[dx, base : base + FEAT, lanes] = block(
                        dx, cin - cout, late_row(jnp.int32(l), odd)
                    )


def fill_proposal(kernel, w_prop):
    wide = kernel.shape[3]
    zero = jnp.zeros((FEAT, wide), BF16)
    for dx in range(3):
        for moment in range(2):
            for y in range(4):
                base = ((dx * 2 + moment) * 4 + y) * FEAT
                for yout in range(2):
                    dy = y - yout
                    value = zero
                    if 0 <= dy <= 2:
                        value = kernel[dy, dx, moment * FEAT : (moment + 1) * FEAT, :]
                    w_prop[base : base + FEAT, yout * wide : (yout + 1) * wide] = value


def fill_heads(score, box, heads):
    lines = heads.shape[0]

    def picked(count, wanted):
        row = iota((lines, count), 0)
        return (wanted(row // HEAD, row % HEAD) == iota((lines, count), 1)).astype(BF16)

    from_score = picked(ANCHORS, lambda g, k: jnp.where((g == 0) & (k < ANCHORS), k, -1))
    from_box = picked(4 * ANCHORS, lambda g, k: jnp.where((g > 0) & (k < ANCHORS), 4 * k + g - 1, -1))
    heads[...] = (dot(from_score, score[...]) + dot(from_box, box[...])).astype(BF16)


def flatten(rx, lines, planes, freq, cols):
    blocks, rows, _ = rx.shape
    values = rx[...].astype(F32)
    marks = values[:, :, LANES - 1 :]
    total = jnp.sum(values * marks, axis=0)
    count = jnp.sum(jnp.broadcast_to(marks, values.shape), axis=0)
    total = functools.reduce(jnp.add, [total[2 * c : 2 * c + 2] for c in range(rows // 2)])
    count = functools.reduce(jnp.add, [count[2 * c : 2 * c + 2] for c in range(rows // 2)])
    baseline = total / jnp.maximum(count, 1.0)
    baseline = jnp.concatenate([baseline] * (rows // 2), axis=0)
    col = WIDTH * freq - 3 + iota((rows, LANES), 1)
    inside = (col >= 0) & (col < cols)
    for block in range(blocks):
        lines[block * rows : (block + 1) * rows, :] = jnp.where(inside, values[block] - baseline, 0.0)
    for y in range(2):
        planes[3 + y] = lines[pl.ds(y, CHANS, stride=2), :].astype(BF16)


def shift_columns(lines, shifted):
    for start in range(0, lines.shape[0], 16):
        part = lines[start : start + 16, :]
        for dx in range(3):
            moved = part if dx == 0 else pltpu.roll(part, LANES - dx, 1)
            shifted[dx, start : start + 16, :] = moved.astype(BF16)


def clear_edges(lines, count):
    for start, stop in ((0, 2 * count), ((CHANS + 2) * count, lines.shape[0])):
        lines[start:stop, :] = jnp.zeros((stop - start, LANES), F32)


def columns_to_rows(shifted, count, span, freq, cols):
    j = iota((ROWS_ONE, 2 * LANES), 0)
    lane = iota((ROWS_ONE, 2 * LANES), 1)
    x = j % 8 * STRIDE + j // SLAB
    col = WIDTH * freq - 2 + x
    inside = (x < WIDTH + 4) & (col >= 0) & (col < cols)
    turn = ((lane == x + j // 8 % 2 * LANES) & inside).astype(BF16)
    zero = jnp.zeros((256 - 3 * span, LANES), BF16)
    blocks = []
    for w in range(WINDOWS + 1):
        halves = []
        for start in (WINDOW * count * w, WINDOW * count * w + count * CHANS // 2):
            parts = [shifted[dx, start : start + span, :] for dx in range(3)]
            halves.append(jnp.concatenate(parts + [zero], axis=0))
        blocks.append(dot_nt(turn, jnp.concatenate(halves, axis=1)).astype(BF16))
    return jnp.concatenate(blocks, axis=0)


def convolve_first(lhs, weights, layer):
    lanes = weights.shape[1]
    chan = lanes // WINDOW
    tail = layer.shape[1] - WINDOWS * lanes
    row = iota((ROWS_ONE, 256), 0) // 8 % 2
    lane = iota((ROWS_ONE, 256), 1)
    for n in range(lanes // 256):
        count = WINDOWS + 1 if 256 * n < tail else WINDOWS
        value = jnp.maximum(dot(lhs[: count * ROWS_ONE], weights[:, 256 * n : 256 * n + 256]), 0.0)
        for w in range(count):
            part = value[ROWS_ONE * w : ROWS_ONE * (w + 1)]
            base = w * lanes + 256 * n
            if base == 0:
                part = jnp.where((row == 0) & (lane < chan), 0.0, part)
            if w == WINDOWS:
                part = jnp.where((row == 1) & (lane >= chan - 256 * n), 0.0, part)
            part = part[:, : min(256, layer.shape[1] - base)].astype(BF16)
            layer[:, base : base + part.shape[1]] = part


def convolve_second(layer, weights, pairs):
    span = weights.shape[1]
    step = span // 2
    total = None
    for dx in range(3):
        parts = [layer[SLAB * dx : SLAB * dx + ROWS_TWO, step * p : step * p + span] for p in pairs]
        part = dot(jnp.concatenate(parts, axis=0), weights[dx])
        total = part if total is None else total + part
    return total


def groups():
    return [range(start, start + GROUP) for start in range(0, PAIRS, GROUP)]


def sum_moments(layer, weights, partial):
    zeroth = jnp.zeros((ROWS_TWO, LANES), F32)
    first = jnp.zeros((ROWS_TWO, LANES), F32)
    for pairs in groups():
        rows = pl.ds(pairs[0] * ROWS_TWO, GROUP * ROWS_TWO)
        total = jnp.maximum(convolve_second(layer, weights, pairs) + partial[rows, :], 0.0)
        for i, p in enumerate(pairs):
            for half in range(2):
                c = 2 * p + half
                value = total[
                    ROWS_TWO * i : ROWS_TWO * (i + 1), LANES * half : LANES * (half + 1)
                ]
                zeroth = zeroth + value
                first = first + ((c + 0.5) / CHANS - 0.5) * value
    low, high = [zeroth.reshape(STRIDE, 2, 8, LANES)[:, h].reshape(-1, LANES) for h in range(2)]
    parts = [first.reshape(STRIDE, 2, 8, LANES)[:, h].reshape(-1, LANES) for h in range(2)]
    first = parts[0] + parts[1] + 0.5 * high
    return (low + high) * (1.0 / CHANS), first * (12.0 / CHANS)


def propose(zeroth, first, w_prop, heads, freq, sky, height, cols, result):
    maps = jnp.concatenate([zeroth, first], axis=1)
    y = 2 * sky - 1 + iota(maps.shape, 1) // FEAT % 4
    maps = jnp.where((y >= 0) & (y < height), maps, 0.0).astype(BF16)
    row = iota((3 * WIDTH, 8 * STRIDE), 0)
    x = row % WIDTH + row // WIDTH
    col = WIDTH * freq - 1 + x
    j = iota((3 * WIDTH, 8 * STRIDE), 1)
    turn = ((j % 8 * STRIDE + j // 8 == x) & (col >= 0) & (col < cols)).astype(BF16)
    framed = dot(turn, maps).astype(BF16)
    framed = jnp.concatenate([framed[WIDTH * dx : WIDTH * (dx + 1)] for dx in range(3)], axis=1)
    hidden = jnp.maximum(dot(framed, w_prop[...]), 0.0).astype(BF16)
    wide = hidden.shape[1] // 2
    stacked = jnp.concatenate([hidden[:, :wide], hidden[:, wide:]], axis=0)
    out = dot_nt(heads[...], stacked)
    score, dx, dy, dw, dh = [out[HEAD * g : HEAD * (g + 1)] for g in range(5)]
    k = iota(score.shape, 0)
    lane = iota(score.shape, 1)
    anchor_width = jnp.ones(score.shape, F32)
    anchor_height = anchor_width
    for anchor in range(ANCHORS):
        scale = 4.0 * 2.0 ** (anchor // 3)
        root = (2.0 ** (anchor % 3 - 1)) ** 0.5
        anchor_width = jnp.where(k == anchor, scale * root, anchor_width)
        anchor_height = jnp.where(k == anchor, scale / root, anchor_height)
    centre_x = (WIDTH * freq + lane % WIDTH).astype(F32) + 0.5 + dx * anchor_width
    centre_y = (2 * sky + lane // WIDTH).astype(F32) + 0.5 + dy * anchor_height
    half_width = 0.5 * (anchor_width * jnp.exp(dw))
    half_height = 0.5 * (anchor_height * jnp.exp(dh))
    corners = (
        centre_x - half_width,
        centre_y - half_height,
        centre_x + half_width,
        centre_y + half_height,
    )
    parts = (score,) + tuple(corner * (1.0 / 64.0) for corner in corners)
    for g, part in enumerate(parts):
        for row in range(2):
            result[:, g, row, :] = part[:ANCHORS, WIDTH * row : WIDTH * (row + 1)]


def body(
    shape,
    cube_hbm, free_hbm, taps_hbm, kernel_hbm, proposal_hbm, score_hbm, box_hbm,
    result,
    cube, free, taps, kernel, proposal, score, box,
    tx, rx, planes, lines, lines_early, lines_late, shifted_early, shifted_late, w_one_early, w_one_late,
    spread_taps, w_two_early, w_two_late, w_prop, heads, layer_early, layer_late, partial,
    load_sem, send_sem, recv_sem, halo_send, halo_recv, late, clear,
    passing, hub_send, hub_recv,
):
    freq_count, sky_count, height, cols = shape
    freq = lax.axis_index("freq")
    sky = lax.axis_index("sky")
    odd = lax.rem(sky, 2) == 1
    barrier = pltpu.get_barrier_semaphore()
    cut = max(2, freq_count * 7 // 16 // 2 * 2)
    is_first = freq < cut
    middle = freq_count * 11 // 16
    end = freq_count * 3 // 4
    hubs = (freq_count - end) // 2
    origin = min(cut, 2 + 2 * hubs)
    is_source = (freq >= origin) & (freq < middle)
    is_hub = (freq >= 2) & (freq < 2 + 2 * hubs)

    def hub_of(target):
        return 2 * (hubs - (target - end) // 2) + target % 2

    def freq_peer(i):
        return i + (i >= freq).astype(jnp.int32)

    def in_sky(i):
        return (sky + i >= 0) & (sky + i < sky_count)

    def greet(i, carry):
        peer = lax.rem(freq + freq_count // 2 + (i + 1) // 2 * (1 - 2 * (i % 2)) + freq_count, freq_count)
        pl.semaphore_signal(barrier, inc=1, device_id={"freq": peer}, device_id_type=MESH)
        return carry

    moves = (
        (cube_hbm, cube), (free_hbm, free), (taps_hbm, taps), (kernel_hbm, kernel),
        (proposal_hbm, proposal), (score_hbm, score), (box_hbm, box),
    )
    loads = [
        pltpu.make_async_copy(source, target, load_sem.at[i])
        for i, (source, target) in enumerate(moves)
    ]
    for load in loads[:2]:
        load.start()

    @pl.when(is_first)
    def _():
        for i in range(freq_count - 1):
            greet(i, 0)

    neighbours = 0
    for i in (-2, -1, 1, 2):
        neighbours += in_sky(i).astype(jnp.int32)

        @pl.when(in_sky(i))
        def _():
            pl.semaphore_signal(barrier, inc=1, device_id={"sky": sky + i}, device_id_type=MESH)

    for load in loads[2:]:
        load.start()
    pl.semaphore_wait(barrier, cut - is_first.astype(jnp.int32) + neighbours)

    def announce(i, carry):
        pl.semaphore_signal(late, inc=1, device_id={"freq": i}, device_id_type=MESH)
        return carry

    @pl.when(jnp.logical_not(is_first))
    def _():
        for i in range(cut):
            announce(i, 0)

    def exchange(peer):
        return pltpu.make_async_remote_copy(
            src_ref=tx.at[peer],
            dst_ref=rx.at[freq],
            send_sem=send_sem.at[peer],
            recv_sem=recv_sem.at[freq],
            device_id={"freq": peer},
            device_id_type=MESH,
        )

    def arrival(peer):
        return pltpu.make_async_remote_copy(
            src_ref=tx.at[peer],
            dst_ref=rx.at[peer],
            send_sem=send_sem.at[peer],
            recv_sem=recv_sem.at[peer],
            device_id={"freq": peer},
            device_id_type=MESH,
        )

    def send(peer):
        wanted = peer != freq
        if peer >= end:
            wanted &= jnp.logical_not(is_source)

        @pl.when(wanted)
        def _():
            exchange(peer).start()

    def to_hub(peer):
        return pltpu.make_async_remote_copy(
            src_ref=tx.at[peer],
            dst_ref=passing.at[freq - origin],
            send_sem=send_sem.at[peer],
            recv_sem=hub_recv.at[freq - origin],
            device_id={"freq": hub_of(peer)},
            device_id_type=MESH,
        )

    def from_hub(slot):
        return pltpu.make_async_remote_copy(
            src_ref=passing.at[slot],
            dst_ref=rx.at[origin + slot],
            send_sem=hub_send.at[slot],
            recv_sem=recv_sem.at[origin + slot],
            device_id={"freq": end + 2 * (hubs - freq // 2) + lax.rem(freq, 2)},
            device_id_type=MESH,
        )

    def at_hub(slot):
        return pltpu.make_async_remote_copy(
            src_ref=passing.at[slot],
            dst_ref=passing.at[slot],
            send_sem=hub_send.at[slot],
            recv_sem=hub_recv.at[slot],
            device_id={"freq": origin + slot},
            device_id_type=MESH,
        )

    def release(i, carry):
        peer = cut + 2 * i + freq
        pl.semaphore_signal(clear, inc=1, device_id={"freq": peer}, device_id_type=MESH)
        return carry

    def finish(i):
        @pl.when(i != freq)
        def _():
            arrival(i).wait_recv()

    def settle(i):
        @pl.when(i != freq)
        def _():
            arrival(i).wait_send()

    loads[0].wait()
    loads[1].wait()
    fill_tx(cube, free, tx, cut, send)

    @pl.when(is_source)
    def _():
        for peer in reversed(range(end, freq_count)):
            to_hub(peer).start()

    rx[freq] = tx[freq]
    for load in loads[2:]:
        load.wait()
    fill_first(taps, sky, height, odd, w_one_early, w_one_late)
    fill_second(kernel, odd, spread_taps, w_two_early, w_two_late)
    fill_proposal(proposal, w_prop)
    fill_heads(score, box, heads)
    clear_edges(lines_early, 4)
    clear_edges(lines_late, 8)

    @pl.when(is_first)
    def _():
        pl.semaphore_wait(late, freq_count - cut)

    @pl.when(freq < 2)
    def _():
        for i in range((freq_count - cut) // 2):
            release(i, 0)

    @pl.when(jnp.logical_not(is_first))
    def _():
        pl.semaphore_wait(clear, 1)

    from_end = (freq >= freq_count * 3 // 16) & (freq < freq_count * 11 // 16)

    @pl.when(from_end)
    def _():
        for i in reversed(range(cut, freq_count)):
            send(i)

    @pl.when(jnp.logical_not(from_end))
    def _():
        for i in range(cut, freq_count):
            send(i)

    @pl.when(is_hub)
    def _():
        for slot in range(middle - origin):
            at_hub(slot).wait_recv()
            from_hub(slot).start()

    for i in range(freq_count):
        finish(i)

    flatten(rx, lines, planes, freq, cols)
    halos = []
    for n, (i, source, target) in enumerate(((2, 4, 0), (-2, 3, 7), (1, 3, 1), (-1, 3, 5))):
        size = 2 if abs(i) == 1 else 1
        halo = pltpu.make_async_remote_copy(
            src_ref=planes.at[pl.ds(source, size)],
            dst_ref=planes.at[pl.ds(target, size)],
            send_sem=halo_send.at[n],
            recv_sem=halo_recv.at[n],
            device_id={"sky": sky + i},
            device_id_type=MESH,
        )
        halos.append((i, halo))
    for i, halo in halos:
        pl.when(in_sky(i))(halo.start)
    mate = dict(halos)
    pl.when(odd)(mate[1].wait_recv)
    pl.when(jnp.logical_not(odd))(mate[-1].wait_recv)
    for i in range(4):
        lines_early[pl.ds(8 + i, CHANS, stride=4), :] = planes[jnp.where(odd, 1, 3) + i].astype(F32)
    shift_columns(lines_early, shifted_early)
    convolve_first(
        columns_to_rows(shifted_early, 4, 48, freq, cols), w_one_early, layer_early
    )
    for pairs in groups():
        rows = pl.ds(pairs[0] * ROWS_TWO, GROUP * ROWS_TWO)
        partial[rows, :] = convolve_second(layer_early, w_two_early, pairs)

    for i, halo in halos:
        pl.when(in_sky(i))(halo.wait_send)
    for i in range(freq_count):
        settle(i)

    @pl.when(is_hub)
    def _():
        for slot in range(middle - origin):
            from_hub(slot).wait_send()

    for i, halo in halos:
        if abs(i) == 2:
            pl.when(in_sky(-i))(halo.wait_recv)
    pl.when(jnp.logical_not(odd) & in_sky(-1))(mate[1].wait_recv)
    pl.when(odd & in_sky(1))(mate[-1].wait_recv)
    for r in range(8):
        y = 2 * sky - 3 + r
        value = planes[r].astype(F32)
        if r not in (3, 4):
            value = jnp.where((y >= 0) & (y < height), value, 0.0)
        lines_late[pl.ds(16 + r, CHANS, stride=8), :] = value
    shift_columns(lines_late, shifted_late)
    convolve_first(columns_to_rows(shifted_late, 8, 80, freq, cols), w_one_late, layer_late)
    zeroth, first = sum_moments(layer_late, w_two_late, partial)
    propose(zeroth, first, w_prop, heads, freq, sky, height, cols, result)


def on_device(sky_cube, free_mask, conv_first, conv_second, proposal_conv, score_head, box_head):
    freq_count = lax.axis_size("freq")
    sky_count = lax.axis_size("sky")
    chans, rows, cols = sky_cube.shape
    wide = proposal_conv.shape[3]
    taps = conv_first.transpose(1, 2, 3, 4, 0).reshape(9, 3, FEAT)
    kernel = conv_second.transpose(2, 3, 4, 0, 1).reshape(27, FEAT, FEAT)
    free = free_mask.reshape(1, chans)
    operands = (sky_cube, free, taps, kernel, proposal_conv, score_head, box_head)
    scratch = [pltpu.VMEM(operand.shape, operand.dtype) for operand in operands] + [
        pltpu.VMEM((freq_count, chans * rows, LANES), BF16),
        pltpu.VMEM((freq_count, chans * rows, LANES), BF16),
        pltpu.VMEM((8, CHANS, LANES), BF16),
        pltpu.VMEM((2 * CHANS, LANES), F32),
        pltpu.VMEM((4 * CHANS + 48, LANES), F32),
        pltpu.VMEM((8 * CHANS + 80, LANES), F32),
        pltpu.VMEM((3, 4 * CHANS + 48, LANES), BF16),
        pltpu.VMEM((3, 8 * CHANS + 80, LANES), BF16),
        pltpu.VMEM((256, WINDOW * EARLY * FEAT), BF16),
        pltpu.VMEM((256, WINDOW * LATE * FEAT), BF16),
        pltpu.VMEM((27, FEAT, LANES), BF16),
        pltpu.VMEM((3, 4 * EARLY * FEAT, 256), BF16),
        pltpu.VMEM((3, 4 * LATE * FEAT, 256), BF16),
        pltpu.VMEM((3 * 256, 2 * wide), BF16),
        pltpu.VMEM((5 * HEAD, wide), BF16),
        pltpu.VMEM((ROWS_ONE, 2 * (PAIRS + 1) * EARLY * FEAT), BF16),
        pltpu.VMEM((ROWS_ONE, 2 * (PAIRS + 1) * LATE * FEAT), BF16),
        pltpu.VMEM((PAIRS * ROWS_TWO, 256), F32),
        pltpu.SemaphoreType.DMA((len(operands),)),
        pltpu.SemaphoreType.DMA((freq_count,)),
        pltpu.SemaphoreType.DMA((freq_count,)),
        pltpu.SemaphoreType.DMA((4,)),
        pltpu.SemaphoreType.DMA((4,)),
        pltpu.SemaphoreType.REGULAR,
        pltpu.SemaphoreType.REGULAR,
        pltpu.VMEM((freq_count // 2, chans * rows, LANES), BF16),
        pltpu.SemaphoreType.DMA((freq_count // 2,)),
        pltpu.SemaphoreType.DMA((freq_count // 2,)),
    ]
    shape = (freq_count, sky_count, rows * sky_count, cols)
    result = pl.pallas_call(
        functools.partial(body, shape),
        out_shape=pltpu.VMEM((ANCHORS, 5, rows, WIDTH), F32),
        in_specs=[pl.BlockSpec(memory_space=pltpu.HBM)] * len(operands),
        out_specs=pl.BlockSpec(memory_space=pltpu.VMEM),
        scratch_shapes=scratch,
        compiler_params=pltpu.CompilerParams(
            collective_id=0, has_side_effects=True, vmem_limit_bytes=60 * 1024 * 1024
        ),
    )(*operands)
    return result[:, 0], result[:, 1:]


def solution(mesh):
    in_specs = (P("freq", "sky", None), P("freq"), P(), P(), P(), P(), P())
    out_specs = (P(None, "sky", "freq"), P(None, None, "sky", "freq"))
    return jax.shard_map(
        on_device, mesh=mesh, in_specs=in_specs, out_specs=out_specs, check_vma=False
    )
```

```python
import functools

import jax
import jax.numpy as jnp
from jax import lax
from jax.experimental import pallas as pl
from jax.experimental.pallas import tpu as pltpu
from jax.sharding import PartitionSpec as P

F32 = jnp.float32
BF16 = jnp.bfloat16
MESH = pl.DeviceIdType.MESH
CHANS = 64
FEAT = 32
ANCHORS = 9
WIDTH = 64
LANES = 128
SLAB = 16
HEAD = 16
STRIDE = 9
ROWS_ONE = (STRIDE + 2) * SLAB
ROWS_TWO = STRIDE * SLAB
PAIRS = CHANS // 4
EARLY = 2
LATE = 4
WINDOW = 8
WINDOWS = CHANS // 2 // WINDOW
GROUP = 2
NT = (((1,), (1,)), ((), ()))


def iota(shape, dim):
    return lax.broadcasted_iota(jnp.int32, shape, dim)


def dot(a, b):
    return jnp.dot(a, b, preferred_element_type=F32)


def dot_nt(a, b):
    return lax.dot_general(a, b, NT, preferred_element_type=F32)


def fill_tx(cube, free, tx, count, send):
    chans, rows, cols = cube.shape
    lines = chans * rows
    values = cube[...].astype(F32).reshape(lines, cols)
    line = iota((lines, LANES), 0)
    lane = iota((lines, LANES), 1)
    marks = jnp.zeros((lines, LANES), F32)
    flags = free[...].astype(F32)
    for c in range(chans):
        marks = jnp.where(line // rows == c, flags[0:1, c : c + 1], marks)
    even = jnp.concatenate([values[:, cols - 3 :], values[:, : cols - 3]], axis=1)
    odd = jnp.concatenate([values[:, WIDTH - 3 :], values[:, : WIDTH - 3]], axis=1)
    for block in range(cols // WIDTH):
        source = odd if block % 2 else even
        start = block // 2 * LANES
        piece = source[:, start : start + LANES]
        tx[block] = jnp.where(lane == LANES - 1, marks, piece).astype(BF16)
        if block == count - 1:
            for peer in range(count):
                send(peer)


def late_row(index, odd):
    return index + 2 * (index >= jnp.where(odd, 1, 3)).astype(jnp.int32)


def fill_first(taps, sky, height, odd, w_early, w_late):
    spread = (iota((FEAT, LANES), 1) % FEAT == iota((FEAT, LANES), 0)).astype(BF16)
    rows = [dot(taps[i], spread) for i in range(9)]
    sub = iota((8, LANES), 0)
    lane = iota((8, LANES), 1)
    zero = jnp.zeros((8, LANES), F32)

    def store(target, base, tile, parts):
        for half in range(len(parts) // 2):
            both = jnp.concatenate([parts[2 * half], parts[2 * half + 1]], axis=0)
            start = base + 16 * half
            target[start : start + 16, tile * LANES : (tile + 1) * LANES] = both.astype(BF16)

    step_rows = [sub % 4 - lane // FEAT % 2 == dy for dy in range(3)]
    apart = sub // 4 - lane // (2 * FEAT)
    masks = {}
    for shift in range(-1, 4):
        for dc in range(3):
            if -1 <= dc - shift <= 1:
                for dy in range(3):
                    masks[shift, dc, dy] = step_rows[dy] & (apart == dc - shift)
    for tile in range(WINDOW * EARLY * FEAT // LANES):
        for dx in range(3):
            parts = []
            for pair in range(6):
                value = zero
                for dc in range(3):
                    for dy in range(3):
                        mask = masks.get((2 * pair - 2 * tile, dc, dy))
                        if mask is not None:
                            value = jnp.where(mask, rows[dc * 3 + dy][dx : dx + 1, :], value)
                parts.append(value)
            store(w_early, 48 * dx, tile, parts)
        w_early[144:256, tile * LANES : (tile + 1) * LANES] = jnp.zeros((112, LANES), BF16)

    q = late_row(lane // FEAT, odd)
    y = 2 * sky - 2 + q
    inside = (y >= 0) & (y < height)
    row_masks = [(sub - q == dy) & inside for dy in range(3)]
    for tile in range(WINDOW):
        for dx in range(3):
            parts = []
            for a in range(10):
                value = zero
                dc = a - tile
                if 0 <= dc <= 2:
                    for dy in range(3):
                        value = jnp.where(row_masks[dy], rows[dc * 3 + dy][dx : dx + 1, :], value)
                parts.append(value)
            store(w_late, 80 * dx, tile, parts)
        w_late[240:256, tile * LANES : (tile + 1) * LANES] = jnp.zeros((16, LANES), BF16)


def fill_second(kernel, odd, spread_taps, w_early, w_late):
    eye = (iota((FEAT, FEAT), 0) == iota((FEAT, FEAT), 1)).astype(BF16)
    source = iota((LANES, 4 * LANES), 0)
    target = iota((LANES, 4 * LANES), 1)
    spread = (source == target // LANES * FEAT + target % FEAT).astype(BF16)
    for t in range(7):
        count = min(4, 27 - 4 * t)
        part = kernel[4 * t : 4 * t + count].reshape(count * FEAT, FEAT)
        if count < 4:
            part = jnp.concatenate([part, jnp.zeros(((4 - count) * FEAT, FEAT), BF16)], axis=0)
        turned = dot_nt(eye, part).astype(BF16)
        wide = dot(turned, spread).astype(BF16)
        for g in range(count):
            spread_taps[4 * t + g] = wide[:, g * LANES : (g + 1) * LANES]
    lane = iota((FEAT, LANES), 1) // FEAT
    zero = jnp.zeros((FEAT, LANES), BF16)

    def block(dx, dc, offset):
        value = zero
        if 0 <= dc <= 2:
            for dy in range(3):
                tap = spread_taps[(dc * 3 + dy) * 3 + dx]
                value = jnp.where(lane == offset - dy, tap, value)
        return value

    for dx in range(3):
        for cin in range(4):
            for cout in range(2):
                lanes = slice(cout * LANES, (cout + 1) * LANES)
                for e in range(EARLY):
                    base = (cin * EARLY + e) * FEAT
                    q = jnp.where(odd, 1, 3) + e
                    w_early[dx, base : base + FEAT, lanes] = block(dx, cin - cout, q)
                for l in range(LATE):
                    base = (cin * LATE + l) * FEAT
                    w_late[dx, base : base + FEAT, lanes] = block(
                        dx, cin - cout, late_row(jnp.int32(l), odd)
                    )


def fill_proposal(kernel, w_prop):
    wide = kernel.shape[3]
    zero = jnp.zeros((FEAT, wide), BF16)
    for dx in range(3):
        for moment in range(2):
            for y in range(4):
                base = ((dx * 2 + moment) * 4 + y) * FEAT
                for yout in range(2):
                    dy = y - yout
                    value = zero
                    if 0 <= dy <= 2:
                        value = kernel[dy, dx, moment * FEAT : (moment + 1) * FEAT, :]
                    w_prop[base : base + FEAT, yout * wide : (yout + 1) * wide] = value


def fill_heads(score, box, heads):
    lines = heads.shape[0]

    def picked(count, wanted):
        row = iota((lines, count), 0)
        return (wanted(row // HEAD, row % HEAD) == iota((lines, count), 1)).astype(BF16)

    from_score = picked(ANCHORS, lambda g, k: jnp.where((g == 0) & (k < ANCHORS), k, -1))
    from_box = picked(4 * ANCHORS, lambda g, k: jnp.where((g > 0) & (k < ANCHORS), 4 * k + g - 1, -1))
    heads[...] = (dot(from_score, score[...]) + dot(from_box, box[...])).astype(BF16)


def flatten(rx, lines, planes, freq, cols):
    blocks, rows, _ = rx.shape
    values = rx[...].astype(F32)
    marks = values[:, :, LANES - 1 :]
    total = jnp.sum(values * marks, axis=0)
    count = jnp.sum(jnp.broadcast_to(marks, values.shape), axis=0)
    total = functools.reduce(jnp.add, [total[2 * c : 2 * c + 2] for c in range(rows // 2)])
    count = functools.reduce(jnp.add, [count[2 * c : 2 * c + 2] for c in range(rows // 2)])
    baseline = total / jnp.maximum(count, 1.0)
    baseline = jnp.concatenate([baseline] * (rows // 2), axis=0)
    col = WIDTH * freq - 3 + iota((rows, LANES), 1)
    inside = (col >= 0) & (col < cols)
    for block in range(blocks):
        lines[block * rows : (block + 1) * rows, :] = jnp.where(inside, values[block] - baseline, 0.0)
    for y in range(2):
        planes[3 + y] = lines[pl.ds(y, CHANS, stride=2), :].astype(BF16)


def shift_columns(lines, shifted):
    for start in range(0, lines.shape[0], 16):
        part = lines[start : start + 16, :]
        for dx in range(3):
            moved = part if dx == 0 else pltpu.roll(part, LANES - dx, 1)
            shifted[dx, start : start + 16, :] = moved.astype(BF16)


def clear_edges(lines, count):
    for start, stop in ((0, 2 * count), ((CHANS + 2) * count, lines.shape[0])):
        lines[start:stop, :] = jnp.zeros((stop - start, LANES), F32)


def columns_to_rows(shifted, count, span, freq, cols):
    j = iota((ROWS_ONE, 2 * LANES), 0)
    lane = iota((ROWS_ONE, 2 * LANES), 1)
    x = j % 8 * STRIDE + j // SLAB
    col = WIDTH * freq - 2 + x
    inside = (x < WIDTH + 4) & (col >= 0) & (col < cols)
    turn = ((lane == x + j // 8 % 2 * LANES) & inside).astype(BF16)
    zero = jnp.zeros((256 - 3 * span, LANES), BF16)
    blocks = []
    for w in range(WINDOWS + 1):
        halves = []
        for start in (WINDOW * count * w, WINDOW * count * w + count * CHANS // 2):
            parts = [shifted[dx, start : start + span, :] for dx in range(3)]
            halves.append(jnp.concatenate(parts + [zero], axis=0))
        blocks.append(dot_nt(turn, jnp.concatenate(halves, axis=1)).astype(BF16))
    return jnp.concatenate(blocks, axis=0)


def convolve_first(lhs, weights, layer):
    lanes = weights.shape[1]
    chan = lanes // WINDOW
    tail = layer.shape[1] - WINDOWS * lanes
    row = iota((ROWS_ONE, 256), 0) // 8 % 2
    lane = iota((ROWS_ONE, 256), 1)
    for n in range(lanes // 256):
        count = WINDOWS + 1 if 256 * n < tail else WINDOWS
        value = jnp.maximum(dot(lhs[: count * ROWS_ONE], weights[:, 256 * n : 256 * n + 256]), 0.0)
        for w in range(count):
            part = value[ROWS_ONE * w : ROWS_ONE * (w + 1)]
            base = w * lanes + 256 * n
            if base == 0:
                part = jnp.where((row == 0) & (lane < chan), 0.0, part)
            if w == WINDOWS:
                part = jnp.where((row == 1) & (lane >= chan - 256 * n), 0.0, part)
            part = part[:, : min(256, layer.shape[1] - base)].astype(BF16)
            layer[:, base : base + part.shape[1]] = part


def convolve_second(layer, weights, pairs):
    span = weights.shape[1]
    step = span // 2
    total = None
    for dx in range(3):
        parts = [layer[SLAB * dx : SLAB * dx + ROWS_TWO, step * p : step * p + span] for p in pairs]
        part = dot(jnp.concatenate(parts, axis=0), weights[dx])
        total = part if total is None else total + part
    return total


def groups():
    return [range(start, start + GROUP) for start in range(0, PAIRS, GROUP)]


def sum_moments(layer, weights, partial):
    zeroth = jnp.zeros((ROWS_TWO, LANES), F32)
    first = jnp.zeros((ROWS_TWO, LANES), F32)
    for pairs in groups():
        rows = pl.ds(pairs[0] * ROWS_TWO, GROUP * ROWS_TWO)
        total = jnp.maximum(convolve_second(layer, weights, pairs) + partial[rows, :], 0.0)
        for i, p in enumerate(pairs):
            for half in range(2):
                c = 2 * p + half
                value = total[
                    ROWS_TWO * i : ROWS_TWO * (i + 1), LANES * half : LANES * (half + 1)
                ]
                zeroth = zeroth + value
                first = first + ((c + 0.5) / CHANS - 0.5) * value
    low, high = [zeroth.reshape(STRIDE, 2, 8, LANES)[:, h].reshape(-1, LANES) for h in range(2)]
    parts = [first.reshape(STRIDE, 2, 8, LANES)[:, h].reshape(-1, LANES) for h in range(2)]
    first = parts[0] + parts[1] + 0.5 * high
    return (low + high) * (1.0 / CHANS), first * (12.0 / CHANS)


def propose(zeroth, first, w_prop, heads, freq, sky, height, cols, result):
    maps = jnp.concatenate([zeroth, first], axis=1)
    y = 2 * sky - 1 + iota(maps.shape, 1) // FEAT % 4
    maps = jnp.where((y >= 0) & (y < height), maps, 0.0).astype(BF16)
    row = iota((3 * WIDTH, 8 * STRIDE), 0)
    x = row % WIDTH + row // WIDTH
    col = WIDTH * freq - 1 + x
    j = iota((3 * WIDTH, 8 * STRIDE), 1)
    turn = ((j % 8 * STRIDE + j // 8 == x) & (col >= 0) & (col < cols)).astype(BF16)
    framed = dot(turn, maps).astype(BF16)
    framed = jnp.concatenate([framed[WIDTH * dx : WIDTH * (dx + 1)] for dx in range(3)], axis=1)
    hidden = jnp.maximum(dot(framed, w_prop[...]), 0.0).astype(BF16)
    wide = hidden.shape[1] // 2
    stacked = jnp.concatenate([hidden[:, :wide], hidden[:, wide:]], axis=0)
    out = dot_nt(heads[...], stacked)
    score, dx, dy, dw, dh = [out[HEAD * g : HEAD * (g + 1)] for g in range(5)]
    k = iota(score.shape, 0)
    lane = iota(score.shape, 1)
    anchor_width = jnp.ones(score.shape, F32)
    anchor_height = anchor_width
    for anchor in range(ANCHORS):
        scale = 4.0 * 2.0 ** (anchor // 3)
        root = (2.0 ** (anchor % 3 - 1)) ** 0.5
        anchor_width = jnp.where(k == anchor, scale * root, anchor_width)
        anchor_height = jnp.where(k == anchor, scale / root, anchor_height)
    centre_x = (WIDTH * freq + lane % WIDTH).astype(F32) + 0.5 + dx * anchor_width
    centre_y = (2 * sky + lane // WIDTH).astype(F32) + 0.5 + dy * anchor_height
    half_width = 0.5 * (anchor_width * jnp.exp(dw))
    half_height = 0.5 * (anchor_height * jnp.exp(dh))
    corners = (
        centre_x - half_width,
        centre_y - half_height,
        centre_x + half_width,
        centre_y + half_height,
    )
    parts = (score,) + tuple(corner * (1.0 / 64.0) for corner in corners)
    for g, part in enumerate(parts):
        for row in range(2):
            result[:, g, row, :] = part[:ANCHORS, WIDTH * row : WIDTH * (row + 1)]


def body(
    shape,
    cube_hbm, free_hbm, taps_hbm, kernel_hbm, proposal_hbm, score_hbm, box_hbm,
    result,
    cube, free, taps, kernel, proposal, score, box,
    tx, rx, planes, lines, lines_early, lines_late, shifted_early, shifted_late, w_one_early, w_one_late,
    spread_taps, w_two_early, w_two_late, w_prop, heads, layer_early, layer_late, partial,
    load_sem, send_sem, recv_sem, halo_send, halo_recv, late, clear,
    passing, hub_send, hub_recv,
):
    freq_count, sky_count, height, cols = shape
    freq = lax.axis_index("freq")
    sky = lax.axis_index("sky")
    odd = lax.rem(sky, 2) == 1
    barrier = pltpu.get_barrier_semaphore()
    cut = max(2, freq_count * 7 // 16 // 2 * 2)
    is_first = freq < cut
    middle = freq_count * 11 // 16
    end = freq_count * 3 // 4
    hubs = (freq_count - end) // 2
    origin = min(cut, 2 + 2 * hubs)
    is_source = (freq >= origin) & (freq < middle)
    is_hub = (freq >= 2) & (freq < 2 + 2 * hubs)

    def hub_of(target):
        return 2 * (hubs - (target - end) // 2) + target % 2

    def freq_peer(i):
        return i + (i >= freq).astype(jnp.int32)

    def in_sky(i):
        return (sky + i >= 0) & (sky + i < sky_count)

    def greet(i, carry):
        peer = lax.rem(freq + freq_count // 2 + (i + 1) // 2 * (1 - 2 * (i % 2)) + freq_count, freq_count)
        pl.semaphore_signal(barrier, inc=1, device_id={"freq": peer}, device_id_type=MESH)
        return carry

    moves = (
        (cube_hbm, cube), (free_hbm, free), (taps_hbm, taps), (kernel_hbm, kernel),
        (proposal_hbm, proposal), (score_hbm, score), (box_hbm, box),
    )
    loads = [
        pltpu.make_async_copy(source, target, load_sem.at[i])
        for i, (source, target) in enumerate(moves)
    ]
    for load in loads[:2]:
        load.start()

    @pl.when(is_first)
    def _():
        for i in range(freq_count - 1):
            greet(i, 0)

    neighbours = 0
    for i in (-2, -1, 1, 2):
        neighbours += in_sky(i).astype(jnp.int32)

        @pl.when(in_sky(i))
        def _():
            pl.semaphore_signal(barrier, inc=1, device_id={"sky": sky + i}, device_id_type=MESH)

    for load in loads[2:]:
        load.start()
    pl.semaphore_wait(barrier, cut - is_first.astype(jnp.int32) + neighbours)

    def announce(i, carry):
        pl.semaphore_signal(late, inc=1, device_id={"freq": i}, device_id_type=MESH)
        return carry

    @pl.when(jnp.logical_not(is_first))
    def _():
        for i in range(cut):
            announce(i, 0)

    def exchange(peer):
        return pltpu.make_async_remote_copy(
            src_ref=tx.at[peer],
            dst_ref=rx.at[freq],
            send_sem=send_sem.at[peer],
            recv_sem=recv_sem.at[freq],
            device_id={"freq": peer},
            device_id_type=MESH,
        )

    def arrival(peer):
        return pltpu.make_async_remote_copy(
            src_ref=tx.at[peer],
            dst_ref=rx.at[peer],
            send_sem=send_sem.at[peer],
            recv_sem=recv_sem.at[peer],
            device_id={"freq": peer},
            device_id_type=MESH,
        )

    def send(peer):
        wanted = peer != freq
        if peer >= end:
            wanted &= jnp.logical_not(is_source)

        @pl.when(wanted)
        def _():
            exchange(peer).start()

    def to_hub(peer):
        return pltpu.make_async_remote_copy(
            src_ref=tx.at[peer],
            dst_ref=passing.at[freq - origin],
            send_sem=send_sem.at[peer],
            recv_sem=hub_recv.at[freq - origin],
            device_id={"freq": hub_of(peer)},
            device_id_type=MESH,
        )

    def from_hub(slot):
        return pltpu.make_async_remote_copy(
            src_ref=passing.at[slot],
            dst_ref=rx.at[origin + slot],
            send_sem=hub_send.at[slot],
            recv_sem=recv_sem.at[origin + slot],
            device_id={"freq": end + 2 * (hubs - freq // 2) + lax.rem(freq, 2)},
            device_id_type=MESH,
        )

    def at_hub(slot):
        return pltpu.make_async_remote_copy(
            src_ref=passing.at[slot],
            dst_ref=passing.at[slot],
            send_sem=hub_send.at[slot],
            recv_sem=hub_recv.at[slot],
            device_id={"freq": origin + slot},
            device_id_type=MESH,
        )

    def release(i, carry):
        peer = cut + 2 * i + freq
        pl.semaphore_signal(clear, inc=1, device_id={"freq": peer}, device_id_type=MESH)
        return carry

    def finish(i):
        @pl.when(i != freq)
        def _():
            arrival(i).wait_recv()

    def settle(i):
        @pl.when(i != freq)
        def _():
            arrival(i).wait_send()

    loads[0].wait()
    loads[1].wait()
    fill_tx(cube, free, tx, cut, send)

    @pl.when(is_source)
    def _():
        for peer in reversed(range(end, freq_count)):
            to_hub(peer).start()

    rx[freq] = tx[freq]
    for load in loads[2:]:
        load.wait()
    fill_first(taps, sky, height, odd, w_one_early, w_one_late)
    fill_second(kernel, odd, spread_taps, w_two_early, w_two_late)
    fill_proposal(proposal, w_prop)
    fill_heads(score, box, heads)
    clear_edges(lines_early, 4)
    clear_edges(lines_late, 8)

    @pl.when(is_first)
    def _():
        pl.semaphore_wait(late, freq_count - cut)

    @pl.when(freq < 2)
    def _():
        for i in range((freq_count - cut) // 2):
            release(i, 0)

    @pl.when(jnp.logical_not(is_first))
    def _():
        pl.semaphore_wait(clear, 1)

    from_end = (freq >= freq_count * 3 // 16) & (freq < freq_count * 11 // 16)

    @pl.when(from_end)
    def _():
        for i in reversed(range(cut, freq_count)):
            send(i)

    @pl.when(jnp.logical_not(from_end))
    def _():
        for i in range(cut, freq_count):
            send(i)

    @pl.when(is_hub)
    def _():
        for slot in range(middle - origin):
            at_hub(slot).wait_recv()
            from_hub(slot).start()

    for i in range(freq_count):
        finish(i)

    flatten(rx, lines, planes, freq, cols)
    halos = []
    for n, (i, source, target) in enumerate(((2, 4, 0), (-2, 3, 7), (1, 3, 1), (-1, 3, 5))):
        size = 2 if abs(i) == 1 else 1
        halo = pltpu.make_async_remote_copy(
            src_ref=planes.at[pl.ds(source, size)],
            dst_ref=planes.at[pl.ds(target, size)],
            send_sem=halo_send.at[n],
            recv_sem=halo_recv.at[n],
            device_id={"sky": sky + i},
            device_id_type=MESH,
        )
        halos.append((i, halo))
    for i, halo in halos:
        pl.when(in_sky(i))(halo.start)
    mate = dict(halos)
    pl.when(odd)(mate[1].wait_recv)
    pl.when(jnp.logical_not(odd))(mate[-1].wait_recv)
    for i in range(4):
        lines_early[pl.ds(8 + i, CHANS, stride=4), :] = planes[jnp.where(odd, 1, 3) + i].astype(F32)
    shift_columns(lines_early, shifted_early)
    convolve_first(
        columns_to_rows(shifted_early, 4, 48, freq, cols), w_one_early, layer_early
    )
    for pairs in groups():
        rows = pl.ds(pairs[0] * ROWS_TWO, GROUP * ROWS_TWO)
        partial[rows, :] = convolve_second(layer_early, w_two_early, pairs)

    for i, halo in halos:
        pl.when(in_sky(i))(halo.wait_send)
    for i in range(freq_count):
        settle(i)

    @pl.when(is_hub)
    def _():
        for slot in range(middle - origin):
            from_hub(slot).wait_send()

    for i, halo in halos:
        if abs(i) == 2:
            pl.when(in_sky(-i))(halo.wait_recv)
    pl.when(jnp.logical_not(odd) & in_sky(-1))(mate[1].wait_recv)
    pl.when(odd & in_sky(1))(mate[-1].wait_recv)
    for r in range(8):
        y = 2 * sky - 3 + r
        value = planes[r].astype(F32)
        if r not in (3, 4):
            value = jnp.where((y >= 0) & (y < height), value, 0.0)
        lines_late[pl.ds(16 + r, CHANS, stride=8), :] = value
    shift_columns(lines_late, shifted_late)
    convolve_first(columns_to_rows(shifted_late, 8, 80, freq, cols), w_one_late, layer_late)
    zeroth, first = sum_moments(layer_late, w_two_late, partial)
    propose(zeroth, first, w_prop, heads, freq, sky, height, cols, result)


def on_device(sky_cube, free_mask, conv_first, conv_second, proposal_conv, score_head, box_head):
    freq_count = lax.axis_size("freq")
    sky_count = lax.axis_size("sky")
    chans, rows, cols = sky_cube.shape
    wide = proposal_conv.shape[3]
    taps = conv_first.transpose(1, 2, 3, 4, 0).reshape(9, 3, FEAT)
    kernel = conv_second.transpose(2, 3, 4, 0, 1).reshape(27, FEAT, FEAT)
    free = free_mask.reshape(1, chans)
    operands = (sky_cube, free, taps, kernel, proposal_conv, score_head, box_head)
    scratch = [pltpu.VMEM(operand.shape, operand.dtype) for operand in operands] + [
        pltpu.VMEM((freq_count, chans * rows, LANES), BF16),
        pltpu.VMEM((freq_count, chans * rows, LANES), BF16),
        pltpu.VMEM((8, CHANS, LANES), BF16),
        pltpu.VMEM((2 * CHANS + 8, LANES), F32),
        pltpu.VMEM((4 * CHANS + 48, LANES), F32),
        pltpu.VMEM((8 * CHANS + 80, LANES), F32),
        pltpu.VMEM((3, 4 * CHANS + 48, LANES), BF16),
        pltpu.VMEM((3, 8 * CHANS + 80, LANES), BF16),
        pltpu.VMEM((256, WINDOW * EARLY * FEAT), BF16),
        pltpu.VMEM((256, WINDOW * LATE * FEAT), BF16),
        pltpu.VMEM((27, FEAT, LANES), BF16),
        pltpu.VMEM((3, 4 * EARLY * FEAT, 256), BF16),
        pltpu.VMEM((3, 4 * LATE * FEAT, 256), BF16),
        pltpu.VMEM((3 * 256, 2 * wide), BF16),
        pltpu.VMEM((5 * HEAD, wide), BF16),
        pltpu.VMEM((ROWS_ONE, 2 * (PAIRS + 1) * EARLY * FEAT), BF16),
        pltpu.VMEM((ROWS_ONE, 2 * (PAIRS + 1) * LATE * FEAT), BF16),
        pltpu.VMEM((PAIRS * ROWS_TWO, 256), F32),
        pltpu.SemaphoreType.DMA((len(operands),)),
        pltpu.SemaphoreType.DMA((freq_count,)),
        pltpu.SemaphoreType.DMA((freq_count,)),
        pltpu.SemaphoreType.DMA((4,)),
        pltpu.SemaphoreType.DMA((4,)),
        pltpu.SemaphoreType.REGULAR,
        pltpu.SemaphoreType.REGULAR,
        pltpu.VMEM((freq_count // 2, chans * rows, LANES), BF16),
        pltpu.SemaphoreType.DMA((freq_count // 2,)),
        pltpu.SemaphoreType.DMA((freq_count // 2,)),
    ]
    shape = (freq_count, sky_count, rows * sky_count, cols)
    result = pl.pallas_call(
        functools.partial(body, shape),
        out_shape=pltpu.VMEM((ANCHORS, 5, rows, WIDTH), F32),
        in_specs=[pl.BlockSpec(memory_space=pltpu.HBM)] * len(operands),
        out_specs=pl.BlockSpec(memory_space=pltpu.VMEM),
        scratch_shapes=scratch,
        compiler_params=pltpu.CompilerParams(
            collective_id=0, has_side_effects=True, vmem_limit_bytes=60 * 1024 * 1024
        ),
    )(*operands)
    return result[:, 0], result[:, 1:]


def solution(mesh):
    in_specs = (P("freq", "sky", None), P("freq"), P(), P(), P(), P(), P())
    out_specs = (P(None, "sky", "freq"), P(None, None, "sky", "freq"))
    return jax.shard_map(
        on_device, mesh=mesh, in_specs=in_specs, out_specs=out_specs, check_vma=False
    )
```

```python
import functools

import jax
import jax.numpy as jnp
from jax import lax
from jax.experimental import pallas as pl
from jax.experimental.pallas import tpu as pltpu
from jax.sharding import PartitionSpec as P

F32 = jnp.float32
BF16 = jnp.bfloat16
MESH = pl.DeviceIdType.MESH
CHANS = 64
FEAT = 32
ANCHORS = 9
WIDTH = 64
LANES = 128
SLAB = 16
HEAD = 16
STRIDE = 9
ROWS_ONE = (STRIDE + 2) * SLAB
ROWS_TWO = STRIDE * SLAB
PAIRS = CHANS // 4
EARLY = 2
LATE = 4
WINDOW = 8
WINDOWS = CHANS // 2 // WINDOW
GROUP = 2
NT = (((1,), (1,)), ((), ()))


def iota(shape, dim):
    return lax.broadcasted_iota(jnp.int32, shape, dim)


def dot(a, b):
    return jnp.dot(a, b, preferred_element_type=F32)


def dot_nt(a, b):
    return lax.dot_general(a, b, NT, preferred_element_type=F32)


def fill_tx(cube, free, tx, count, send):
    chans, rows, cols = cube.shape
    lines = chans * rows
    values = cube[...].astype(F32).reshape(lines, cols)
    line = iota((lines, LANES), 0)
    lane = iota((lines, LANES), 1)
    marks = jnp.zeros((lines, LANES), F32)
    flags = free[...].astype(F32)
    for c in range(chans):
        marks = jnp.where(line // rows == c, flags[0:1, c : c + 1], marks)
    even = jnp.concatenate([values[:, cols - 3 :], values[:, : cols - 3]], axis=1)
    odd = jnp.concatenate([values[:, WIDTH - 3 :], values[:, : WIDTH - 3]], axis=1)
    for block in range(cols // WIDTH):
        source = odd if block % 2 else even
        start = block // 2 * LANES
        piece = source[:, start : start + LANES]
        tx[block] = jnp.where(lane == LANES - 1, marks, piece).astype(BF16)
        if block == count - 1:
            for peer in range(count):
                send(peer)


def late_row(index, odd):
    return index + 2 * (index >= jnp.where(odd, 1, 3)).astype(jnp.int32)


def fill_first(taps, sky, height, odd, w_early, w_late):
    spread = (iota((FEAT, LANES), 1) % FEAT == iota((FEAT, LANES), 0)).astype(BF16)
    rows = [dot(taps[i], spread) for i in range(9)]
    sub = iota((8, LANES), 0)
    lane = iota((8, LANES), 1)
    zero = jnp.zeros((8, LANES), F32)

    def store(target, base, tile, parts):
        for half in range(len(parts) // 2):
            both = jnp.concatenate([parts[2 * half], parts[2 * half + 1]], axis=0)
            start = base + 16 * half
            target[start : start + 16, tile * LANES : (tile + 1) * LANES] = both.astype(BF16)

    step_rows = [sub % 4 - lane // FEAT % 2 == dy for dy in range(3)]
    apart = sub // 4 - lane // (2 * FEAT)
    masks = {}
    for shift in range(-1, 4):
        for dc in range(3):
            if -1 <= dc - shift <= 1:
                for dy in range(3):
                    masks[shift, dc, dy] = step_rows[dy] & (apart == dc - shift)
    for tile in range(WINDOW * EARLY * FEAT // LANES):
        for dx in range(3):
            parts = []
            for pair in range(6):
                value = zero
                for dc in range(3):
                    for dy in range(3):
                        mask = masks.get((2 * pair - 2 * tile, dc, dy))
                        if mask is not None:
                            value = jnp.where(mask, rows[dc * 3 + dy][dx : dx + 1, :], value)
                parts.append(value)
            store(w_early, 48 * dx, tile, parts)
        w_early[144:256, tile * LANES : (tile + 1) * LANES] = jnp.zeros((112, LANES), BF16)

    q = late_row(lane // FEAT, odd)
    y = 2 * sky - 2 + q
    inside = (y >= 0) & (y < height)
    row_masks = [(sub - q == dy) & inside for dy in range(3)]
    for tile in range(WINDOW):
        for dx in range(3):
            parts = []
            for a in range(10):
                value = zero
                dc = a - tile
                if 0 <= dc <= 2:
                    for dy in range(3):
                        value = jnp.where(row_masks[dy], rows[dc * 3 + dy][dx : dx + 1, :], value)
                parts.append(value)
            store(w_late, 80 * dx, tile, parts)
        w_late[240:256, tile * LANES : (tile + 1) * LANES] = jnp.zeros((16, LANES), BF16)


def fill_second(kernel, odd, spread_taps, w_early, w_late):
    eye = (iota((FEAT, FEAT), 0) == iota((FEAT, FEAT), 1)).astype(BF16)
    source = iota((LANES, 4 * LANES), 0)
    target = iota((LANES, 4 * LANES), 1)
    spread = (source == target // LANES * FEAT + target % FEAT).astype(BF16)
    for t in range(7):
        count = min(4, 27 - 4 * t)
        part = kernel[4 * t : 4 * t + count].reshape(count * FEAT, FEAT)
        if count < 4:
            part = jnp.concatenate([part, jnp.zeros(((4 - count) * FEAT, FEAT), BF16)], axis=0)
        turned = dot_nt(eye, part).astype(BF16)
        wide = dot(turned, spread).astype(BF16)
        for g in range(count):
            spread_taps[4 * t + g] = wide[:, g * LANES : (g + 1) * LANES]
    lane = iota((FEAT, LANES), 1) // FEAT
    zero = jnp.zeros((FEAT, LANES), BF16)

    def block(dx, dc, offset):
        value = zero
        if 0 <= dc <= 2:
            for dy in range(3):
                tap = spread_taps[(dc * 3 + dy) * 3 + dx]
                value = jnp.where(lane == offset - dy, tap, value)
        return value

    for dx in range(3):
        for cin in range(4):
            for cout in range(2):
                lanes = slice(cout * LANES, (cout + 1) * LANES)
                for e in range(EARLY):
                    base = (cin * EARLY + e) * FEAT
                    q = jnp.where(odd, 1, 3) + e
                    w_early[dx, base : base + FEAT, lanes] = block(dx, cin - cout, q)
                for l in range(LATE):
                    base = (cin * LATE + l) * FEAT
                    w_late[dx, base : base + FEAT, lanes] = block(
                        dx, cin - cout, late_row(jnp.int32(l), odd)
                    )


def fill_proposal(kernel, w_prop):
    wide = kernel.shape[3]
    zero = jnp.zeros((FEAT, wide), BF16)
    for dx in range(3):
        for moment in range(2):
            for y in range(4):
                base = ((dx * 2 + moment) * 4 + y) * FEAT
                for yout in range(2):
                    dy = y - yout
                    value = zero
                    if 0 <= dy <= 2:
                        value = kernel[dy, dx, moment * FEAT : (moment + 1) * FEAT, :]
                    w_prop[base : base + FEAT, yout * wide : (yout + 1) * wide] = value


def fill_heads(score, box, heads):
    lines = heads.shape[0]

    def picked(count, wanted):
        row = iota((lines, count), 0)
        return (wanted(row // HEAD, row % HEAD) == iota((lines, count), 1)).astype(BF16)

    from_score = picked(ANCHORS, lambda g, k: jnp.where((g == 0) & (k < ANCHORS), k, -1))
    from_box = picked(4 * ANCHORS, lambda g, k: jnp.where((g > 0) & (k < ANCHORS), 4 * k + g - 1, -1))
    heads[...] = (dot(from_score, score[...]) + dot(from_box, box[...])).astype(BF16)


def flatten(rx, lines, planes, freq, cols):
    blocks, rows, _ = rx.shape
    values = rx[...].astype(F32)
    marks = values[:, :, LANES - 1 :]
    total = jnp.sum(values * marks, axis=0)
    count = jnp.sum(jnp.broadcast_to(marks, values.shape), axis=0)
    total = functools.reduce(jnp.add, [total[2 * c : 2 * c + 2] for c in range(rows // 2)])
    count = functools.reduce(jnp.add, [count[2 * c : 2 * c + 2] for c in range(rows // 2)])
    baseline = total / jnp.maximum(count, 1.0)
    baseline = jnp.concatenate([baseline] * (rows // 2), axis=0)
    col = WIDTH * freq - 3 + iota((rows, LANES), 1)
    inside = (col >= 0) & (col < cols)
    for block in range(blocks):
        lines[block * rows : (block + 1) * rows, :] = jnp.where(inside, values[block] - baseline, 0.0)
    for y in range(2):
        planes[3 + y] = lines[pl.ds(y, CHANS, stride=2), :].astype(BF16)


def shift_columns(lines, shifted):
    for start in range(0, lines.shape[0], 16):
        part = lines[start : start + 16, :]
        for dx in range(3):
            moved = part if dx == 0 else pltpu.roll(part, LANES - dx, 1)
            shifted[dx, start : start + 16, :] = moved.astype(BF16)


def clear_edges(lines, count):
    for start, stop in ((0, 2 * count), ((CHANS + 2) * count, lines.shape[0])):
        lines[start:stop, :] = jnp.zeros((stop - start, LANES), F32)


def columns_to_rows(shifted, count, span, freq, cols):
    j = iota((ROWS_ONE, 2 * LANES), 0)
    lane = iota((ROWS_ONE, 2 * LANES), 1)
    x = j % 8 * STRIDE + j // SLAB
    col = WIDTH * freq - 2 + x
    inside = (x < WIDTH + 4) & (col >= 0) & (col < cols)
    turn = ((lane == x + j // 8 % 2 * LANES) & inside).astype(BF16)
    zero = jnp.zeros((256 - 3 * span, LANES), BF16)
    blocks = []
    for w in range(WINDOWS + 1):
        halves = []
        for start in (WINDOW * count * w, WINDOW * count * w + count * CHANS // 2):
            parts = [shifted[dx, start : start + span, :] for dx in range(3)]
            halves.append(jnp.concatenate(parts + [zero], axis=0))
        blocks.append(dot_nt(turn, jnp.concatenate(halves, axis=1)).astype(BF16))
    return jnp.concatenate(blocks, axis=0)


def convolve_first(lhs, weights, layer):
    lanes = weights.shape[1]
    chan = lanes // WINDOW
    tail = layer.shape[1] - WINDOWS * lanes
    row = iota((ROWS_ONE, 256), 0) // 8 % 2
    lane = iota((ROWS_ONE, 256), 1)
    for n in range(lanes // 256):
        count = WINDOWS + 1 if 256 * n < tail else WINDOWS
        value = jnp.maximum(dot(lhs[: count * ROWS_ONE], weights[:, 256 * n : 256 * n + 256]), 0.0)
        for w in range(count):
            part = value[ROWS_ONE * w : ROWS_ONE * (w + 1)]
            base = w * lanes + 256 * n
            if base == 0:
                part = jnp.where((row == 0) & (lane < chan), 0.0, part)
            if w == WINDOWS:
                part = jnp.where((row == 1) & (lane >= chan - 256 * n), 0.0, part)
            part = part[:, : min(256, layer.shape[1] - base)].astype(BF16)
            layer[:, base : base + part.shape[1]] = part


def convolve_second(layer, weights, pairs):
    span = weights.shape[1]
    step = span // 2
    total = None
    for dx in range(3):
        parts = [layer[SLAB * dx : SLAB * dx + ROWS_TWO, step * p : step * p + span] for p in pairs]
        part = dot(jnp.concatenate(parts, axis=0), weights[dx])
        total = part if total is None else total + part
    return total


def groups():
    return [range(start, start + GROUP) for start in range(0, PAIRS, GROUP)]


def sum_moments(layer, weights, partial):
    zeroth = jnp.zeros((ROWS_TWO, LANES), F32)
    first = jnp.zeros((ROWS_TWO, LANES), F32)
    for pairs in groups():
        rows = pl.ds(pairs[0] * ROWS_TWO, GROUP * ROWS_TWO)
        total = jnp.maximum(convolve_second(layer, weights, pairs) + partial[rows, :], 0.0)
        for i, p in enumerate(pairs):
            for half in range(2):
                c = 2 * p + half
                value = total[
                    ROWS_TWO * i : ROWS_TWO * (i + 1), LANES * half : LANES * (half + 1)
                ]
                zeroth = zeroth + value
                first = first + ((c + 0.5) / CHANS - 0.5) * value
    low, high = [zeroth.reshape(STRIDE, 2, 8, LANES)[:, h].reshape(-1, LANES) for h in range(2)]
    parts = [first.reshape(STRIDE, 2, 8, LANES)[:, h].reshape(-1, LANES) for h in range(2)]
    first = parts[0] + parts[1] + 0.5 * high
    return (low + high) * (1.0 / CHANS), first * (12.0 / CHANS)


def propose(zeroth, first, w_prop, heads, freq, sky, height, cols, result):
    maps = jnp.concatenate([zeroth, first], axis=1)
    y = 2 * sky - 1 + iota(maps.shape, 1) // FEAT % 4
    maps = jnp.where((y >= 0) & (y < height), maps, 0.0).astype(BF16)
    row = iota((3 * WIDTH, 8 * STRIDE), 0)
    x = row % WIDTH + row // WIDTH
    col = WIDTH * freq - 1 + x
    j = iota((3 * WIDTH, 8 * STRIDE), 1)
    turn = ((j % 8 * STRIDE + j // 8 == x) & (col >= 0) & (col < cols)).astype(BF16)
    framed = dot(turn, maps).astype(BF16)
    framed = jnp.concatenate([framed[WIDTH * dx : WIDTH * (dx + 1)] for dx in range(3)], axis=1)
    hidden = jnp.maximum(dot(framed, w_prop[...]), 0.0).astype(BF16)
    wide = hidden.shape[1] // 2
    stacked = jnp.concatenate([hidden[:, :wide], hidden[:, wide:]], axis=0)
    out = dot_nt(heads[...], stacked)
    score, dx, dy, dw, dh = [out[HEAD * g : HEAD * (g + 1)] for g in range(5)]
    k = iota(score.shape, 0)
    lane = iota(score.shape, 1)
    anchor_width = jnp.ones(score.shape, F32)
    anchor_height = anchor_width
    for anchor in range(ANCHORS):
        scale = 4.0 * 2.0 ** (anchor // 3)
        root = (2.0 ** (anchor % 3 - 1)) ** 0.5
        anchor_width = jnp.where(k == anchor, scale * root, anchor_width)
        anchor_height = jnp.where(k == anchor, scale / root, anchor_height)
    centre_x = (WIDTH * freq + lane % WIDTH).astype(F32) + 0.5 + dx * anchor_width
    centre_y = (2 * sky + lane // WIDTH).astype(F32) + 0.5 + dy * anchor_height
    half_width = 0.5 * (anchor_width * jnp.exp(dw))
    half_height = 0.5 * (anchor_height * jnp.exp(dh))
    corners = (
        centre_x - half_width,
        centre_y - half_height,
        centre_x + half_width,
        centre_y + half_height,
    )
    parts = (score,) + tuple(corner * (1.0 / 64.0) for corner in corners)
    for g, part in enumerate(parts):
        for row in range(2):
            result[:, g, row, :] = part[:ANCHORS, WIDTH * row : WIDTH * (row + 1)]


def body(
    shape,
    cube_hbm, free_hbm, taps_hbm, kernel_hbm, proposal_hbm, score_hbm, box_hbm,
    result,
    cube, free, taps, kernel, proposal, score, box,
    tx, rx, planes, lines, lines_early, lines_late, shifted_early, shifted_late, w_one_early, w_one_late,
    spread_taps, w_two_early, w_two_late, w_prop, heads, layer_early, layer_late, partial,
    load_sem, send_sem, recv_sem, halo_send, halo_recv, late, clear,
    passing, hub_send, hub_recv,
):
    freq_count, sky_count, height, cols = shape
    freq = lax.axis_index("freq")
    sky = lax.axis_index("sky")
    odd = lax.rem(sky, 2) == 1
    barrier = pltpu.get_barrier_semaphore()
    cut = max(2, freq_count * 8 // 16 // 2 * 2)
    is_first = freq < cut
    middle = freq_count * 11 // 16
    end = freq_count * 3 // 4
    hubs = (freq_count - end) // 2
    origin = min(cut, 2 + 2 * hubs)
    is_source = (freq >= origin) & (freq < middle)
    is_hub = (freq >= 2) & (freq < 2 + 2 * hubs)

    def hub_of(target):
        return 2 * (hubs - (target - end) // 2) + target % 2

    def freq_peer(i):
        return i + (i >= freq).astype(jnp.int32)

    def in_sky(i):
        return (sky + i >= 0) & (sky + i < sky_count)

    def greet(i, carry):
        peer = lax.rem(freq + freq_count // 2 + (i + 1) // 2 * (1 - 2 * (i % 2)) + freq_count, freq_count)
        pl.semaphore_signal(barrier, inc=1, device_id={"freq": peer}, device_id_type=MESH)
        return carry

    moves = (
        (cube_hbm, cube), (free_hbm, free), (taps_hbm, taps), (kernel_hbm, kernel),
        (proposal_hbm, proposal), (score_hbm, score), (box_hbm, box),
    )
    loads = [
        pltpu.make_async_copy(source, target, load_sem.at[i])
        for i, (source, target) in enumerate(moves)
    ]
    for load in loads[:2]:
        load.start()

    @pl.when(is_first)
    def _():
        for i in range(freq_count - 1):
            greet(i, 0)

    neighbours = 0
    for i in (-2, -1, 1, 2):
        neighbours += in_sky(i).astype(jnp.int32)

        @pl.when(in_sky(i))
        def _():
            pl.semaphore_signal(barrier, inc=1, device_id={"sky": sky + i}, device_id_type=MESH)

    for load in loads[2:]:
        load.start()
    pl.semaphore_wait(barrier, cut - is_first.astype(jnp.int32) + neighbours)

    def announce(i, carry):
        pl.semaphore_signal(late, inc=1, device_id={"freq": i}, device_id_type=MESH)
        return carry

    @pl.when(jnp.logical_not(is_first))
    def _():
        for i in range(cut):
            announce(i, 0)

    def exchange(peer):
        return pltpu.make_async_remote_copy(
            src_ref=tx.at[peer],
            dst_ref=rx.at[freq],
            send_sem=send_sem.at[peer],
            recv_sem=recv_sem.at[freq],
            device_id={"freq": peer},
            device_id_type=MESH,
        )

    def arrival(peer):
        return pltpu.make_async_remote_copy(
            src_ref=tx.at[peer],
            dst_ref=rx.at[peer],
            send_sem=send_sem.at[peer],
            recv_sem=recv_sem.at[peer],
            device_id={"freq": peer},
            device_id_type=MESH,
        )

    def send(peer):
        wanted = peer != freq
        if peer >= end:
            wanted &= jnp.logical_not(is_source)

        @pl.when(wanted)
        def _():
            exchange(peer).start()

    def to_hub(peer):
        return pltpu.make_async_remote_copy(
            src_ref=tx.at[peer],
            dst_ref=passing.at[freq - origin],
            send_sem=send_sem.at[peer],
            recv_sem=hub_recv.at[freq - origin],
            device_id={"freq": hub_of(peer)},
            device_id_type=MESH,
        )

    def from_hub(slot):
        return pltpu.make_async_remote_copy(
            src_ref=passing.at[slot],
            dst_ref=rx.at[origin + slot],
            send_sem=hub_send.at[slot],
            recv_sem=recv_sem.at[origin + slot],
            device_id={"freq": end + 2 * (hubs - freq // 2) + lax.rem(freq, 2)},
            device_id_type=MESH,
        )

    def at_hub(slot):
        return pltpu.make_async_remote_copy(
            src_ref=passing.at[slot],
            dst_ref=passing.at[slot],
            send_sem=hub_send.at[slot],
            recv_sem=hub_recv.at[slot],
            device_id={"freq": origin + slot},
            device_id_type=MESH,
        )

    def release(i, carry):
        peer = cut + 2 * i + freq
        pl.semaphore_signal(clear, inc=1, device_id={"freq": peer}, device_id_type=MESH)
        return carry

    def finish(i):
        @pl.when(i != freq)
        def _():
            arrival(i).wait_recv()

    def settle(i):
        @pl.when(i != freq)
        def _():
            arrival(i).wait_send()

    loads[0].wait()
    loads[1].wait()
    fill_tx(cube, free, tx, cut, send)

    @pl.when(is_source)
    def _():
        for peer in reversed(range(end, freq_count)):
            to_hub(peer).start()

    rx[freq] = tx[freq]
    for load in loads[2:]:
        load.wait()
    fill_first(taps, sky, height, odd, w_one_early, w_one_late)
    fill_second(kernel, odd, spread_taps, w_two_early, w_two_late)
    fill_proposal(proposal, w_prop)
    fill_heads(score, box, heads)
    clear_edges(lines_early, 4)
    clear_edges(lines_late, 8)

    @pl.when(is_first)
    def _():
        pl.semaphore_wait(late, freq_count - cut)

    @pl.when(freq < 2)
    def _():
        for i in range((freq_count - cut) // 2):
            release(i, 0)

    @pl.when(jnp.logical_not(is_first))
    def _():
        pl.semaphore_wait(clear, 1)

    from_end = (freq >= freq_count * 3 // 16) & (freq < freq_count * 11 // 16)

    @pl.when(from_end)
    def _():
        for i in reversed(range(cut, freq_count)):
            send(i)

    @pl.when(jnp.logical_not(from_end))
    def _():
        for i in range(cut, freq_count):
            send(i)

    @pl.when(is_hub)
    def _():
        for slot in range(middle - origin):
            at_hub(slot).wait_recv()
            from_hub(slot).start()

    for i in range(freq_count):
        finish(i)

    flatten(rx, lines, planes, freq, cols)
    halos = []
    for n, (i, source, target) in enumerate(((2, 4, 0), (-2, 3, 7), (1, 3, 1), (-1, 3, 5))):
        size = 2 if abs(i) == 1 else 1
        halo = pltpu.make_async_remote_copy(
            src_ref=planes.at[pl.ds(source, size)],
            dst_ref=planes.at[pl.ds(target, size)],
            send_sem=halo_send.at[n],
            recv_sem=halo_recv.at[n],
            device_id={"sky": sky + i},
            device_id_type=MESH,
        )
        halos.append((i, halo))
    for i, halo in halos:
        pl.when(in_sky(i))(halo.start)
    mate = dict(halos)
    pl.when(odd)(mate[1].wait_recv)
    pl.when(jnp.logical_not(odd))(mate[-1].wait_recv)
    for i in range(4):
        lines_early[pl.ds(8 + i, CHANS, stride=4), :] = planes[jnp.where(odd, 1, 3) + i].astype(F32)
    shift_columns(lines_early, shifted_early)
    convolve_first(
        columns_to_rows(shifted_early, 4, 48, freq, cols), w_one_early, layer_early
    )
    for pairs in groups():
        rows = pl.ds(pairs[0] * ROWS_TWO, GROUP * ROWS_TWO)
        partial[rows, :] = convolve_second(layer_early, w_two_early, pairs)

    for i, halo in halos:
        pl.when(in_sky(i))(halo.wait_send)
    for i in range(freq_count):
        settle(i)

    @pl.when(is_hub)
    def _():
        for slot in range(middle - origin):
            from_hub(slot).wait_send()

    for i, halo in halos:
        if abs(i) == 2:
            pl.when(in_sky(-i))(halo.wait_recv)
    pl.when(jnp.logical_not(odd) & in_sky(-1))(mate[1].wait_recv)
    pl.when(odd & in_sky(1))(mate[-1].wait_recv)
    for r in range(8):
        y = 2 * sky - 3 + r
        value = planes[r].astype(F32)
        if r not in (3, 4):
            value = jnp.where((y >= 0) & (y < height), value, 0.0)
        lines_late[pl.ds(16 + r, CHANS, stride=8), :] = value
    shift_columns(lines_late, shifted_late)
    convolve_first(columns_to_rows(shifted_late, 8, 80, freq, cols), w_one_late, layer_late)
    zeroth, first = sum_moments(layer_late, w_two_late, partial)
    propose(zeroth, first, w_prop, heads, freq, sky, height, cols, result)


def on_device(sky_cube, free_mask, conv_first, conv_second, proposal_conv, score_head, box_head):
    freq_count = lax.axis_size("freq")
    sky_count = lax.axis_size("sky")
    chans, rows, cols = sky_cube.shape
    wide = proposal_conv.shape[3]
    taps = conv_first.transpose(1, 2, 3, 4, 0).reshape(9, 3, FEAT)
    kernel = conv_second.transpose(2, 3, 4, 0, 1).reshape(27, FEAT, FEAT)
    free = free_mask.reshape(1, chans)
    operands = (sky_cube, free, taps, kernel, proposal_conv, score_head, box_head)
    scratch = [pltpu.VMEM(operand.shape, operand.dtype) for operand in operands] + [
        pltpu.VMEM((freq_count, chans * rows, LANES), BF16),
        pltpu.VMEM((freq_count, chans * rows, LANES), BF16),
        pltpu.VMEM((8, CHANS, LANES), BF16),
        pltpu.VMEM((2 * CHANS + 8, LANES), F32),
        pltpu.VMEM((4 * CHANS + 48, LANES), F32),
        pltpu.VMEM((8 * CHANS + 80, LANES), F32),
        pltpu.VMEM((3, 4 * CHANS + 48, LANES), BF16),
        pltpu.VMEM((3, 8 * CHANS + 80, LANES), BF16),
        pltpu.VMEM((256, WINDOW * EARLY * FEAT), BF16),
        pltpu.VMEM((256, WINDOW * LATE * FEAT), BF16),
        pltpu.VMEM((27, FEAT, LANES), BF16),
        pltpu.VMEM((3, 4 * EARLY * FEAT, 256), BF16),
        pltpu.VMEM((3, 4 * LATE * FEAT, 256), BF16),
        pltpu.VMEM((3 * 256, 2 * wide), BF16),
        pltpu.VMEM((5 * HEAD, wide), BF16),
        pltpu.VMEM((ROWS_ONE, 2 * (PAIRS + 1) * EARLY * FEAT), BF16),
        pltpu.VMEM((ROWS_ONE, 2 * (PAIRS + 1) * LATE * FEAT), BF16),
        pltpu.VMEM((PAIRS * ROWS_TWO, 256), F32),
        pltpu.SemaphoreType.DMA((len(operands),)),
        pltpu.SemaphoreType.DMA((freq_count,)),
        pltpu.SemaphoreType.DMA((freq_count,)),
        pltpu.SemaphoreType.DMA((4,)),
        pltpu.SemaphoreType.DMA((4,)),
        pltpu.SemaphoreType.REGULAR,
        pltpu.SemaphoreType.REGULAR,
        pltpu.VMEM((freq_count // 2, chans * rows, LANES), BF16),
        pltpu.SemaphoreType.DMA((freq_count // 2,)),
        pltpu.SemaphoreType.DMA((freq_count // 2,)),
    ]
    shape = (freq_count, sky_count, rows * sky_count, cols)
    result = pl.pallas_call(
        functools.partial(body, shape),
        out_shape=pltpu.VMEM((ANCHORS, 5, rows, WIDTH), F32),
        in_specs=[pl.BlockSpec(memory_space=pltpu.HBM)] * len(operands),
        out_specs=pl.BlockSpec(memory_space=pltpu.VMEM),
        scratch_shapes=scratch,
        compiler_params=pltpu.CompilerParams(
            collective_id=0, has_side_effects=True, vmem_limit_bytes=60 * 1024 * 1024
        ),
    )(*operands)
    return result[:, 0], result[:, 1:]


def solution(mesh):
    in_specs = (P("freq", "sky", None), P("freq"), P(), P(), P(), P(), P())
    out_specs = (P(None, "sky", "freq"), P(None, None, "sky", "freq"))
    return jax.shard_map(
        on_device, mesh=mesh, in_specs=in_specs, out_specs=out_specs, check_vma=False
    )
```
